32 devices in a mesh: group: 2 (over x), comp: 16 (over z, y, core).
Axes of the slice: x: 2, y: 2, z: 4, core: 2. Of those that a mesh axis runs over, the one named last changes fastest.
Arguments:
- state: float32 [2, 5, 163840], P(None, None, ('group', 'comp')), parts along dimension 2, may hold values from -6 to 6
- surface_kind: int32 [81920], P('comp'), may hold values from 0 to 2
- send_block: int32 [16, 8, 32], P('comp'), may hold values from 0 to 39, as said below
- send_count: int32 [16, 8], P('comp'), may hold values from 0 to 32, as said below
- src_slot: int32 [640, 4], P('comp'), may hold values from 0 to 255, as said below
- src_count: int32 [640], P('comp'), may hold values from 1 to 4
- remap_weight: float32 [640, 4, 128, 128], P('comp'), may hold values from -0.25 to 0.25
Outputs:
- fluxes: float32 [2, 4, 163840], P(None, None, ('group', 'comp')), parts along dimension 2
The draws below stay inside these ranges and needn't reach their ends.
There are 2 independent parts, one for each index of `group`. The reference program is written for one: setup_inputs(seed, part) draws one part's arguments, and reference() takes and returns one part's arrays. A program takes and returns all parts, laid end to end along the dimension named above; an argument that names none is the same for every part. Nothing has to cross between parts.
Inputs may be any that keep to these rules, and one draw needn't show every extreme that they name: `send_count`: A tile at position p = s mod (8) intersects the other half's tiles at positions p - n + 4 that lie in 0 to 7; such pairs count 1 to 32, all others 0. Some source tile sends 32 slots to every tile it intersects, and some tile receives 32 slots from every tile that intersects it. send_block[s, n, c] is a block of tile s; entries with c at or beyond send_count[s, n] are 0. src_slot[b, k] = n * 32 + c with c below send_count[s, n] for the source tile s of offset n as in the reference program, so s intersects the tile owning block b.
All inputs are finite; a program needn't handle non-finite values.
Results may differ from the reference program's by a relative error of at most 0.000059.
Values sent between devices are 32-bit elements; how exact they have to be, the bound alone decides.
No kernel may reach another device: no remote copies, remote signals or barrier semaphores. Data moves between devices by JAX's collectives and lax.ppermute only.
A program may use at most 64 MiB of HBM per device.

```python
import jax
import jax.numpy as jnp
from jax import lax

STEPS = 2
FIELDS = 5
BLOCK_CELLS = 128
SOURCES = 4
NEIGH = 8
CAPACITY = 32
TILE_BLOCKS = 40
TILE_CELLS = 5120
ALL_BLOCKS = 640
ALL_CELLS = 81920
N_COMP = 16


def pair_counts(key):
    half_way = N_COMP // 2
    key_list = jax.random.split(key, 5)
    base_count = jax.random.randint(key_list[0], (N_COMP, NEIGH), 1, CAPACITY + 1)
    busy_rows = (jax.random.randint(key_list[1], (N_COMP,), 0, 8) == 0) | (jnp.arange(N_COMP) == jax.random.randint(key_list[2], (), 0, N_COMP))
    heavy_tiles = (jax.random.randint(key_list[3], (N_COMP,), 0, 8) == 0) | (jnp.arange(N_COMP) == jax.random.randint(key_list[4], (), 0, N_COMP))
    tile_ids = jnp.arange(N_COMP)[:, None]
    shift_of = jnp.arange(NEIGH)[None, :] - NEIGH // 2
    target = (tile_ids + half_way - shift_of) % N_COMP
    target_pos = tile_ids % half_way - shift_of
    valid = (target_pos >= 0) & (target_pos < half_way)
    full_pair = busy_rows[:, None] | heavy_tiles[target]
    counts = jnp.where(full_pair, CAPACITY, base_count)
    return jnp.where(valid, counts, 0).astype(jnp.int32)


def draw_send_count(key, part):
    return pair_counts(key)


def draw_send_block(key, part):
    counts = pair_counts(key)
    key = jax.random.fold_in(key, 7)
    chosen = jax.random.randint(key, (N_COMP, NEIGH, CAPACITY), 0, TILE_BLOCKS)
    live_slot = jnp.arange(CAPACITY)[None, None, :] < counts[:, :, None]
    return jnp.where(live_slot, chosen, 0).astype(jnp.int32)


def draw_src_slot(key, part):
    counts = pair_counts(key)
    key = jax.random.fold_in(key, 11)
    key_one, key_two = jax.random.split(key)
    half_way = N_COMP // 2
    total_blocks = N_COMP * TILE_BLOCKS
    owner_dev = jnp.arange(total_blocks) // TILE_BLOCKS
    owner_pos = owner_dev % half_way
    low_shift = jnp.maximum(-(NEIGH // 2), -owner_pos)
    high_shift = jnp.minimum(NEIGH // 2 - 1, half_way - 1 - owner_pos)
    shift_of = jax.random.randint(key_one, (total_blocks, SOURCES), low_shift[:, None], high_shift[:, None] + 1)
    offset = shift_of + NEIGH // 2
    source = (owner_dev[:, None] - half_way + shift_of) % N_COMP
    limit = counts[source, offset]
    position = jax.random.randint(key_two, (total_blocks, SOURCES), 0, limit)
    return (offset * CAPACITY + position).astype(jnp.int32)


def set_ends(array, key, smallest, high):
    spot = [jax.random.randint(jax.random.fold_in(key, axis), (), 0, length) for axis, length in enumerate(array.shape)]
    widest = array.shape.index(max(array.shape))
    neighbour = spot[:widest] + [(spot[widest] + 1) % array.shape[widest]] + spot[widest + 1:]
    return array.at[tuple(spot)].set(smallest).at[tuple(neighbour)].set(high)


def block_levels(key, shape, cuts, smallest, largest):
    loudness = 1.0
    for dim, parts in cuts:
        steps = jax.random.uniform(jax.random.fold_in(jax.random.fold_in(key, 6), dim), (parts,), jnp.float32, smallest / len(cuts), largest / len(cuts))
        loudness = loudness * jnp.repeat(jnp.exp(steps), shape[dim] // parts).reshape((-1,) + (1,) * (len(shape) - 1 - dim))
    return loudness


def noise(stream_key, dims, scale, most, cuts=(), held_as=jnp.bfloat16):
    entries = jax.random.normal(stream_key, dims, jnp.float32) * scale
    if len(cuts) > 0:
        entries = block_levels(stream_key, dims, cuts, -0.22, 0.18) * entries
    return jnp.clip(entries, min=-most, max=most).astype(held_as)


def setup_inputs(seed: int = 0, part: int = 0) -> dict:
    splits = jax.random.split(jax.random.key(seed), 8)
    part_splits = jax.random.split(jax.random.fold_in(splits[7], part), 8)
    return {
        "state": noise(part_splits[0], (STEPS, FIELDS, ALL_CELLS), 1.0, 6.0, ((2, 16),), jnp.float32),
        "surface_kind": set_ends(jax.random.randint(splits[1], (ALL_CELLS,), 0, 3), jax.random.fold_in(splits[1], 1), 0, 2).astype(jnp.int32),
        "send_block": draw_send_block(jax.random.fold_in(splits[7], 71), part),
        "send_count": draw_send_count(jax.random.fold_in(splits[7], 71), part),
        "src_slot": draw_src_slot(jax.random.fold_in(splits[7], 71), part),
        "src_count": set_ends(jax.random.randint(splits[5], (ALL_BLOCKS,), 1, SOURCES + 1), jax.random.fold_in(splits[5], 1), 1, SOURCES).astype(jnp.int32),
        "remap_weight": noise(splits[6], (ALL_BLOCKS, SOURCES, BLOCK_CELLS, BLOCK_CELLS), (BLOCK_CELLS * SOURCES) ** -0.5, 0.25, ((0, 16),), jnp.float32),
    }


def bulk_fluxes(air, sea, surface_kind):
    wind_u, wind_v, air_temp, air_humid, radiation = (air[:, 0], air[:, 1], air[:, 2], air[:, 3], air[:, 4])
    sea_temp, ice_conc, ice_temp, current_u, current_v = (sea[:, 0], sea[:, 1], sea[:, 2], sea[:, 3], sea[:, 4])
    wet_cell = (surface_kind > 0).astype(air.dtype)
    ice_frac = jnp.clip(ice_conc, 0.0, 1.0) * (surface_kind == 2).astype(air.dtype)
    rel_u = wind_u - current_u
    rel_v = wind_v - current_v
    wind_speed = jnp.sqrt(rel_u * rel_u + rel_v * rel_v + 1.0)
    drag_coef = 0.8 * (1.0 - ice_frac) + 1.2 * ice_frac

    def surface_terms(surf_temp, sens_coef, albedo, latent):
        evaporation = 0.5 * wind_speed * (0.6 * jnp.exp(0.3 * surf_temp) - air_humid)
        heat_total = sens_coef * wind_speed * (surf_temp - air_temp) + latent * evaporation - ((1.0 - albedo) * radiation - 0.25 * surf_temp)
        return (heat_total, evaporation)
    heat_water, evap_water = surface_terms(sea_temp, 0.6, 0.07, 1.0)
    heat_ice, evap_ice = surface_terms(ice_temp, 0.4, 0.6, 1.2)
    stress_x = wet_cell * drag_coef * wind_speed * rel_u
    stress_y = wet_cell * drag_coef * wind_speed * rel_v
    heat_flux = wet_cell * ((1.0 - ice_frac) * heat_water + ice_frac * heat_ice)
    water_flux = wet_cell * ((1.0 - ice_frac) * evap_water + ice_frac * evap_ice)
    return jnp.stack([stress_x, stress_y, heat_flux, water_flux], axis=1)

def reference(state, surface_kind, send_block, send_count, src_slot, src_count, remap_weight):
    steps = state.shape[0]
    fields = state.shape[1]
    nblk_all = remap_weight.shape[0]
    width = remap_weight.shape[2]
    half_way = N_COMP // 2
    blocks_first = state.reshape(steps * fields, nblk_all, width).transpose(1, 0, 2)
    owner_dev = (jnp.arange(nblk_all) // TILE_BLOCKS).astype(jnp.int32)
    offset = (src_slot // CAPACITY).astype(jnp.int32)
    position = (src_slot % CAPACITY).astype(jnp.int32)
    source = ((owner_dev[:, None] - half_way - NEIGH // 2 + offset) % N_COMP).astype(jnp.int32)
    picked = send_block[source, offset, position]
    slot_index = lax.broadcasted_iota(jnp.int32, src_slot.shape, 1)
    live_slot = (position < send_count[source, offset]) & (slot_index < src_count[:, None])
    taken = blocks_first[source * TILE_BLOCKS + picked] * live_slot[:, :, None, None].astype(state.dtype)
    remapped = jnp.einsum('bkci,bkit->cbt', taken, remap_weight, precision=lax.Precision.HIGHEST)
    remapped = remapped.reshape(steps, fields, nblk_all * width)
    split_col = half_way * TILE_CELLS
    is_air_col = (jnp.arange(state.shape[2]) < split_col)[None, None, :]
    air = jnp.where(is_air_col, state, remapped)
    sea = jnp.where(is_air_col, remapped, state)
    return bulk_fluxes(air, sea, surface_kind)
```

```python
import jax
import jax.numpy as jnp
import numpy as np
from jax import lax
from jax.experimental import pallas as pl
from jax.experimental.pallas import tpu as pltpu
from jax.sharding import PartitionSpec as P


def exchange_plan(tiles, neigh):
    half = tiles // 2
    before, after = neigh // 2, neigh - 1 - neigh // 2
    wanted = set()
    for p in range(half):
        for s in range(max(0, p - before), min(half - 1, p + after) + 1):
            for core in (0, 1):
                if s // 2 != p // 2:
                    wanted.add((2 * (s // 2) + s % 2, 2 * (p // 2) + s % 2))
    reach = max((abs(s // 2 - p // 2) for s, p in wanted), default=0)
    passes, place = [], {}
    for p in range(half):
        place[p // 2, p // 2] = 0
    for d in range(1, reach + 1):
        for phase in (0, 1):
            pairs = []
            for s, p in sorted(wanted):
                low = min(s // 2, p // 2)
                if abs(s // 2 - p // 2) == d and (low // d) % 2 == phase:
                    pairs.append((s, p))
                    place[s // 2, p // 2] = len(passes) + 1
            if pairs:
                passes.append(pairs)
    held = 1 + len(passes)
    where = np.zeros((half, neigh), np.int32)
    for p in range(half):
        for n in range(neigh):
            s = p + n - before
            if 0 <= s < half:
                where[p, n] = place[s // 2, p // 2] + held * (s % 2 != p % 2)
    return passes, where, held


def split_kernel(chunks, w_hbm, out_ref, buf, sems):
    slots = w_hbm.shape[0]
    per = slots // chunks
    copies = [
        pltpu.make_async_copy(
            w_hbm.at[pl.ds(i * per, per)], buf.at[pl.ds(i * per, per)], sems.at[i]
        )
        for i in range(chunks)
    ]
    for copy in copies:
        copy.start()
    width = w_hbm.shape[2]
    for i in range(chunks):
        copies[i].wait()

        def one(j, carry):
            w = buf[j]
            high = w.astype(jnp.bfloat16)
            low = (w - high.astype(jnp.float32)).astype(jnp.bfloat16)
            out_ref[j, :, :width] = high
            out_ref[j, :, width:] = low
            return carry

        lax.fori_loop(i * per, (i + 1) * per, one, 0, unroll=2)


def split_weights(weight):
    slots, width, _ = weight.shape
    chunks = 10 if slots % 10 == 0 else 1
    return pl.pallas_call(
        lambda *refs: split_kernel(chunks, *refs),
        out_shape=pltpu.VMEM((slots, width, 2 * width), jnp.bfloat16),
        in_specs=[pl.BlockSpec(memory_space=pl.ANY)],
        out_specs=pl.BlockSpec(memory_space=pltpu.VMEM),
        scratch_shapes=[
            pltpu.VMEM(weight.shape, jnp.float32),
            pltpu.SemaphoreType.DMA((chunks,)),
        ],
        compiler_params=pltpu.CompilerParams(vmem_limit_bytes=32 * 2**20),
        cost_estimate=pl.CostEstimate(
            flops=slots * width * width * 4, bytes_accessed=weight.size * 8, transcendentals=0
        ),
        name="split_weights",
    )(weight)


def fluxes_of(air, sea, kind):
    wind_u, wind_v, air_temp, air_humid, radiation = air
    sea_temp, ice_conc, ice_temp, current_u, current_v = sea
    wet = (kind > 0).astype(jnp.float32)
    frac = jnp.clip(ice_conc, 0.0, 1.0) * (kind == 2).astype(jnp.float32)
    du = wind_u - current_u
    dv = wind_v - current_v
    speed = jnp.sqrt(du * du + dv * dv + 1.0)
    drag = 0.8 * (1.0 - frac) + 1.2 * frac

    def terms(ts, sens, albedo, latent):
        evap = 0.5 * speed * (0.6 * jnp.exp(0.3 * ts) - air_humid)
        heat = (
            sens * speed * (ts - air_temp)
            + latent * evap
            - ((1.0 - albedo) * radiation - 0.25 * ts)
        )
        return heat, evap

    heat_water, evap_water = terms(sea_temp, 0.6, 0.07, 1.0)
    heat_ice, evap_ice = terms(ice_temp, 0.4, 0.6, 1.2)
    pull = wet * drag * speed
    return (
        pull * du,
        pull * dv,
        wet * ((1.0 - frac) * heat_water + frac * heat_ice),
        wet * ((1.0 - frac) * evap_water + frac * evap_ice),
    )


def remap_kernel(dims, base_ref, slot_ref, count_ref, air_ref, x_ref, w_ref, state_ref, kind_ref, out_ref, acc):
    steps, fields, nblk, sources, zero_row = dims
    span = nblk * steps
    rows = 8
    width = w_ref.shape[1]

    def block(b, carry):
        count = count_ref[b]
        parts = []
        for k in range(sources):
            base = jnp.where(k < count, base_ref[slot_ref[b * sources + k]], zero_row)
            x = jnp.concatenate(
                [x_ref[pl.ds(base + m, rows, stride=span), :] for m in range(steps)], axis=0
            )
            high = x.astype(jnp.bfloat16)
            low = (x - high.astype(jnp.float32)).astype(jnp.bfloat16)
            parts.append(jnp.concatenate([high, low], axis=0))
        left = jnp.concatenate(parts, axis=1)
        right = w_ref[pl.ds(b * sources, sources)].reshape(sources * width, 2 * width)
        both = jnp.dot(left, right, preferred_element_type=jnp.float32)
        both = both[:, :width] + both[:, width:]
        n = rows * steps
        total = both[:n] + both[n:]
        for m in range(steps):
            acc[pl.ds(m * rows * nblk + b, rows, stride=nblk), :] = total[m * rows:(m + 1) * rows]
        return carry

    lax.fori_loop(0, nblk, block, 0, unroll=4)
    is_air = air_ref[0] > 0
    for m in range(steps):
        for j in range(nblk // 8):
            mapped = [acc[pl.ds((m * rows + f) * nblk + 8 * j, 8), :] for f in range(fields)]
            own = [
                state_ref[pl.ds(f * span + 8 * j * steps + m, 8, stride=steps), :]
                for f in range(fields)
            ]
            air = [jnp.where(is_air, s, r) for s, r in zip(own, mapped)]
            sea = [jnp.where(is_air, r, s) for s, r in zip(own, mapped)]
            for o, value in enumerate(fluxes_of(air, sea, kind_ref[pl.ds(8 * j, 8), :])):
                out_ref[pl.ds(m * 4 * nblk + 32 * j + o, 8, stride=4), :] = value


def remap_and_fluxes(base, slot, count, is_air, x, split, state, kind, dims):
    steps, fields, nblk, sources, zero_row = dims
    width = kind.shape[1]
    smem = pl.BlockSpec(memory_space=pltpu.SMEM)
    vmem = pl.BlockSpec(memory_space=pltpu.VMEM)
    return pl.pallas_call(
        lambda *refs: remap_kernel(dims, *refs),
        out_shape=jax.ShapeDtypeStruct((steps * nblk * 4, width), jnp.float32),
        in_specs=[smem] * 4 + [vmem] * 4,
        out_specs=vmem,
        scratch_shapes=[pltpu.VMEM((steps * 8 * nblk, width), jnp.float32)],
        compiler_params=pltpu.CompilerParams(vmem_limit_bytes=32 * 2**20),
        cost_estimate=pl.CostEstimate(
            flops=nblk * sources * 32 * width * width * 4,
            bytes_accessed=split.size * 2,
            transcendentals=2 * steps * nblk * width,
        ),
        name="remap_and_fluxes",
    )(base, slot, count, is_air, x, pltpu.with_memory_space_constraint(split, pltpu.VMEM), state, kind)


def local(state, surface_kind, send_block, send_count, src_slot, src_count, remap_weight):
    tiles = lax.axis_size("comp")
    tile = lax.axis_index("comp")
    half = tiles // 2
    position = tile % half
    steps, fields, _ = state.shape
    nblk, sources, width, _ = remap_weight.shape
    neigh, capacity = send_block.shape[1:]
    passes, where, held = exchange_plan(tiles, neigh)
    span = nblk * steps
    rows = fields * span

    def passed(array, pairs):
        return lax.ppermute(array, "comp", pairs)

    def both_halves(pairs):
        return pairs + [(s + half, t + half) for s, t in pairs]

    mine = state.reshape(steps, fields, nblk, width).transpose(1, 2, 0, 3).reshape(rows, width)
    across = passed(mine, [(i, (i + half) % tiles) for i in range(tiles)])
    near = [across] + [passed(across, both_halves(pairs)) for pairs in passes]
    near = jnp.concatenate(near)
    sibling = passed(near, [(i, i ^ 1) for i in range(tiles)])
    pad = 8 * span
    x = jnp.concatenate([near, sibling, jnp.zeros((pad, width), jnp.float32)])
    zero_row = 2 * held * rows

    live = lax.broadcasted_iota(jnp.int32, (neigh, capacity), 1) < send_count[0][:, None]
    coded = lax.all_gather(jnp.where(live, send_block[0], -1), "comp")
    offset = jnp.arange(neigh, dtype=jnp.int32)
    source = (tile + half - neigh // 2 + offset) % tiles
    picked = coded[source, offset]
    start = jnp.asarray(where)[position] * rows
    base = jnp.where(picked >= 0, start[:, None] + steps * picked, zero_row).reshape(-1)

    split = split_weights(remap_weight.reshape(nblk * sources, width, width))
    is_air = (tile < half).astype(jnp.int32).reshape(1)
    out = remap_and_fluxes(
        base, src_slot.reshape(-1), src_count, is_air, x, split, mine,
        surface_kind.reshape(nblk, width), (steps, fields, nblk, sources, zero_row),
    )
    out = out.reshape(steps, nblk, 4, width).transpose(0, 2, 1, 3)
    return out.reshape(steps, 4, nblk * width)


def solution(mesh):
    return jax.shard_map(
        local,
        mesh=mesh,
        in_specs=(
            P(None, None, ("group", "comp")),
            P("comp"),
            P("comp", None, None),
            P("comp", None),
            P("comp", None),
            P("comp"),
            P("comp", None, None, None),
        ),
        out_specs=P(None, None, ("group", "comp")),
        check_vma=False,
    )
```

```python
import jax
import jax.numpy as jnp
import numpy as np
from jax import lax
from jax.experimental import pallas as pl
from jax.experimental.pallas import tpu as pltpu
from jax.sharding import PartitionSpec as P


def exchange_plan(tiles, neigh):
    half = tiles // 2
    before, after = neigh // 2, neigh - 1 - neigh // 2
    wanted = set()
    for p in range(half):
        for s in range(max(0, p - before), min(half - 1, p + after) + 1):
            for core in (0, 1):
                if s // 2 != p // 2:
                    wanted.add((2 * (s // 2) + s % 2, 2 * (p // 2) + s % 2))
    reach = max((abs(s // 2 - p // 2) for s, p in wanted), default=0)
    passes, place = [], {}
    for p in range(half):
        place[p // 2, p // 2] = 0
    for d in range(1, reach + 1):
        for phase in (0, 1):
            pairs = []
            for s, p in sorted(wanted):
                low = min(s // 2, p // 2)
                if abs(s // 2 - p // 2) == d and (low // d) % 2 == phase:
                    pairs.append((s, p))
                    place[s // 2, p // 2] = len(passes) + 1
            if pairs:
                passes.append(pairs)
    held = 1 + len(passes)
    where = np.zeros((half, neigh), np.int32)
    for p in range(half):
        for n in range(neigh):
            s = p + n - before
            if 0 <= s < half:
                where[p, n] = place[s // 2, p // 2] + held * (s % 2 != p % 2)
    return passes, where, held


def split_kernel(chunks, w_hbm, out_ref, buf, sems):
    slots = w_hbm.shape[0]
    per = slots // chunks
    copies = [
        pltpu.make_async_copy(
            w_hbm.at[pl.ds(i * per, per)], buf.at[pl.ds(i * per, per)], sems.at[i]
        )
        for i in range(chunks)
    ]
    for copy in copies:
        copy.start()
    width = w_hbm.shape[2]
    for i in range(chunks):
        copies[i].wait()

        def one(j, carry):
            w = buf[j]
            high = w.astype(jnp.bfloat16)
            low = (w - high.astype(jnp.float32)).astype(jnp.bfloat16)
            out_ref[j, :, :width] = high
            out_ref[j, :, width:] = low
            return carry

        lax.fori_loop(i * per, (i + 1) * per, one, 0, unroll=2)


def split_weights(weight):
    slots, width, _ = weight.shape
    chunks = 10 if slots % 10 == 0 else 1
    return pl.pallas_call(
        lambda *refs: split_kernel(chunks, *refs),
        out_shape=pltpu.VMEM((slots, width, 2 * width), jnp.bfloat16),
        in_specs=[pl.BlockSpec(memory_space=pl.ANY)],
        out_specs=pl.BlockSpec(memory_space=pltpu.VMEM),
        scratch_shapes=[
            pltpu.VMEM(weight.shape, jnp.float32),
            pltpu.SemaphoreType.DMA((chunks,)),
        ],
        compiler_params=pltpu.CompilerParams(vmem_limit_bytes=32 * 2**20),
        cost_estimate=pl.CostEstimate(
            flops=slots * width * width * 4, bytes_accessed=weight.size * 8, transcendentals=0
        ),
        name="split_weights",
    )(pltpu.with_memory_space_constraint(weight, pltpu.HBM))


def fluxes_of(air, sea, kind):
    wind_u, wind_v, air_temp, air_humid, radiation = air
    sea_temp, ice_conc, ice_temp, current_u, current_v = sea
    wet = (kind > 0).astype(jnp.float32)
    frac = jnp.clip(ice_conc, 0.0, 1.0) * (kind == 2).astype(jnp.float32)
    du = wind_u - current_u
    dv = wind_v - current_v
    speed = jnp.sqrt(du * du + dv * dv + 1.0)
    drag = 0.8 * (1.0 - frac) + 1.2 * frac

    def terms(ts, sens, albedo, latent):
        evap = 0.5 * speed * (0.6 * jnp.exp(0.3 * ts) - air_humid)
        heat = (
            sens * speed * (ts - air_temp)
            + latent * evap
            - ((1.0 - albedo) * radiation - 0.25 * ts)
        )
        return heat, evap

    heat_water, evap_water = terms(sea_temp, 0.6, 0.07, 1.0)
    heat_ice, evap_ice = terms(ice_temp, 0.4, 0.6, 1.2)
    pull = wet * drag * speed
    return (
        pull * du,
        pull * dv,
        wet * ((1.0 - frac) * heat_water + frac * heat_ice),
        wet * ((1.0 - frac) * evap_water + frac * evap_ice),
    )


def remap_kernel(
    dims, place_ref, slot_ref, count_ref, air_ref, x_ref, w_ref, state_ref, kind_ref, out_ref,
    acc, starts, base_ref, sem,
):
    steps, fields, nblk, sources, capacity, stride, zero_row = dims
    span = nblk * steps
    rows = 8
    width = w_ref.shape[1]

    lines = starts.shape[1]
    for i in range(starts.shape[0]):
        code = x_ref[pl.ds(i * stride + stride - lines, lines), :]
        at = (code * steps + i * stride).astype(jnp.int32)
        starts[i] = jnp.where(code >= 0.0, at, zero_row)
    copy = pltpu.make_async_copy(starts, base_ref, sem)
    copy.start()
    copy.wait()

    def block(b, carry):
        count = count_ref[b]
        parts = []
        for k in range(sources):
            slot = slot_ref[b * sources + k]
            base = base_ref[place_ref[slot // capacity], slot // width, slot % width]
            base = jnp.where(k < count, base, zero_row)
            x = jnp.concatenate(
                [x_ref[pl.ds(base + m, rows, stride=span), :] for m in range(steps)], axis=0
            )
            high = x.astype(jnp.bfloat16)
            low = (x - high.astype(jnp.float32)).astype(jnp.bfloat16)
            parts.append(jnp.concatenate([high, low], axis=0))
        left = jnp.concatenate(parts, axis=1)
        right = w_ref[pl.ds(b * sources, sources)].reshape(sources * width, 2 * width)
        both = jnp.dot(left, right, preferred_element_type=jnp.float32)
        both = both[:, :width] + both[:, width:]
        n = rows * steps
        total = both[:n] + both[n:]
        for m in range(steps):
            acc[pl.ds(m * rows * nblk + b, rows, stride=nblk), :] = total[m * rows:(m + 1) * rows]
        return carry

    lax.fori_loop(0, nblk, block, 0, unroll=4)
    is_air = air_ref[0] > 0
    for m in range(steps):
        for j in range(nblk // 8):
            mapped = [acc[pl.ds((m * rows + f) * nblk + 8 * j, 8), :] for f in range(fields)]
            own = [
                state_ref[pl.ds(f * span + 8 * j * steps + m, 8, stride=steps), :]
                for f in range(fields)
            ]
            air = [jnp.where(is_air, s, r) for s, r in zip(own, mapped)]
            sea = [jnp.where(is_air, r, s) for s, r in zip(own, mapped)]
            for o, value in enumerate(fluxes_of(air, sea, kind_ref[pl.ds(8 * j, 8), :])):
                out_ref[pl.ds(m * 4 * nblk + 32 * j + o, 8, stride=4), :] = value


def remap_and_fluxes(place, slot, count, is_air, x, split, state, kind, dims):
    steps, fields, nblk, sources, capacity, stride, zero_row = dims
    width = kind.shape[1]
    table = (zero_row // stride, stride - steps * fields * nblk, width)
    smem = pl.BlockSpec(memory_space=pltpu.SMEM)
    vmem = pl.BlockSpec(memory_space=pltpu.VMEM)
    return pl.pallas_call(
        lambda *refs: remap_kernel(dims, *refs),
        out_shape=jax.ShapeDtypeStruct((steps * nblk * 4, width), jnp.float32),
        in_specs=[smem] * 4 + [vmem] * 4,
        out_specs=vmem,
        scratch_shapes=[
            pltpu.VMEM((steps * 8 * nblk, width), jnp.float32),
            pltpu.VMEM(table, jnp.int32),
            pltpu.SMEM(table, jnp.int32),
            pltpu.SemaphoreType.DMA,
        ],
        compiler_params=pltpu.CompilerParams(vmem_limit_bytes=32 * 2**20),
        cost_estimate=pl.CostEstimate(
            flops=nblk * sources * 32 * width * width * 4,
            bytes_accessed=split.size * 2,
            transcendentals=2 * steps * nblk * width,
        ),
        name="remap_and_fluxes",
    )(place, slot, count, is_air, x, pltpu.with_memory_space_constraint(split, pltpu.VMEM), state, kind)


def local(state, surface_kind, send_block, send_count, src_slot, src_count, remap_weight):
    tiles = lax.axis_size("comp")
    tile = lax.axis_index("comp")
    half = tiles // 2
    position = tile % half
    steps, fields, _ = state.shape
    nblk, sources, width, _ = remap_weight.shape
    neigh, capacity = send_block.shape[1:]
    passes, where, held = exchange_plan(tiles, neigh)
    span = nblk * steps
    rows = fields * span

    def passed(array, pairs):
        return lax.ppermute(array, "comp", pairs)

    def both_halves(pairs):
        return pairs + [(s + half, t + half) for s, t in pairs]

    mine = state.reshape(steps, fields, nblk, width).transpose(1, 2, 0, 3).reshape(rows, width)
    live = lax.broadcasted_iota(jnp.int32, (neigh, capacity), 1) < send_count[0][:, None]
    table = jnp.where(live, send_block[0], -1).astype(jnp.float32).reshape(-1, width)
    table = jnp.pad(table, ((0, -table.shape[0] % 8), (0, 0)))
    across_pairs = [(i, (i + half) % tiles) for i in range(tiles)]
    across = jnp.concatenate([passed(mine, across_pairs), passed(table, across_pairs)])
    near = [across] + [passed(across, both_halves(pairs)) for pairs in passes]
    near = jnp.concatenate(near)
    sibling = passed(near, [(i, i ^ 1) for i in range(tiles)])
    stride = rows + table.shape[0]
    zero_row = 2 * held * stride
    x = jnp.concatenate([near, sibling, jnp.zeros((8 * span, width), jnp.float32)])
    place = jnp.asarray(where)[position]

    split = split_weights(remap_weight.reshape(nblk * sources, width, width))
    is_air = (tile < half).astype(jnp.int32).reshape(1)
    out = remap_and_fluxes(
        place, src_slot.reshape(-1), src_count, is_air, x, split, mine,
        surface_kind.reshape(nblk, width),
        (steps, fields, nblk, sources, capacity, stride, zero_row),
    )
    out = out.reshape(steps, nblk, 4, width).transpose(0, 2, 1, 3)
    return out.reshape(steps, 4, nblk * width)


def solution(mesh):
    return jax.shard_map(
        local,
        mesh=mesh,
        in_specs=(
            P(None, None, ("group", "comp")),
            P("comp"),
            P("comp", None, None),
            P("comp", None),
            P("comp", None),
            P("comp"),
            P("comp", None, None, None),
        ),
        out_specs=P(None, None, ("group", "comp")),
        check_vma=False,
    )
```

```python
import jax
import jax.numpy as jnp
import numpy as np
from jax import lax
from jax.experimental import pallas as pl
from jax.experimental.pallas import tpu as pltpu
from jax.sharding import PartitionSpec as P


def exchange_plan(tiles, neigh):
    half = tiles // 2
    before, after = neigh // 2, neigh - 1 - neigh // 2
    where = np.zeros((half, neigh), np.int32)
    offsets = [
        (p, n, p + n - before)
        for p in range(half)
        for n in range(neigh)
        if 0 <= p + n - before < half
    ]
    if half == 8:
        passes = [[(p, p ^ 2) for p in range(half)], [(p, p ^ 4) for p in range(half)]]
        land = 0
        for p, n, s in offsets:
            chip, other = (s ^ p ^ land) // 2, (s ^ p) % 2
            where[p, n] = 2 * 16 + other if chip == 3 else other * 16 + chip
        return passes, True, land, where
    wanted = set()
    for p, n, s in offsets:
        for core in (0, 1):
            if s // 2 != p // 2:
                wanted.add((2 * (s // 2) + s % 2, 2 * (p // 2) + s % 2))
    reach = max((abs(s // 2 - p // 2) for s, p in wanted), default=0)
    passes, place = [], {(c, c): 0 for c in range(half // 2)}
    for d in range(1, reach + 1):
        for phase in (0, 1):
            pairs = []
            for s, p in sorted(wanted):
                low = min(s // 2, p // 2)
                if abs(s // 2 - p // 2) == d and (low // d) % 2 == phase:
                    pairs.append((s, p))
                    place[s // 2, p // 2] = len(passes) + 1
            if pairs:
                passes.append(pairs)
    for p, n, s in offsets:
        where[p, n] = place[s // 2, p // 2] + 16 * (s % 2 != p % 2)
    return passes, False, 0, where


def tile_facts(tiles, where):
    half = tiles // 2
    return np.array(
        [[*where[t % half], t % 2 == 0, t < half] for t in range(tiles)], np.int32
    )


def encode_kernel(block_ref, count_ref, out_ref):
    neigh, capacity = block_ref.shape
    slot = lax.broadcasted_iota(jnp.int32, (1, capacity), 1)
    out_ref[...] = jnp.full(out_ref.shape, -1.0, jnp.float32)
    for n in range(neigh):
        code = jnp.where(slot < count_ref[0, n], block_ref[n:n + 1, :], -1)
        out_ref[n:n + 1, :capacity] = code.astype(jnp.float32)


def encode(block, count, width):
    neigh = block.shape[0]
    return pl.pallas_call(
        encode_kernel,
        out_shape=jax.ShapeDtypeStruct((neigh + -neigh % 8, width), jnp.float32),
        in_specs=[pl.BlockSpec(memory_space=pltpu.VMEM), pl.BlockSpec(memory_space=pltpu.SMEM)],
        out_specs=pl.BlockSpec(memory_space=pltpu.VMEM),
        cost_estimate=pl.CostEstimate(flops=4096, bytes_accessed=8192, transcendentals=0),
        name="encode",
    )(block, count)


def power(n):
    return 1 << (n - 1).bit_length()


UNROLL = 8


def prepare_kernel(dims, chunks, slot_ref, count_ref, facts_ref, w_hbm, split_ref, list_ref, total_ref, even_ref, buf, sems):
    nblk, sources, capacity, groups, received = dims
    tile = lax.axis_index("comp")
    neigh = received // capacity
    slots, width = w_hbm.shape[:2]
    per = slots // chunks
    copies = [
        pltpu.make_async_copy(
            w_hbm.at[pl.ds(i * per, per)], buf.at[pl.ds(i * per, per)], sems.at[i]
        )
        for i in range(chunks)
    ]
    for copy in copies:
        copy.start()

    room = slots + UNROLL
    low, high = power(slots + 1), power(received)
    for g in range(groups):
        total_ref[g] = 0

    def block(b, carry):
        count = count_ref[b]
        for k in range(sources):
            slot = slot_ref[k, b]
            place = facts_ref[tile, slot // capacity]
            g = place // 16
            n = total_ref[g]
            list_ref[g * room + n] = ((place % 16) * high + slot) * low + b * sources + k
            total_ref[g] = n + (k < count).astype(jnp.int32)
        return carry

    lax.fori_loop(0, nblk, block, 0)
    total_ref[groups] = facts_ref[tile, neigh + 1]
    even_ref[...] = jnp.full(even_ref.shape, facts_ref[tile, neigh])
    for g in range(groups):
        n = total_ref[g]
        for u in range(UNROLL):
            list_ref[g * room + n + u] = slots

    split_ref[slots] = jnp.zeros(split_ref.shape[1:], split_ref.dtype)
    for i in range(chunks):
        copies[i].wait()

        def one(j, carry):
            w = buf[j]
            first = w.astype(jnp.bfloat16)
            rest = (w - first.astype(jnp.float32)).astype(jnp.bfloat16)
            split_ref[j, :, :width] = first
            split_ref[j, :, width:] = rest
            return carry

        lax.fori_loop(i * per, (i + 1) * per, one, 0, unroll=2)


def prepare(slot, count, facts, weight, dims):
    nblk, sources, capacity, groups, received = dims
    slots, width, _ = weight.shape
    chunks = 10 if slots % 10 == 0 else 1
    smem = pl.BlockSpec(memory_space=pltpu.SMEM)
    vmem = pl.BlockSpec(memory_space=pltpu.VMEM)
    return pl.pallas_call(
        lambda *refs: prepare_kernel(dims, chunks, *refs),
        out_shape=(
            pltpu.VMEM((slots + 1, width, 2 * width), jnp.bfloat16),
            jax.ShapeDtypeStruct((groups * (slots + UNROLL),), jnp.int32),
            jax.ShapeDtypeStruct((groups + 1,), jnp.int32),
            jax.ShapeDtypeStruct((8, width), jnp.int32),
        ),
        in_specs=[smem, smem, smem, pl.BlockSpec(memory_space=pl.ANY)],
        out_specs=(vmem, smem, smem, vmem),
        scratch_shapes=[
            pltpu.VMEM(weight.shape, jnp.float32),
            pltpu.SemaphoreType.DMA((chunks,)),
        ],
        compiler_params=pltpu.CompilerParams(vmem_limit_bytes=16 * 2**20),
        cost_estimate=pl.CostEstimate(
            flops=slots * width * width * 4, bytes_accessed=weight.size * 8, transcendentals=0
        ),
        name="prepare",
    )(slot, count, facts, pltpu.with_memory_space_constraint(weight, pltpu.HBM))


def fluxes_of(air, sea, kind):
    wind_u, wind_v, air_temp, air_humid, radiation = air
    sea_temp, ice_conc, ice_temp, current_u, current_v = sea
    wet = (kind > 0).astype(jnp.float32)
    frac = jnp.clip(ice_conc, 0.0, 1.0) * (kind == 2).astype(jnp.float32)
    du = wind_u - current_u
    dv = wind_v - current_v
    speed = jnp.sqrt(du * du + dv * dv + 1.0)
    drag = 0.8 * (1.0 - frac) + 1.2 * frac

    def terms(ts, sens, albedo, latent):
        evap = 0.5 * speed * (0.6 * jnp.exp(0.3 * ts) - air_humid)
        heat = (
            sens * speed * (ts - air_temp)
            + latent * evap
            - ((1.0 - albedo) * radiation - 0.25 * ts)
        )
        return heat, evap

    heat_water, evap_water = terms(sea_temp, 0.6, 0.07, 1.0)
    heat_ice, evap_ice = terms(ice_temp, 0.4, 0.6, 1.2)
    pull = wet * drag * speed
    return (
        pull * du,
        pull * dv,
        wet * ((1.0 - frac) * heat_water + frac * heat_ice),
        wet * ((1.0 - frac) * evap_water + frac * evap_ice),
    )


def remap_group(dims, group, list_ref, total_ref, x_ref, split_ref, acc, starts, base_ref, sem):
    steps, fields, nblk, sources, received, capacity, stride = dims
    span = nblk * steps
    rows = 8
    slots, width = nblk * sources, split_ref.shape[1]
    room = slots + UNROLL
    low, high = power(slots + 1), power(received)

    lines = starts.shape[1]
    for i in range(starts.shape[0]):
        code = x_ref[pl.ds(i * stride + stride - lines, lines), :]
        at = (code * steps + i * stride).astype(jnp.int32)
        starts[i] = jnp.where(code >= 0.0, at, -1)
    copy = pltpu.make_async_copy(starts, base_ref, sem)
    copy.start()
    copy.wait()

    def batch(i, carry):
        for u in range(UNROLL):
            entry = list_ref[group * room + i * UNROLL + u]
            j = entry % low
            slot = (entry // low) % high
            base = base_ref[entry // (low * high), slot // capacity, slot % capacity]
            j = jnp.where(base < 0, slots, j)
            base = jnp.maximum(base, 0)
            x = jnp.concatenate(
                [x_ref[pl.ds(base + m, rows, stride=span), :] for m in range(steps)], axis=0
            )
            first = x.astype(jnp.bfloat16)
            rest = (x - first.astype(jnp.float32)).astype(jnp.bfloat16)
            both = jnp.dot(
                jnp.concatenate([first, rest], axis=0), split_ref[j],
                preferred_element_type=jnp.float32,
            )
            both = both[:, :width] + both[:, width:]
            n = rows * steps
            both = both[:n] + both[n:]
            for m in range(steps):
                at = pl.ds(m * rows * nblk + j // sources, rows, stride=nblk)
                acc[at, :] += both[m * rows:(m + 1) * rows]
        return carry

    lax.fori_loop(0, (total_ref[group] + UNROLL - 1) // UNROLL, batch, 0)


def remap_kernel(dims, group, first, list_ref, total_ref, x_ref, split_ref, *refs):
    if first:
        acc, starts, base_ref, sem = refs
        acc[...] = jnp.zeros_like(acc)
    else:
        before, acc, starts, base_ref, sem = refs
        acc[...] = before[...]
    remap_group(dims, group, list_ref, total_ref, x_ref, split_ref, acc, starts, base_ref, sem)


def last_kernel(dims, group, groups, list_ref, total_ref, x_ref, split_ref, before, state_ref, kind_ref, out_ref, acc, starts, base_ref, sem):
    steps, fields, nblk = dims[:3]
    span = nblk * steps
    acc[...] = before[...]
    remap_group(dims, group, list_ref, total_ref, x_ref, split_ref, acc, starts, base_ref, sem)
    is_air = total_ref[groups] > 0
    for m in range(steps):
        for j in range(nblk // 8):
            mapped = [acc[pl.ds((m * 8 + f) * nblk + 8 * j, 8), :] for f in range(fields)]
            own = [
                state_ref[pl.ds(f * span + 8 * j * steps + m, 8, stride=steps), :]
                for f in range(fields)
            ]
            air = [jnp.where(is_air, s, r) for s, r in zip(own, mapped)]
            sea = [jnp.where(is_air, r, s) for s, r in zip(own, mapped)]
            for o, value in enumerate(fluxes_of(air, sea, kind_ref[pl.ds(8 * j, 8), :])):
                out_ref[pl.ds(m * 4 * nblk + 32 * j + o, 8, stride=4), :] = value


def remap(dims, group, lists, totals, x, tiles, split, before=None, last=None):
    steps, fields, nblk, sources, received, capacity, stride = dims
    width = x.shape[1]
    groups = totals.shape[0] - 1
    table = (tiles, stride - steps * fields * nblk, width)
    sums = (steps * 8 * nblk + 8, width)
    smem = pl.BlockSpec(memory_space=pltpu.SMEM)
    vmem = pl.BlockSpec(memory_space=pltpu.VMEM)
    scratch = [pltpu.VMEM(table, jnp.int32), pltpu.SMEM(table, jnp.int32), pltpu.SemaphoreType.DMA]
    args = [lists, totals, x, pltpu.with_memory_space_constraint(split, pltpu.VMEM)]
    specs = [smem, smem, vmem, vmem]
    if before is not None:
        args.append(before)
        specs.append(vmem)
    if last is None:
        out = jax.ShapeDtypeStruct(sums, jnp.float32)
        body = lambda *refs: remap_kernel(dims, group, before is None, *refs)
    else:
        args += list(last)
        specs += [vmem, vmem]
        out = jax.ShapeDtypeStruct((steps * nblk * 4, width), jnp.float32)
        scratch = [pltpu.VMEM(sums, jnp.float32)] + scratch
        body = lambda *refs: last_kernel(dims, group, groups, *refs)
    return pl.pallas_call(
        body,
        out_shape=out,
        in_specs=specs,
        out_specs=vmem,
        scratch_shapes=scratch,
        compiler_params=pltpu.CompilerParams(vmem_limit_bytes=16 * 2**20),
        cost_estimate=pl.CostEstimate(
            flops=nblk * sources * 32 * width * width,
            bytes_accessed=split.size,
            transcendentals=0 if last is None else 2 * steps * nblk * width,
        ),
        name="remap_last" if last is not None else "remap_%d" % group,
    )(*args)


def local(state, surface_kind, send_block, send_count, src_slot, src_count, remap_weight):
    tiles = lax.axis_size("comp")
    half = tiles // 2
    steps, fields, _ = state.shape
    nblk, sources, width, _ = remap_weight.shape
    neigh, capacity = send_block.shape[1:]
    passes, relayed, land, where = exchange_plan(tiles, neigh)
    span = nblk * steps
    rows = fields * span

    def passed(array, pairs):
        return lax.ppermute(array, "comp", pairs)

    def within(pairs):
        return pairs + [(s + half, t + half) for s, t in pairs]

    def ahead(early, late):
        return lax.optimization_barrier((early, late))

    siblings = [(i, i ^ 1) for i in range(tiles)]

    mine = state.reshape(steps, fields, nblk, width).transpose(1, 2, 0, 3).reshape(rows, width)
    table = encode(send_block[0], send_count, width)
    stride = rows + table.shape[0]
    over = [(i, (i % half ^ land) + (half if i < half else 0)) for i in range(tiles)]
    across = jnp.concatenate([passed(mine, over), passed(table, over)])

    groups = 3 if relayed else 2
    received = neigh * capacity
    split, lists, totals, even = prepare(
        src_slot.T, src_count, jnp.asarray(tile_facts(tiles, where)),
        remap_weight.reshape(nblk * sources, width, width),
        (nblk, sources, capacity, groups, received),
    )
    across, lists = ahead(across, lists)

    spare = jnp.zeros(((8 - fields) * span, width), jnp.float32)
    others = [passed(across, within(pairs)) for pairs in passes]
    near = jnp.concatenate([across] + others + [spare])
    held = 1 + len(passes)
    sibling = passed(near, siblings)

    dims = (steps, fields, nblk, sources, received, capacity, stride)
    last = (mine, surface_kind.reshape(nblk, width))
    sums = remap(dims, 0, lists, totals, near, held, split)
    if relayed:
        by_eight = [o.reshape(-1, 8, width) for o in others]
        relay = passed(
            jnp.where(even[None] > 0, by_eight[1], by_eight[0]).reshape(stride, width),
            within([(p, p ^ 2) if p % 2 == 0 else (p, p ^ 4) for p in range(half)]),
        )
        sums = remap(dims, 1, lists, totals, sibling, held, split, sums)
        relay, sums = ahead(relay, sums)
        extra = jnp.concatenate([relay, passed(relay, siblings), spare])
        out = remap(dims, 2, lists, totals, extra, 2, split, sums, last)
    else:
        out = remap(dims, 1, lists, totals, sibling, held, split, sums, last)
    out = out.reshape(steps, nblk, 4, width).transpose(0, 2, 1, 3)
    return out.reshape(steps, 4, nblk * width)


def solution(mesh):
    return jax.shard_map(
        local,
        mesh=mesh,
        in_specs=(
            P(None, None, ("group", "comp")),
            P("comp"),
            P("comp", None, None),
            P("comp", None),
            P("comp", None),
            P("comp"),
            P("comp", None, None, None),
        ),
        out_specs=P(None, None, ("group", "comp")),
        check_vma=False,
    )
```

```python
import jax
import jax.numpy as jnp
import numpy as np
from jax import lax
from jax.experimental import pallas as pl
from jax.experimental.pallas import tpu as pltpu
from jax.sharding import PartitionSpec as P


def exchange_plan(tiles, neigh):
    half = tiles // 2
    before, after = neigh // 2, neigh - 1 - neigh // 2
    where = np.zeros((half, neigh), np.int32)
    offsets = [
        (p, n, p + n - before)
        for p in range(half)
        for n in range(neigh)
        if 0 <= p + n - before < half
    ]
    if half == 8:
        passes = [[(p, p ^ 2) for p in range(half)], [(p, p ^ 4) for p in range(half)]]
        land = 4
        for p, n, s in offsets:
            chip, other = (s ^ p ^ land) // 2, (s ^ p) % 2
            where[p, n] = 2 * 16 + other if chip == 3 else other * 16 + chip
        return passes, True, land, where
    wanted = set()
    for p, n, s in offsets:
        for core in (0, 1):
            if s // 2 != p // 2:
                wanted.add((2 * (s // 2) + s % 2, 2 * (p // 2) + s % 2))
    reach = max((abs(s // 2 - p // 2) for s, p in wanted), default=0)
    passes, place = [], {(c, c): 0 for c in range(half // 2)}
    for d in range(1, reach + 1):
        for phase in (0, 1):
            pairs = []
            for s, p in sorted(wanted):
                low = min(s // 2, p // 2)
                if abs(s // 2 - p // 2) == d and (low // d) % 2 == phase:
                    pairs.append((s, p))
                    place[s // 2, p // 2] = len(passes) + 1
            if pairs:
                passes.append(pairs)
    for p, n, s in offsets:
        where[p, n] = place[s // 2, p // 2] + 16 * (s % 2 != p % 2)
    return passes, False, 0, where


def tile_facts(tiles, where):
    half = tiles // 2
    return np.array(
        [[*where[t % half], t % 2 == 0, t < half] for t in range(tiles)], np.int32
    )


def encode_kernel(block_ref, count_ref, out_ref):
    neigh, capacity = block_ref.shape
    slot = lax.broadcasted_iota(jnp.int32, (1, capacity), 1)
    out_ref[...] = jnp.full(out_ref.shape, -1.0, jnp.float32)
    for n in range(neigh):
        code = jnp.where(slot < count_ref[0, n], block_ref[n:n + 1, :], -1)
        out_ref[n:n + 1, :capacity] = code.astype(jnp.float32)


def encode(block, count, width):
    neigh = block.shape[0]
    return pl.pallas_call(
        encode_kernel,
        out_shape=jax.ShapeDtypeStruct((neigh + -neigh % 8, width), jnp.float32),
        in_specs=[pl.BlockSpec(memory_space=pltpu.VMEM), pl.BlockSpec(memory_space=pltpu.SMEM)],
        out_specs=pl.BlockSpec(memory_space=pltpu.VMEM),
        cost_estimate=pl.CostEstimate(flops=4096, bytes_accessed=8192, transcendentals=0),
        name="encode",
    )(block, count)


def power(n):
    return 1 << (n - 1).bit_length()


UNROLL = 16


def prepare_kernel(
    dims, chunks, slot_hbm, count_hbm, facts_hbm, w_hbm, split_ref, list_ref, total_ref, even_ref,
    buf, slot_ref, count_ref, facts_ref, sems, small_sems,
):
    nblk, sources, capacity, groups, received = dims
    tile = lax.axis_index("comp")
    neigh = received // capacity
    slots, width = w_hbm.shape[:2]
    per = slots // chunks
    small = [
        pltpu.make_async_copy(src, dst, small_sems.at[i])
        for i, (src, dst) in enumerate(
            [(slot_hbm, slot_ref), (count_hbm, count_ref), (facts_hbm, facts_ref)]
        )
    ]
    copies = [
        pltpu.make_async_copy(
            w_hbm.at[pl.ds(i * per, per)], buf.at[pl.ds(i * per, per)], sems.at[i]
        )
        for i in range(chunks)
    ]
    for copy in small + copies:
        copy.start()
    for copy in small:
        copy.wait()

    room = slots + UNROLL
    low = power(slots + 1)
    lines = neigh + -neigh % 8
    for g in range(groups):
        total_ref[g] = 0

    def block(b, carry):
        count = count_ref[b]
        for k in range(sources):
            slot = slot_ref[k, b]
            place = facts_ref[tile, slot // capacity]
            g = place // 16
            n = total_ref[g]
            at = ((place % 16) * lines + slot // capacity) * width + slot % capacity
            list_ref[g * room + n] = at * low + b * sources + k
            total_ref[g] = n + (k < count).astype(jnp.int32)
        return carry

    lax.fori_loop(0, nblk, block, 0)
    total_ref[groups] = facts_ref[tile, neigh + 1]
    even_ref[...] = jnp.full(even_ref.shape, facts_ref[tile, neigh])
    for g in range(groups):
        n = total_ref[g]
        for u in range(UNROLL):
            list_ref[g * room + n + u] = slots

    split_ref[slots] = jnp.zeros(split_ref.shape[1:], split_ref.dtype)
    for i in range(chunks):
        copies[i].wait()

        def one(j, carry):
            w = buf[j]
            first = w.astype(jnp.bfloat16)
            rest = (w - first.astype(jnp.float32)).astype(jnp.bfloat16)
            split_ref[j, :, :width] = first
            split_ref[j, :, width:] = rest
            return carry

        lax.fori_loop(i * per, (i + 1) * per, one, 0, unroll=2)


def prepare(slot, count, facts, weight, dims):
    nblk, sources, capacity, groups, received = dims
    slots, width, _ = weight.shape
    chunks = 10 if slots % 10 == 0 else 1
    smem = pl.BlockSpec(memory_space=pltpu.SMEM)
    vmem = pl.BlockSpec(memory_space=pltpu.VMEM)
    args = [pltpu.with_memory_space_constraint(a, pltpu.HBM) for a in (slot, count, facts, weight)]
    return pl.pallas_call(
        lambda *refs: prepare_kernel(dims, chunks, *refs),
        out_shape=(
            pltpu.VMEM((slots + 1, width, 2 * width), jnp.bfloat16),
            jax.ShapeDtypeStruct((groups * (slots + UNROLL),), jnp.int32),
            jax.ShapeDtypeStruct((groups + 1,), jnp.int32),
            jax.ShapeDtypeStruct((8, width), jnp.int32),
        ),
        in_specs=[pl.BlockSpec(memory_space=pl.ANY)] * 4,
        out_specs=(vmem, smem, smem, vmem),
        scratch_shapes=[
            pltpu.VMEM(weight.shape, jnp.float32),
            pltpu.SMEM(slot.shape, jnp.int32),
            pltpu.SMEM(count.shape, jnp.int32),
            pltpu.SMEM(facts.shape, jnp.int32),
            pltpu.SemaphoreType.DMA((chunks,)),
            pltpu.SemaphoreType.DMA((3,)),
        ],
        compiler_params=pltpu.CompilerParams(vmem_limit_bytes=16 * 2**20),
        cost_estimate=pl.CostEstimate(
            flops=slots * width * width * 4, bytes_accessed=weight.size * 8, transcendentals=0
        ),
        name="prepare",
    )(*args)


def fluxes_of(air, sea, kind):
    wind_u, wind_v, air_temp, air_humid, radiation = air
    sea_temp, ice_conc, ice_temp, current_u, current_v = sea
    wet = (kind > 0).astype(jnp.float32)
    frac = jnp.clip(ice_conc, 0.0, 1.0) * (kind == 2).astype(jnp.float32)
    du = wind_u - current_u
    dv = wind_v - current_v
    speed = jnp.sqrt(du * du + dv * dv + 1.0)
    drag = 0.8 * (1.0 - frac) + 1.2 * frac

    def terms(ts, sens, albedo, latent):
        evap = 0.5 * speed * (0.6 * jnp.exp(0.3 * ts) - air_humid)
        heat = (
            sens * speed * (ts - air_temp)
            + latent * evap
            - ((1.0 - albedo) * radiation - 0.25 * ts)
        )
        return heat, evap

    heat_water, evap_water = terms(sea_temp, 0.6, 0.07, 1.0)
    heat_ice, evap_ice = terms(ice_temp, 0.4, 0.6, 1.2)
    pull = wet * drag * speed
    return (
        pull * du,
        pull * dv,
        wet * ((1.0 - frac) * heat_water + frac * heat_ice),
        wet * ((1.0 - frac) * evap_water + frac * evap_ice),
    )


def remap_group(dims, group, list_ref, total_ref, x_ref, split_ref, before, acc, starts, base_ref, sem):
    steps, fields, nblk, sources, received, capacity, stride = dims
    span = nblk * steps
    rows = 8
    slots, width = nblk * sources, split_ref.shape[1]
    room = slots + UNROLL
    low = power(slots + 1)

    lines = stride - steps * fields * nblk
    for i in range(starts.shape[0] // lines):
        code = x_ref[pl.ds(i * stride + stride - lines, lines), :]
        at = (code * steps + i * stride).astype(jnp.int32)
        starts[pl.ds(i * lines, lines), :] = jnp.where(code >= 0.0, at, -1)
    copy = pltpu.make_async_copy(starts, base_ref, sem)
    copy.start()
    acc[...] = jnp.zeros_like(acc) if before is None else before[...]
    copy.wait()

    def batch(i, carry):
        for u in range(UNROLL):
            entry = list_ref[group * room + i * UNROLL + u]
            j = entry % low
            base = base_ref[entry // (low * width), (entry // low) % width]
            j = jnp.where(base < 0, slots, j)
            base = jnp.maximum(base, 0)
            x = jnp.concatenate(
                [x_ref[pl.ds(base + m, rows, stride=span), :] for m in range(steps)], axis=0
            )
            first = x.astype(jnp.bfloat16)
            rest = (x - first.astype(jnp.float32)).astype(jnp.bfloat16)
            both = jnp.dot(
                jnp.concatenate([first, rest], axis=0), split_ref[j],
                preferred_element_type=jnp.float32,
            )
            both = both[:, :width] + both[:, width:]
            n = rows * steps
            both = both[:n] + both[n:]
            for m in range(steps):
                at = pl.ds(m * rows * nblk + j // sources, rows, stride=nblk)
                acc[at, :] += both[m * rows:(m + 1) * rows]
        return carry

    lax.fori_loop(0, (total_ref[group] + UNROLL - 1) // UNROLL, batch, 0)


def remap_kernel(dims, group, first, list_ref, total_ref, x_ref, split_ref, *refs):
    if first:
        refs = (None,) + refs
    remap_group(dims, group, list_ref, total_ref, x_ref, split_ref, *refs)


def last_kernel(dims, group, groups, list_ref, total_ref, x_ref, split_ref, before, state_ref, kind_ref, out_ref, acc, starts, base_ref, sem):
    steps, fields, nblk = dims[:3]
    span = nblk * steps
    remap_group(dims, group, list_ref, total_ref, x_ref, split_ref, before, acc, starts, base_ref, sem)
    is_air = total_ref[groups] > 0
    for m in range(steps):
        for j in range(nblk // 8):
            mapped = [acc[pl.ds((m * 8 + f) * nblk + 8 * j, 8), :] for f in range(fields)]
            own = [
                state_ref[pl.ds(f * span + 8 * j * steps + m, 8, stride=steps), :]
                for f in range(fields)
            ]
            air = [jnp.where(is_air, s, r) for s, r in zip(own, mapped)]
            sea = [jnp.where(is_air, r, s) for s, r in zip(own, mapped)]
            for o, value in enumerate(fluxes_of(air, sea, kind_ref[pl.ds(8 * j, 8), :])):
                out_ref[pl.ds(m * 4 * nblk + 32 * j + o, 8, stride=4), :] = value


def remap(dims, group, lists, totals, x, tiles, split, before=None, last=None):
    steps, fields, nblk, sources, received, capacity, stride = dims
    width = x.shape[1]
    groups = totals.shape[0] - 1
    table = (tiles * (stride - steps * fields * nblk), width)
    sums = (steps * 8 * nblk + 8, width)
    smem = pl.BlockSpec(memory_space=pltpu.SMEM)
    vmem = pl.BlockSpec(memory_space=pltpu.VMEM)
    scratch = [pltpu.VMEM(table, jnp.int32), pltpu.SMEM(table, jnp.int32), pltpu.SemaphoreType.DMA]
    args = [lists, totals, x, pltpu.with_memory_space_constraint(split, pltpu.VMEM)]
    specs = [smem, smem, vmem, vmem]
    if before is not None:
        args.append(before)
        specs.append(vmem)
    if last is None:
        out = jax.ShapeDtypeStruct(sums, jnp.float32)
        body = lambda *refs: remap_kernel(dims, group, before is None, *refs)
    else:
        args += list(last)
        specs += [vmem, vmem]
        out = jax.ShapeDtypeStruct((steps * nblk * 4, width), jnp.float32)
        scratch = [pltpu.VMEM(sums, jnp.float32)] + scratch
        body = lambda *refs: last_kernel(dims, group, groups, *refs)
    return pl.pallas_call(
        body,
        out_shape=out,
        in_specs=specs,
        out_specs=vmem,
        scratch_shapes=scratch,
        compiler_params=pltpu.CompilerParams(vmem_limit_bytes=16 * 2**20),
        cost_estimate=pl.CostEstimate(
            flops=nblk * sources * 32 * width * width,
            bytes_accessed=split.size,
            transcendentals=0 if last is None else 2 * steps * nblk * width,
        ),
        name="remap_last" if last is not None else "remap_%d" % group,
    )(*args)


def local(state, surface_kind, send_block, send_count, src_slot, src_count, remap_weight):
    tiles = lax.axis_size("comp")
    half = tiles // 2
    steps, fields, _ = state.shape
    nblk, sources, width, _ = remap_weight.shape
    neigh, capacity = send_block.shape[1:]
    passes, relayed, land, where = exchange_plan(tiles, neigh)
    span = nblk * steps
    rows = fields * span

    def passed(array, pairs):
        return lax.ppermute(array, "comp", pairs)

    def within(pairs):
        return pairs + [(s + half, t + half) for s, t in pairs]

    def ahead(early, late):
        return lax.optimization_barrier((early, late))

    siblings = [(i, i ^ 1) for i in range(tiles)]

    mine = state.reshape(steps, fields, nblk, width).transpose(1, 2, 0, 3).reshape(rows, width)
    table = encode(send_block[0], send_count, width)
    stride = rows + table.shape[0]
    over = [(i, (i % half ^ land) + (half if i < half else 0)) for i in range(tiles)]
    across = jnp.concatenate([passed(mine, over), passed(table, over)])

    groups = 3 if relayed else 2
    received = neigh * capacity
    split, lists, totals, even = prepare(
        src_slot.T, src_count, jnp.asarray(tile_facts(tiles, where)),
        remap_weight.reshape(nblk * sources, width, width),
        (nblk, sources, capacity, groups, received),
    )
    across, lists = ahead(across, lists)

    spare = jnp.zeros(((8 - fields) * span, width), jnp.float32)
    others = [passed(across, within(pairs)) for pairs in passes]
    held = 1 + len(passes)
    if relayed:
        by_eight = [o.reshape(-1, 8, width) for o in others]
        relay = passed(
            jnp.where(even[None] > 0, by_eight[1], by_eight[0]).reshape(stride, width),
            within([(p, p ^ 2) if p % 2 == 0 else (p, p ^ 4) for p in range(half)]),
        )
    near = jnp.concatenate([across] + others + [spare])
    sibling = passed(near, siblings)

    dims = (steps, fields, nblk, sources, received, capacity, stride)
    last = (mine, surface_kind.reshape(nblk, width))
    sums = remap(dims, 0, lists, totals, near, held, split)
    if relayed:
        sums = remap(dims, 1, lists, totals, sibling, held, split, sums)
        relay, sums = ahead(relay, sums)
        extra = jnp.concatenate([relay, passed(relay, siblings), spare])
        out = remap(dims, 2, lists, totals, extra, 2, split, sums, last)
    else:
        out = remap(dims, 1, lists, totals, sibling, held, split, sums, last)
    out = out.reshape(steps, nblk, 4, width).transpose(0, 2, 1, 3)
    return out.reshape(steps, 4, nblk * width)


def solution(mesh):
    return jax.shard_map(
        local,
        mesh=mesh,
        in_specs=(
            P(None, None, ("group", "comp")),
            P("comp"),
            P("comp", None, None),
            P("comp", None),
            P("comp", None),
            P("comp"),
            P("comp", None, None, None),
        ),
        out_specs=P(None, None, ("group", "comp")),
        check_vma=False,
    )
```

```python
import jax
import jax.numpy as jnp
import numpy as np
from jax import lax
from jax.experimental import pallas as pl
from jax.experimental.pallas import tpu as pltpu
from jax.sharding import PartitionSpec as P


def exchange_plan(tiles, neigh):
    half = tiles // 2
    before, after = neigh // 2, neigh - 1 - neigh // 2
    where = np.zeros((half, neigh), np.int32)
    offsets = [
        (p, n, p + n - before)
        for p in range(half)
        for n in range(neigh)
        if 0 <= p + n - before < half
    ]
    if half == 8:
        passes = [[(p, p ^ 2) for p in range(half)], [(p, p ^ 4) for p in range(half)]]
        land = 4
        for p, n, s in offsets:
            chip, other = (s ^ p ^ land) // 2, (s ^ p) % 2
            where[p, n] = (2 + other) * 16 if chip == 3 else other * 16 + chip
        return passes, True, land, where
    wanted = set()
    for p, n, s in offsets:
        for core in (0, 1):
            if s // 2 != p // 2:
                wanted.add((2 * (s // 2) + s % 2, 2 * (p // 2) + s % 2))
    reach = max((abs(s // 2 - p // 2) for s, p in wanted), default=0)
    passes, place = [], {(c, c): 0 for c in range(half // 2)}
    for d in range(1, reach + 1):
        for phase in (0, 1):
            pairs = []
            for s, p in sorted(wanted):
                low = min(s // 2, p // 2)
                if abs(s // 2 - p // 2) == d and (low // d) % 2 == phase:
                    pairs.append((s, p))
                    place[s // 2, p // 2] = len(passes) + 1
            if pairs:
                passes.append(pairs)
    for p, n, s in offsets:
        where[p, n] = place[s // 2, p // 2] + 16 * (s % 2 != p % 2)
    return passes, False, 0, where


def tile_facts(tiles, where):
    half = tiles // 2
    return np.array(
        [[*where[t % half], t % 2 == 0, t < half] for t in range(tiles)], np.int32
    )


def encode_kernel(block_ref, count_ref, out_ref):
    neigh, capacity = block_ref.shape
    slot = lax.broadcasted_iota(jnp.int32, (1, capacity), 1)
    out_ref[...] = jnp.full(out_ref.shape, -1.0, jnp.float32)
    for n in range(neigh):
        code = jnp.where(slot < count_ref[0, n], block_ref[n:n + 1, :], -1)
        out_ref[n:n + 1, :capacity] = code.astype(jnp.float32)


def encode(block, count, width):
    neigh = block.shape[0]
    return pl.pallas_call(
        encode_kernel,
        out_shape=jax.ShapeDtypeStruct((neigh + -neigh % 8, width), jnp.float32),
        in_specs=[pl.BlockSpec(memory_space=pltpu.VMEM), pl.BlockSpec(memory_space=pltpu.SMEM)],
        out_specs=pl.BlockSpec(memory_space=pltpu.VMEM),
        cost_estimate=pl.CostEstimate(flops=4096, bytes_accessed=8192, transcendentals=0),
        name="encode",
    )(block, count)


def power(n):
    return 1 << (n - 1).bit_length()


UNROLL = 16


def prepare_kernel(
    dims, chunks, slot_hbm, count_hbm, facts_hbm, w_hbm, split_ref, plan_ref, even_ref,
    buf, slot_ref, count_ref, facts_ref, sems, small_sems,
):
    nblk, sources, capacity, groups, received = dims
    tile = lax.axis_index("comp")
    neigh = received // capacity
    slots, width = w_hbm.shape[:2]
    per = slots // chunks
    small = [
        pltpu.make_async_copy(src, dst, small_sems.at[i])
        for i, (src, dst) in enumerate(
            [(slot_hbm, slot_ref), (count_hbm, count_ref), (facts_hbm, facts_ref)]
        )
    ]
    copies = [
        pltpu.make_async_copy(
            w_hbm.at[pl.ds(i * per, per)], buf.at[pl.ds(i * per, per)], sems.at[i]
        )
        for i in range(chunks)
    ]
    for copy in small + copies:
        copy.start()
    for copy in small:
        copy.wait()

    low = power(slots + 1)
    lines = neigh + -neigh % 8
    even_ref[...] = jnp.full(even_ref.shape, facts_ref[tile, neigh])
    split_ref[slots] = jnp.zeros(split_ref.shape[1:], split_ref.dtype)

    def block(b, numbers):
        count = count_ref[b]
        numbers = list(numbers)
        for k in range(sources):
            j = b * sources + k
            slot = slot_ref[k, b]
            place = facts_ref[tile, slot // capacity]
            at = ((place % 16) * lines + slot // capacity) * width + slot % capacity
            group = place // 16
            n = numbers[0]
            for g in range(1, groups):
                n = jnp.where(group == g, numbers[g], n)
            plan_ref[group, n] = at * low + j
            for g in range(groups):
                numbers[g] += ((group == g) & (k < count)).astype(jnp.int32)
            w = buf[j]
            first = w.astype(jnp.bfloat16)
            rest = (w - first.astype(jnp.float32)).astype(jnp.bfloat16)
            split_ref[j, :, :width] = first
            split_ref[j, :, width:] = rest
        return tuple(numbers)

    numbers = (jnp.int32(0),) * groups
    blocks = nblk // chunks
    for i in range(chunks):
        copies[i].wait()
        numbers = lax.fori_loop(i * blocks, (i + 1) * blocks, block, numbers)
    for g in range(groups):
        for u in range(UNROLL):
            plan_ref[g, numbers[g] + u] = slots
        plan_ref[groups, g] = numbers[g]
    plan_ref[groups, groups] = facts_ref[tile, neigh + 1]


def prepare(slot, count, facts, weight, dims):
    nblk, sources, capacity, groups, received = dims
    slots, width, _ = weight.shape
    chunks = 10 if nblk % 10 == 0 else 1
    smem = pl.BlockSpec(memory_space=pltpu.SMEM)
    vmem = pl.BlockSpec(memory_space=pltpu.VMEM)
    args = [pltpu.with_memory_space_constraint(a, pltpu.HBM) for a in (slot, count, facts, weight)]
    return pl.pallas_call(
        lambda *refs: prepare_kernel(dims, chunks, *refs),
        out_shape=(
            pltpu.VMEM((slots + 1, width, 2 * width), jnp.bfloat16),
            jax.ShapeDtypeStruct((groups + 1, slots + UNROLL + -(slots + UNROLL) % 128), jnp.int32),
            jax.ShapeDtypeStruct((8, width), jnp.int32),
        ),
        in_specs=[pl.BlockSpec(memory_space=pl.ANY)] * 4,
        out_specs=(vmem, smem, vmem),
        scratch_shapes=[
            pltpu.VMEM(weight.shape, jnp.float32),
            pltpu.SMEM(slot.shape, jnp.int32),
            pltpu.SMEM(count.shape, jnp.int32),
            pltpu.SMEM(facts.shape, jnp.int32),
            pltpu.SemaphoreType.DMA((chunks,)),
            pltpu.SemaphoreType.DMA((3,)),
        ],
        compiler_params=pltpu.CompilerParams(vmem_limit_bytes=16 * 2**20),
        cost_estimate=pl.CostEstimate(
            flops=slots * width * width * 4, bytes_accessed=weight.size * 8, transcendentals=0
        ),
        name="prepare",
    )(*args)


def fluxes_of(air, sea, kind):
    wind_u, wind_v, air_temp, air_humid, radiation = air
    sea_temp, ice_conc, ice_temp, current_u, current_v = sea
    wet = (kind > 0).astype(jnp.float32)
    frac = jnp.clip(ice_conc, 0.0, 1.0) * (kind == 2).astype(jnp.float32)
    du = wind_u - current_u
    dv = wind_v - current_v
    speed = jnp.sqrt(du * du + dv * dv + 1.0)
    drag = 0.8 * (1.0 - frac) + 1.2 * frac

    def terms(ts, sens, albedo, latent):
        evap = 0.5 * speed * (0.6 * jnp.exp(0.3 * ts) - air_humid)
        heat = (
            sens * speed * (ts - air_temp)
            + latent * evap
            - ((1.0 - albedo) * radiation - 0.25 * ts)
        )
        return heat, evap

    heat_water, evap_water = terms(sea_temp, 0.6, 0.07, 1.0)
    heat_ice, evap_ice = terms(ice_temp, 0.4, 0.6, 1.2)
    pull = wet * drag * speed
    return (
        pull * du,
        pull * dv,
        wet * ((1.0 - frac) * heat_water + frac * heat_ice),
        wet * ((1.0 - frac) * evap_water + frac * evap_ice),
    )


def remap_group(dims, group, plan_any, x_ref, split_ref, before, acc, plan_ref, starts, base_ref, sems):
    steps, fields, nblk, sources, received, capacity, stride = dims
    span = nblk * steps
    rows = 8
    slots, width = nblk * sources, split_ref.shape[1]
    low = power(slots + 1)
    groups = plan_ref.shape[0] - 1
    fetch = pltpu.make_async_copy(plan_any, plan_ref, sems.at[0])
    fetch.start()

    lines = stride - steps * fields * nblk
    for i in range(starts.shape[0] // lines):
        code = x_ref[pl.ds(i * stride + stride - lines, lines), :]
        at = (code * steps + i * stride).astype(jnp.int32)
        starts[pl.ds(i * lines, lines), :] = jnp.where(code >= 0.0, at, -1)
    copy = pltpu.make_async_copy(starts, base_ref, sems.at[1])
    copy.start()
    acc[...] = jnp.zeros_like(acc) if before is None else before[...]
    fetch.wait()
    copy.wait()

    def batch(i, carry):
        places = []
        for u in range(UNROLL):
            entry = plan_ref[group, i * UNROLL + u]
            base = base_ref[entry // (low * width), (entry // low) % width]
            j = jnp.where(base < 0, slots, entry % low)
            places.append((j, jnp.maximum(base, 0)))
        for j, base in places:
            x = jnp.concatenate(
                [x_ref[pl.ds(base + m, rows, stride=span), :] for m in range(steps)], axis=0
            )
            first = x.astype(jnp.bfloat16)
            rest = (x - first.astype(jnp.float32)).astype(jnp.bfloat16)
            both = jnp.dot(
                jnp.concatenate([first, rest], axis=0), split_ref[j],
                preferred_element_type=jnp.float32,
            )
            both = both[:, :width] + both[:, width:]
            n = rows * steps
            both = both[:n] + both[n:]
            for m in range(steps):
                at = pl.ds(m * rows * nblk + j // sources, rows, stride=nblk)
                acc[at, :] += both[m * rows:(m + 1) * rows]
        return carry

    lax.fori_loop(0, (plan_ref[groups, group] + UNROLL - 1) // UNROLL, batch, 0)


def remap_kernel(dims, group, first, plan_any, x_ref, split_ref, *refs):
    if first:
        refs = (None,) + refs
    remap_group(dims, group, plan_any, x_ref, split_ref, *refs)


def last_kernel(
    dims, group, plan_any, x_ref, split_ref, before, state_ref, kind_ref, out_ref, acc, plan_ref,
    starts, base_ref, sems,
):
    steps, fields, nblk = dims[:3]
    span = nblk * steps
    remap_group(
        dims, group, plan_any, x_ref, split_ref, before, acc, plan_ref, starts, base_ref, sems
    )
    groups = plan_ref.shape[0] - 1
    is_air = plan_ref[groups, groups] > 0
    for m in range(steps):
        for j in range(nblk // 8):
            mapped = [acc[pl.ds((m * 8 + f) * nblk + 8 * j, 8), :] for f in range(fields)]
            own = [
                state_ref[pl.ds(f * span + 8 * j * steps + m, 8, stride=steps), :]
                for f in range(fields)
            ]
            air = [jnp.where(is_air, s, r) for s, r in zip(own, mapped)]
            sea = [jnp.where(is_air, r, s) for s, r in zip(own, mapped)]
            for o, value in enumerate(fluxes_of(air, sea, kind_ref[pl.ds(8 * j, 8), :])):
                out_ref[pl.ds(m * 4 * nblk + 32 * j + o, 8, stride=4), :] = value


def remap(dims, group, plan, x, tiles, split, before=None, last=None):
    steps, fields, nblk, sources, received, capacity, stride = dims
    width = x.shape[1]
    table = (tiles * (stride - steps * fields * nblk), width)
    sums = (steps * 8 * nblk + 8, width)
    vmem = pl.BlockSpec(memory_space=pltpu.VMEM)
    scratch = [
        pltpu.SMEM(plan.shape, jnp.int32),
        pltpu.VMEM(table, jnp.int32),
        pltpu.SMEM(table, jnp.int32),
        pltpu.SemaphoreType.DMA((2,)),
    ]
    args = [plan, x, pltpu.with_memory_space_constraint(split, pltpu.VMEM)]
    specs = [pl.BlockSpec(memory_space=pl.ANY), vmem, vmem]
    if before is not None:
        args.append(before)
        specs.append(vmem)
    if last is None:
        out = jax.ShapeDtypeStruct(sums, jnp.float32)
        body = lambda *refs: remap_kernel(dims, group, before is None, *refs)
    else:
        args += list(last)
        specs += [vmem, vmem]
        out = jax.ShapeDtypeStruct((steps * nblk * 4, width), jnp.float32)
        scratch = [pltpu.VMEM(sums, jnp.float32)] + scratch
        body = lambda *refs: last_kernel(dims, group, *refs)
    return pl.pallas_call(
        body,
        out_shape=out,
        in_specs=specs,
        out_specs=vmem,
        scratch_shapes=scratch,
        compiler_params=pltpu.CompilerParams(vmem_limit_bytes=16 * 2**20),
        cost_estimate=pl.CostEstimate(
            flops=nblk * sources * 32 * width * width,
            bytes_accessed=split.size,
            transcendentals=0 if last is None else 2 * steps * nblk * width,
        ),
        name="remap_last" if last is not None else "remap_%d" % group,
    )(*args)


def local(state, surface_kind, send_block, send_count, src_slot, src_count, remap_weight):
    tiles = lax.axis_size("comp")
    half = tiles // 2
    steps, fields, _ = state.shape
    nblk, sources, width, _ = remap_weight.shape
    neigh, capacity = send_block.shape[1:]
    passes, relayed, land, where = exchange_plan(tiles, neigh)
    span = nblk * steps
    rows = fields * span

    def passed(array, pairs):
        return lax.ppermute(array, "comp", pairs)

    def within(pairs):
        return pairs + [(s + half, t + half) for s, t in pairs]

    def ahead(early, late):
        return lax.optimization_barrier((early, late))

    siblings = [(i, i ^ 1) for i in range(tiles)]

    mine = state.reshape(steps, fields, nblk, width).transpose(1, 2, 0, 3).reshape(rows, width)
    table = encode(send_block[0], send_count, width)
    stride = rows + table.shape[0]
    over = [(i, (i % half ^ land) + (half if i < half else 0)) for i in range(tiles)]
    across = jnp.concatenate([passed(mine, over), passed(table, over)])

    groups = 4 if relayed else 2
    received = neigh * capacity
    split, plan, even = prepare(
        src_slot.T, src_count, jnp.asarray(tile_facts(tiles, where)),
        remap_weight.reshape(nblk * sources, width, width),
        (nblk, sources, capacity, groups, received),
    )
    across, plan = ahead(across, plan)

    spare = jnp.zeros(((8 - fields) * span, width), jnp.float32)
    others = [passed(across, within(pairs)) for pairs in passes]
    held = 1 + len(passes)
    if relayed:
        by_eight = [o.reshape(-1, 8, width) for o in others]
        relay = passed(
            jnp.where(even[None] > 0, by_eight[1], by_eight[0]).reshape(stride, width),
            within([(p, p ^ 2) if p % 2 == 0 else (p, p ^ 4) for p in range(half)]),
        )
    near = jnp.concatenate([across] + others + [spare])
    sibling = passed(near, siblings)

    dims = (steps, fields, nblk, sources, received, capacity, stride)
    last = (mine, surface_kind.reshape(nblk, width))
    sums = remap(dims, 0, plan, near, held, split)
    if relayed:
        sums = remap(dims, 1, plan, sibling, held, split, sums)
        relay, sums = ahead(relay, sums)
        met = passed(relay, siblings)
        sums = remap(dims, 2, plan, jnp.concatenate([relay, spare]), 1, split, sums)
        out = remap(dims, 3, plan, jnp.concatenate([met, spare]), 1, split, sums, last)
    else:
        out = remap(dims, 1, plan, sibling, held, split, sums, last)
    out = out.reshape(steps, nblk, 4, width).transpose(0, 2, 1, 3)
    return out.reshape(steps, 4, nblk * width)


def solution(mesh):
    return jax.shard_map(
        local,
        mesh=mesh,
        in_specs=(
            P(None, None, ("group", "comp")),
            P("comp"),
            P("comp", None, None),
            P("comp", None),
            P("comp", None),
            P("comp"),
            P("comp", None, None, None),
        ),
        out_specs=P(None, None, ("group", "comp")),
        check_vma=False,
    )
```

```python
import jax
import jax.numpy as jnp
import numpy as np
from jax import lax
from jax.experimental import pallas as pl
from jax.experimental.pallas import tpu as pltpu
from jax.sharding import PartitionSpec as P


def exchange_plan(tiles, neigh):
    half = tiles // 2
    before, after = neigh // 2, neigh - 1 - neigh // 2
    where = np.zeros((half, neigh), np.int32)
    offsets = [
        (p, n, p + n - before)
        for p in range(half)
        for n in range(neigh)
        if 0 <= p + n - before < half
    ]
    if half == 8:
        passes = [
            [(p, p ^ (4 if p % 2 else 2)) for p in range(half)],
            [(p, p ^ (2 if p % 2 else 4)) for p in range(half)],
        ]
        land = 4
        for p, n, s in offsets:
            chip, other = (s ^ p ^ land) // 2, (s ^ p) % 2
            if s % 2 and chip in (1, 2):
                chip = 3 - chip
            where[p, n] = (2 + other) * 16 if chip == 3 else other * 16 + chip
        return passes, True, land, where
    wanted = set()
    for p, n, s in offsets:
        for core in (0, 1):
            if s // 2 != p // 2:
                wanted.add((2 * (s // 2) + s % 2, 2 * (p // 2) + s % 2))
    reach = max((abs(s // 2 - p // 2) for s, p in wanted), default=0)
    passes, place = [], {(c, c): 0 for c in range(half // 2)}
    for d in range(1, reach + 1):
        for phase in (0, 1):
            pairs = []
            for s, p in sorted(wanted):
                low = min(s // 2, p // 2)
                if abs(s // 2 - p // 2) == d and (low // d) % 2 == phase:
                    pairs.append((s, p))
                    place[s // 2, p // 2] = len(passes) + 1
            if pairs:
                passes.append(pairs)
    for p, n, s in offsets:
        where[p, n] = place[s // 2, p // 2] + 16 * (s % 2 != p % 2)
    return passes, False, 0, where


def tile_facts(tiles, where):
    half = tiles // 2
    return np.array(
        [[*where[t % half], t < half] for t in range(tiles)], np.int32
    )


def encode_kernel(block_ref, count_ref, out_ref):
    neigh, capacity = block_ref.shape
    slot = lax.broadcasted_iota(jnp.int32, (1, capacity), 1)
    out_ref[...] = jnp.full(out_ref.shape, -1.0, jnp.float32)
    for n in range(neigh):
        code = jnp.where(slot < count_ref[0, n], block_ref[n:n + 1, :], -1)
        out_ref[n:n + 1, :capacity] = code.astype(jnp.float32)


def encode(block, count, width):
    neigh = block.shape[0]
    return pl.pallas_call(
        encode_kernel,
        out_shape=jax.ShapeDtypeStruct((neigh + -neigh % 8, width), jnp.float32),
        in_specs=[pl.BlockSpec(memory_space=pltpu.VMEM), pl.BlockSpec(memory_space=pltpu.SMEM)],
        out_specs=pl.BlockSpec(memory_space=pltpu.VMEM),
        cost_estimate=pl.CostEstimate(flops=4096, bytes_accessed=8192, transcendentals=0),
        name="encode",
    )(block, count)


def power(n):
    return 1 << (n - 1).bit_length()


def over(x, n):
    return x >> (n.bit_length() - 1) if n == power(n) else lax.div(x, jnp.int32(n))


def rest_of(x, n):
    return x & (n - 1) if n == power(n) else lax.rem(x, jnp.int32(n))


UNROLL = 16


def prepare_kernel(
    dims, chunks, slot_hbm, count_hbm, facts_hbm, w_hbm, split_ref, plan_ref,
    buf, slot_ref, count_ref, facts_ref, sems, small_sems,
):
    nblk, sources, capacity, groups, received = dims
    tile = lax.axis_index("comp")
    neigh = received // capacity
    slots, width = w_hbm.shape[:2]
    per = slots // chunks
    small = [
        pltpu.make_async_copy(src, dst, small_sems.at[i])
        for i, (src, dst) in enumerate(
            [(slot_hbm, slot_ref), (count_hbm, count_ref), (facts_hbm, facts_ref)]
        )
    ]
    copies = [
        pltpu.make_async_copy(
            w_hbm.at[pl.ds(i * per, per)], buf.at[pl.ds(i * per, per)], sems.at[i]
        )
        for i in range(chunks)
    ]
    for copy in small + copies:
        copy.start()
    for copy in small:
        copy.wait()

    low = power(slots + 1)
    lines = neigh + -neigh % 8
    split_ref[slots] = jnp.zeros(split_ref.shape[1:], split_ref.dtype)

    def block(b, numbers):
        count = count_ref[b]
        numbers = list(numbers)
        slot = [slot_ref[k, b] for k in range(sources)]
        place = [facts_ref[tile, over(s, capacity)] for s in slot]
        spots = []
        for k in range(sources):
            line = rest_of(place[k], 16) * lines + over(slot[k], capacity)
            group = over(place[k], 16)
            n = numbers[0]
            for g in range(1, groups):
                n = jnp.where(group == g, numbers[g], n)
            for g in range(groups):
                numbers[g] += ((group == g) & (k < count)).astype(jnp.int32)
            spots.append((group, n, (line * width + rest_of(slot[k], capacity)) * low + b * sources + k))
        for group, n, entry in spots:
            plan_ref[group, n] = entry
        for k in range(sources):
            j = b * sources + k
            w = buf[j]
            first = w.astype(jnp.bfloat16)
            rest = (w - first.astype(jnp.float32)).astype(jnp.bfloat16)
            split_ref[j, :, :width] = first
            split_ref[j, :, width:] = rest
        return tuple(numbers)

    numbers = (jnp.int32(0),) * groups
    blocks = nblk // chunks
    for i in range(chunks):
        copies[i].wait()
        numbers = lax.fori_loop(i * blocks, (i + 1) * blocks, block, numbers, unroll=2)
    for g in range(groups):
        for u in range(UNROLL):
            plan_ref[g, numbers[g] + u] = slots
        plan_ref[groups, g] = numbers[g]
    plan_ref[groups, groups] = facts_ref[tile, neigh]


def prepare(slot, count, facts, weight, dims):
    nblk, sources, capacity, groups, received = dims
    slots, width, _ = weight.shape
    chunks = 10 if nblk % 10 == 0 else 1
    smem = pl.BlockSpec(memory_space=pltpu.SMEM)
    vmem = pl.BlockSpec(memory_space=pltpu.VMEM)
    args = [pltpu.with_memory_space_constraint(a, pltpu.HBM) for a in (slot, count, facts, weight)]
    return pl.pallas_call(
        lambda *refs: prepare_kernel(dims, chunks, *refs),
        out_shape=(
            pltpu.VMEM((slots + 1, width, 2 * width), jnp.bfloat16),
            pltpu.SMEM((groups + 1, slots + UNROLL + -(slots + UNROLL) % 128), jnp.int32),
        ),
        in_specs=[pl.BlockSpec(memory_space=pl.ANY)] * 4,
        out_specs=(vmem, smem),
        scratch_shapes=[
            pltpu.VMEM(weight.shape, jnp.float32),
            pltpu.SMEM(slot.shape, jnp.int32),
            pltpu.SMEM(count.shape, jnp.int32),
            pltpu.SMEM(facts.shape, jnp.int32),
            pltpu.SemaphoreType.DMA((chunks,)),
            pltpu.SemaphoreType.DMA((3,)),
        ],
        compiler_params=pltpu.CompilerParams(vmem_limit_bytes=16 * 2**20),
        cost_estimate=pl.CostEstimate(
            flops=slots * width * width * 4, bytes_accessed=weight.size * 8, transcendentals=0
        ),
        name="prepare",
    )(*args)


def fluxes_of(air, sea, kind):
    wind_u, wind_v, air_temp, air_humid, radiation = air
    sea_temp, ice_conc, ice_temp, current_u, current_v = sea
    wet = (kind > 0).astype(jnp.float32)
    frac = jnp.clip(ice_conc, 0.0, 1.0) * (kind == 2).astype(jnp.float32)
    du = wind_u - current_u
    dv = wind_v - current_v
    speed = jnp.sqrt(du * du + dv * dv + 1.0)
    drag = 0.8 * (1.0 - frac) + 1.2 * frac

    def terms(ts, sens, albedo, latent):
        evap = 0.5 * speed * (0.6 * jnp.exp(0.3 * ts) - air_humid)
        heat = (
            sens * speed * (ts - air_temp)
            + latent * evap
            - ((1.0 - albedo) * radiation - 0.25 * ts)
        )
        return heat, evap

    heat_water, evap_water = terms(sea_temp, 0.6, 0.07, 1.0)
    heat_ice, evap_ice = terms(ice_temp, 0.4, 0.6, 1.2)
    pull = wet * drag * speed
    return (
        pull * du,
        pull * dv,
        wet * ((1.0 - frac) * heat_water + frac * heat_ice),
        wet * ((1.0 - frac) * evap_water + frac * evap_ice),
    )


def remap_group(dims, group, plan_any, x_ref, split_ref, before, acc, plan_ref, starts, base_ref, sems):
    steps, fields, nblk, sources, received, capacity, stride = dims
    span = nblk * steps
    rows = 8
    slots, width = nblk * sources, split_ref.shape[1]
    low = power(slots + 1)
    groups = plan_ref.shape[0] - 1
    plan_ref = plan_any

    lines = stride - steps * fields * nblk
    for i in range(starts.shape[0] // lines):
        code = x_ref[pl.ds(i * stride + stride - lines, lines), :]
        at = (code * steps + i * stride).astype(jnp.int32)
        starts[pl.ds(i * lines, lines), :] = jnp.where(code >= 0.0, at, -1)
    copy = pltpu.make_async_copy(starts, base_ref, sems.at[1])
    copy.start()
    acc[...] = jnp.zeros_like(acc) if before is None else before[...]
    copy.wait()

    spare = jnp.zeros((rows - fields, width), jnp.float32)

    def batch(i, carry):
        places = []
        for u in range(UNROLL):
            entry = plan_ref[group, i * UNROLL + u]
            base = base_ref[over(entry, low * width), rest_of(over(entry, low), width)]
            j = jnp.where(base < 0, slots, rest_of(entry, low))
            places.append((j, jnp.maximum(base, 0)))
        for j, base in places:
            x = []
            for m in range(steps):
                x += [x_ref[pl.ds(base + m, fields, stride=span), :], spare]
            x = jnp.concatenate(x, axis=0)
            first = x.astype(jnp.bfloat16)
            rest = (x - first.astype(jnp.float32)).astype(jnp.bfloat16)
            both = jnp.dot(
                jnp.concatenate([first, rest], axis=0), split_ref[j],
                preferred_element_type=jnp.float32,
            )
            both = both[:, :width] + both[:, width:]
            n = rows * steps
            both = both[:n] + both[n:]
            for m in range(steps):
                at = pl.ds(m * rows * nblk + over(j, sources), rows, stride=nblk)
                acc[at, :] += both[m * rows:(m + 1) * rows]
        return carry

    lax.fori_loop(0, over(plan_ref[groups, group] + UNROLL - 1, UNROLL), batch, 0)


def remap_kernel(dims, group, first, plan_any, x_ref, split_ref, *refs):
    if first:
        refs = (None,) + refs
    remap_group(dims, group, plan_any, x_ref, split_ref, *refs)


def last_kernel(
    dims, group, plan_any, x_ref, split_ref, before, state_ref, kind_ref, out_ref, acc, plan_ref,
    starts, base_ref, sems,
):
    steps, fields, nblk = dims[:3]
    span = nblk * steps
    remap_group(
        dims, group, plan_any, x_ref, split_ref, before, acc, plan_ref, starts, base_ref, sems
    )
    plan_ref = plan_any
    groups = plan_ref.shape[0] - 1
    is_air = plan_ref[groups, groups] > 0
    for m in range(steps):
        for j in range(nblk // 8):
            mapped = [acc[pl.ds((m * 8 + f) * nblk + 8 * j, 8), :] for f in range(fields)]
            own = [
                state_ref[pl.ds(f * span + 8 * j * steps + m, 8, stride=steps), :]
                for f in range(fields)
            ]
            air = [jnp.where(is_air, s, r) for s, r in zip(own, mapped)]
            sea = [jnp.where(is_air, r, s) for s, r in zip(own, mapped)]
            for o, value in enumerate(fluxes_of(air, sea, kind_ref[pl.ds(8 * j, 8), :])):
                out_ref[pl.ds(m * 4 * nblk + 32 * j + o, 8, stride=4), :] = value


def remap(dims, group, plan, x, tiles, split, before=None, last=None):
    steps, fields, nblk, sources, received, capacity, stride = dims
    width = x.shape[1]
    table = (tiles * (stride - steps * fields * nblk), width)
    sums = (steps * 8 * nblk + 8, width)
    vmem = pl.BlockSpec(memory_space=pltpu.VMEM)
    scratch = [
        pltpu.SMEM(plan.shape, jnp.int32),
        pltpu.VMEM(table, jnp.int32),
        pltpu.SMEM(table, jnp.int32),
        pltpu.SemaphoreType.DMA((2,)),
    ]
    args = [pltpu.with_memory_space_constraint(plan, pltpu.SMEM), x, pltpu.with_memory_space_constraint(split, pltpu.VMEM)]
    specs = [pl.BlockSpec(memory_space=pltpu.SMEM), vmem, vmem]
    if before is not None:
        args.append(before)
        specs.append(vmem)
    if last is None:
        out = jax.ShapeDtypeStruct(sums, jnp.float32)
        body = lambda *refs: remap_kernel(dims, group, before is None, *refs)
    else:
        args += list(last)
        specs += [vmem, vmem]
        out = jax.ShapeDtypeStruct((steps * nblk * 4, width), jnp.float32)
        scratch = [pltpu.VMEM(sums, jnp.float32)] + scratch
        body = lambda *refs: last_kernel(dims, group, *refs)
    return pl.pallas_call(
        body,
        out_shape=out,
        in_specs=specs,
        out_specs=vmem,
        scratch_shapes=scratch,
        compiler_params=pltpu.CompilerParams(vmem_limit_bytes=16 * 2**20),
        cost_estimate=pl.CostEstimate(
            flops=nblk * sources * 32 * width * width,
            bytes_accessed=split.size,
            transcendentals=0 if last is None else 2 * steps * nblk * width,
        ),
        name="remap_last" if last is not None else "remap_%d" % group,
    )(*args)


def local(state, surface_kind, send_block, send_count, src_slot, src_count, remap_weight):
    tiles = lax.axis_size("comp")
    half = tiles // 2
    steps, fields, _ = state.shape
    nblk, sources, width, _ = remap_weight.shape
    neigh, capacity = send_block.shape[1:]
    passes, relayed, land, where = exchange_plan(tiles, neigh)
    span = nblk * steps
    rows = fields * span

    def passed(array, pairs):
        return lax.ppermute(array, "comp", pairs)

    def within(pairs):
        return pairs + [(s + half, t + half) for s, t in pairs]

    def ahead(early, late):
        return lax.optimization_barrier((early, late))

    siblings = [(i, i ^ 1) for i in range(tiles)]

    mine = state.reshape(steps, fields, nblk, width).transpose(1, 2, 0, 3).reshape(rows, width)
    table = encode(send_block[0], send_count, width)
    stride = rows + table.shape[0]
    over = [(i, (i % half ^ land) + (half if i < half else 0)) for i in range(tiles)]
    across = jnp.concatenate([passed(mine, over), passed(table, over)])

    groups = 4 if relayed else 2
    received = neigh * capacity
    split, plan = prepare(
        src_slot.T, src_count, jnp.asarray(tile_facts(tiles, where)),
        remap_weight.reshape(nblk * sources, width, width),
        (nblk, sources, capacity, groups, received),
    )
    across, plan = ahead(across, plan)

    others = [passed(across, within(pairs)) for pairs in passes]
    held = 1 + len(passes)
    if relayed:
        relay = passed(others[1], within(passes[0]))
    near = jnp.concatenate([across] + others)
    sibling = passed(near, siblings)

    dims = (steps, fields, nblk, sources, received, capacity, stride)
    last = (mine, surface_kind.reshape(nblk, width))
    sums = remap(dims, 0, plan, near, held, split)
    if relayed:
        sums = remap(dims, 1, plan, sibling, held, split, sums)
        relay, sums = ahead(relay, sums)
        met = passed(relay, siblings)
        sums = remap(dims, 2, plan, relay, 1, split, sums)
        out = remap(dims, 3, plan, met, 1, split, sums, last)
    else:
        out = remap(dims, 1, plan, sibling, held, split, sums, last)
    out = out.reshape(steps, nblk, 4, width).transpose(0, 2, 1, 3)
    return out.reshape(steps, 4, nblk * width)


def solution(mesh):
    return jax.shard_map(
        local,
        mesh=mesh,
        in_specs=(
            P(None, None, ("group", "comp")),
            P("comp"),
            P("comp", None, None),
            P("comp", None),
            P("comp", None),
            P("comp"),
            P("comp", None, None, None),
        ),
        out_specs=P(None, None, ("group", "comp")),
        check_vma=False,
    )
```

```python
import jax
import jax.numpy as jnp
import numpy as np
from jax import lax
from jax.experimental import pallas as pl
from jax.experimental.pallas import tpu as pltpu
from jax.sharding import PartitionSpec as P


def exchange_plan(tiles, neigh):
    half = tiles // 2
    before, after = neigh // 2, neigh - 1 - neigh // 2
    where = np.zeros((half, neigh), np.int32)
    offsets = [
        (p, n, p + n - before)
        for p in range(half)
        for n in range(neigh)
        if 0 <= p + n - before < half
    ]
    if half == 8:
        passes = [
            [(p, p ^ (4 if p % 2 else 2)) for p in range(half)],
            [(p, p ^ (2 if p % 2 else 4)) for p in range(half)],
        ]
        land = 4
        for p, n, s in offsets:
            chip, other = (s ^ p ^ land) // 2, (s ^ p) % 2
            if s % 2 and chip in (1, 2):
                chip = 3 - chip
            where[p, n] = (2 + other) * 16 if chip == 3 else other * 16 + chip
        return passes, True, land, where
    wanted = set()
    for p, n, s in offsets:
        for core in (0, 1):
            if s // 2 != p // 2:
                wanted.add((2 * (s // 2) + s % 2, 2 * (p // 2) + s % 2))
    reach = max((abs(s // 2 - p // 2) for s, p in wanted), default=0)
    passes, place = [], {(c, c): 0 for c in range(half // 2)}
    for d in range(1, reach + 1):
        for phase in (0, 1):
            pairs = []
            for s, p in sorted(wanted):
                low = min(s // 2, p // 2)
                if abs(s // 2 - p // 2) == d and (low // d) % 2 == phase:
                    pairs.append((s, p))
                    place[s // 2, p // 2] = len(passes) + 1
            if pairs:
                passes.append(pairs)
    for p, n, s in offsets:
        where[p, n] = place[s // 2, p // 2] + 16 * (s % 2 != p % 2)
    return passes, False, 0, where


def tile_facts(tiles, where):
    half = tiles // 2
    return np.array(
        [[*where[t % half], t < half] for t in range(tiles)], np.int32
    )


def encode_kernel(block_ref, count_ref, out_ref):
    neigh, capacity = block_ref.shape
    slot = lax.broadcasted_iota(jnp.int32, (1, capacity), 1)
    out_ref[...] = jnp.full(out_ref.shape, -1.0, jnp.float32)
    for n in range(neigh):
        code = jnp.where(slot < count_ref[0, n], block_ref[n:n + 1, :], -1)
        out_ref[n:n + 1, :capacity] = code.astype(jnp.float32)


def encode(block, count, width):
    neigh = block.shape[0]
    return pl.pallas_call(
        encode_kernel,
        out_shape=jax.ShapeDtypeStruct((neigh + -neigh % 8, width), jnp.float32),
        in_specs=[pl.BlockSpec(memory_space=pltpu.VMEM), pl.BlockSpec(memory_space=pltpu.SMEM)],
        out_specs=pl.BlockSpec(memory_space=pltpu.VMEM),
        cost_estimate=pl.CostEstimate(flops=4096, bytes_accessed=8192, transcendentals=0),
        name="encode",
    )(block, count)


def power(n):
    return 1 << (n - 1).bit_length()


def over(x, n):
    return x >> (n.bit_length() - 1) if n == power(n) else lax.div(x, jnp.int32(n))


def rest_of(x, n):
    return x & (n - 1) if n == power(n) else lax.rem(x, jnp.int32(n))


UNROLL = 16
LATE = 32


def prepare_kernel(
    dims, chunks, slot_hbm, count_hbm, facts_hbm, w_hbm, split_ref, plan_ref,
    buf, slot_ref, count_ref, facts_ref, sems, small_sems,
):
    nblk, sources, capacity, groups, received = dims
    tile = lax.axis_index("comp")
    neigh = received // capacity
    slots, width = w_hbm.shape[:2]
    per = slots // chunks
    small = [
        pltpu.make_async_copy(src, dst, small_sems.at[i])
        for i, (src, dst) in enumerate(
            [(slot_hbm, slot_ref), (count_hbm, count_ref), (facts_hbm, facts_ref)]
        )
    ]
    copies = [
        pltpu.make_async_copy(
            w_hbm.at[pl.ds(i * per, per)], buf.at[pl.ds(i * per, per)], sems.at[i]
        )
        for i in range(chunks)
    ]
    for copy in small + copies:
        copy.start()
    for copy in small:
        copy.wait()

    low = power(slots + 1)
    lines = neigh + -neigh % 8
    split_ref[slots] = jnp.zeros(split_ref.shape[1:], split_ref.dtype)

    def block(b, numbers):
        count = count_ref[b]
        numbers = list(numbers)
        slot = [slot_ref[k, b] for k in range(sources)]
        place = [facts_ref[tile, over(s, capacity)] for s in slot]
        spots = []
        for k in range(sources):
            line = rest_of(place[k], 16) * lines + over(slot[k], capacity)
            group = over(place[k], 16)
            n = numbers[0]
            for g in range(1, groups):
                n = jnp.where(group == g, numbers[g], n)
            for g in range(groups):
                numbers[g] += ((group == g) & (k < count)).astype(jnp.int32)
            spots.append((group, n, (line * width + rest_of(slot[k], capacity)) * low + b * sources + k))
        for group, n, entry in spots:
            plan_ref[group, n] = entry
        for k in range(sources):
            j = b * sources + k
            w = buf[j]
            first = w.astype(jnp.bfloat16)
            rest = (w - first.astype(jnp.float32)).astype(jnp.bfloat16)
            split_ref[j, :, :width] = first
            split_ref[j, :, width:] = rest
        return tuple(numbers)

    numbers = (jnp.int32(0),) * groups
    blocks = nblk // chunks
    for i in range(chunks):
        copies[i].wait()
        numbers = lax.fori_loop(i * blocks, (i + 1) * blocks, block, numbers, unroll=2)
    for g in range(groups):
        for u in range(LATE):
            plan_ref[g, numbers[g] + u] = slots
        plan_ref[groups, g] = numbers[g]
    plan_ref[groups, groups] = facts_ref[tile, neigh]


def prepare(slot, count, facts, weight, dims):
    nblk, sources, capacity, groups, received = dims
    slots, width, _ = weight.shape
    chunks = 10 if nblk % 10 == 0 else 1
    smem = pl.BlockSpec(memory_space=pltpu.SMEM)
    vmem = pl.BlockSpec(memory_space=pltpu.VMEM)
    args = [pltpu.with_memory_space_constraint(a, pltpu.HBM) for a in (slot, count, facts, weight)]
    return pl.pallas_call(
        lambda *refs: prepare_kernel(dims, chunks, *refs),
        out_shape=(
            pltpu.VMEM((slots + 1, width, 2 * width), jnp.bfloat16),
            pltpu.SMEM((groups + 1, slots + LATE + -(slots + LATE) % 128), jnp.int32),
        ),
        in_specs=[pl.BlockSpec(memory_space=pl.ANY)] * 4,
        out_specs=(vmem, smem),
        scratch_shapes=[
            pltpu.VMEM(weight.shape, jnp.float32),
            pltpu.SMEM(slot.shape, jnp.int32),
            pltpu.SMEM(count.shape, jnp.int32),
            pltpu.SMEM(facts.shape, jnp.int32),
            pltpu.SemaphoreType.DMA((chunks,)),
            pltpu.SemaphoreType.DMA((3,)),
        ],
        compiler_params=pltpu.CompilerParams(vmem_limit_bytes=16 * 2**20),
        cost_estimate=pl.CostEstimate(
            flops=slots * width * width * 4, bytes_accessed=weight.size * 8, transcendentals=0
        ),
        name="prepare",
    )(*args)


def fluxes_of(air, sea, kind):
    wind_u, wind_v, air_temp, air_humid, radiation = air
    sea_temp, ice_conc, ice_temp, current_u, current_v = sea
    wet = (kind > 0).astype(jnp.float32)
    frac = jnp.clip(ice_conc, 0.0, 1.0) * (kind == 2).astype(jnp.float32)
    du = wind_u - current_u
    dv = wind_v - current_v
    speed = jnp.sqrt(du * du + dv * dv + 1.0)
    drag = 0.8 * (1.0 - frac) + 1.2 * frac

    def terms(ts, sens, albedo, latent):
        evap = 0.5 * speed * (0.6 * jnp.exp(0.3 * ts) - air_humid)
        heat = (
            sens * speed * (ts - air_temp)
            + latent * evap
            - ((1.0 - albedo) * radiation - 0.25 * ts)
        )
        return heat, evap

    heat_water, evap_water = terms(sea_temp, 0.6, 0.07, 1.0)
    heat_ice, evap_ice = terms(ice_temp, 0.4, 0.6, 1.2)
    pull = wet * drag * speed
    return (
        pull * du,
        pull * dv,
        wet * ((1.0 - frac) * heat_water + frac * heat_ice),
        wet * ((1.0 - frac) * evap_water + frac * evap_ice),
    )


def add_slots(dims, number, spot, x_ref, split_ref, acc, each=UNROLL):
    steps, fields, nblk, sources, received, capacity, stride = dims
    span = nblk * steps
    rows = 8
    width = split_ref.shape[1]
    spare = jnp.zeros((rows - fields, width), jnp.float32)

    def batch(i, carry):
        for j, base in [spot(i * each + u) for u in range(each)]:
            x = []
            for m in range(steps):
                x += [x_ref[pl.ds(base + m, fields, stride=span), :], spare]
            x = jnp.concatenate(x, axis=0)
            first = x.astype(jnp.bfloat16)
            rest = (x - first.astype(jnp.float32)).astype(jnp.bfloat16)
            both = jnp.dot(
                jnp.concatenate([first, rest], axis=0), split_ref[j],
                preferred_element_type=jnp.float32,
            )
            both = both[:, :width] + both[:, width:]
            n = rows * steps
            both = both[:n] + both[n:]
            for m in range(steps):
                at = pl.ds(m * rows * nblk + over(j, sources), rows, stride=nblk)
                acc[at, :] += both[m * rows:(m + 1) * rows]
        return carry

    lax.fori_loop(0, over(number + each - 1, each), batch, 0)


def find_starts(dims, x_ref, tiles, at, starts):
    steps, fields, nblk, sources, received, capacity, stride = dims
    lines = stride - steps * fields * nblk
    for i in range(tiles):
        code = x_ref[pl.ds(i * stride + stride - lines, lines), :]
        row = (code * steps + i * stride).astype(jnp.int32)
        starts[pl.ds(at + i * lines, lines), :] = jnp.where(code >= 0.0, row, -1)


def found(dims, entry, line, base_ref):
    steps, fields, nblk, sources, received, capacity, stride = dims
    low, width = power(nblk * sources + 1), base_ref.shape[1]
    base = base_ref[line + over(entry, low * width), rest_of(over(entry, low), width)]
    j = jnp.where(base < 0, nblk * sources, rest_of(entry, low))
    return j, jnp.maximum(base, 0)


def remap_kernel(dims, group, last, plan_ref, x_ref, split_ref, *refs):
    refs = list(refs)
    before = refs.pop(0) if group else None
    state_ref, kind_ref = (refs.pop(0), refs.pop(0)) if last else (None, None)
    out_ref = refs.pop(0)
    acc = refs.pop(0) if last else out_ref
    starts, base_ref, sem = refs
    groups = plan_ref.shape[0] - 1
    lines = dims[-1] - dims[0] * dims[1] * dims[2]
    find_starts(dims, x_ref, starts.shape[0] // lines, 0, starts)
    copy = pltpu.make_async_copy(starts, base_ref, sem)
    copy.start()
    acc[...] = jnp.zeros_like(acc) if before is None else before[...]
    copy.wait()
    add_slots(
        dims, plan_ref[groups, group], lambda i: found(dims, plan_ref[group, i], 0, base_ref),
        x_ref, split_ref, acc,
    )
    if last:
        write_fluxes(dims, plan_ref[groups, groups] > 0, state_ref, kind_ref, acc, out_ref)


def second_kernel(
    dims, tiles, plan_ref, x_ref, table_ref, split_ref, before, acc, spots_ref, starts, base_ref, sem,
):
    groups = plan_ref.shape[0] - 1
    steps = dims[0]
    lines = dims[-1] - dims[0] * dims[1] * dims[2]
    low = power(dims[2] * dims[3] + 1)
    find_starts(dims, x_ref, tiles, 0, starts)
    for g, code in enumerate((table_ref[...], x_ref[pl.ds(tiles * dims[-1], lines), :])):
        row = jnp.where(code >= 0.0, (code * steps).astype(jnp.int32), -1)
        starts[pl.ds((tiles + g) * lines, lines), :] = row
    copy = pltpu.make_async_copy(starts, base_ref, sem)
    copy.start()
    acc[...] = before[...]
    copy.wait()
    add_slots(
        dims, plan_ref[groups, 1], lambda i: found(dims, plan_ref[1, i], 0, base_ref),
        x_ref, split_ref, acc,
    )
    for g in range(2):

        def place(i, carry):
            for u in range(LATE):
                at = i * LATE + u
                j, base = found(dims, plan_ref[2 + g, at], (tiles + g) * lines, base_ref)
                spots_ref[g, at] = base * low + j
            return carry

        lax.fori_loop(0, over(plan_ref[groups, 2 + g] + LATE - 1, LATE), place, 0)


def relayed_kernel(dims, group, last, plan_ref, spots_ref, x_ref, split_ref, before, *refs):
    if last:
        state_ref, kind_ref, out_ref, acc = refs
    else:
        (acc,) = refs
    groups = plan_ref.shape[0] - 1
    low = power(dims[2] * dims[3] + 1)

    def spot(i):
        entry = spots_ref[group - 2, i]
        return rest_of(entry, low), over(entry, low)

    acc[...] = before[...]
    add_slots(dims, plan_ref[groups, group], spot, x_ref, split_ref, acc, LATE)
    if last:
        write_fluxes(dims, plan_ref[groups, groups] > 0, state_ref, kind_ref, acc, out_ref)


def write_fluxes(dims, is_air, state_ref, kind_ref, acc, out_ref):
    steps, fields, nblk = dims[:3]
    span = nblk * steps
    for m in range(steps):
        for j in range(nblk // 8):
            mapped = [acc[pl.ds((m * 8 + f) * nblk + 8 * j, 8), :] for f in range(fields)]
            own = [
                state_ref[pl.ds(f * span + 8 * j * steps + m, 8, stride=steps), :]
                for f in range(fields)
            ]
            air = [jnp.where(is_air, s, r) for s, r in zip(own, mapped)]
            sea = [jnp.where(is_air, r, s) for s, r in zip(own, mapped)]
            for o, value in enumerate(fluxes_of(air, sea, kind_ref[pl.ds(8 * j, 8), :])):
                out_ref[pl.ds(m * 4 * nblk + 32 * j + o, 8, stride=4), :] = value


def remap(dims, group, plan, x, tiles, split, before=None, last=None, table=None, spots=None):
    steps, fields, nblk, sources, received, capacity, stride = dims
    width = x.shape[1]
    lines = stride - steps * fields * nblk
    sums = jax.ShapeDtypeStruct((steps * 8 * nblk + 8, width), jnp.float32)
    smem = pl.BlockSpec(memory_space=pltpu.SMEM)
    vmem = pl.BlockSpec(memory_space=pltpu.VMEM)
    fixed = pltpu.with_memory_space_constraint
    args = [(fixed(plan, pltpu.SMEM), smem)]
    if spots is not None:
        args.append((fixed(spots, pltpu.SMEM), smem))
    args.append((x, vmem))
    if table is not None:
        args.append((table, vmem))
    args.append((fixed(split, pltpu.VMEM), vmem))
    args += [(a, vmem) for a in (before,) + (last or ()) if a is not None]
    found_in = ((tiles + 2 * (table is not None)) * lines, width)
    scratch = []
    if spots is None:
        scratch = [
            pltpu.VMEM(found_in, jnp.int32), pltpu.SMEM(found_in, jnp.int32), pltpu.SemaphoreType.DMA,
        ]
    out, out_specs = sums, vmem
    if last is not None:
        out = jax.ShapeDtypeStruct((steps * nblk * 4, width), jnp.float32)
        scratch = [pltpu.VMEM(sums.shape, jnp.float32)] + scratch
    if table is not None:
        body = lambda *refs: second_kernel(dims, tiles, *refs)
        out = (sums, pltpu.SMEM((2, plan.shape[1]), jnp.int32))
        out_specs = (vmem, smem)
    elif spots is not None:
        body = lambda *refs: relayed_kernel(dims, group, last is not None, *refs)
    else:
        body = lambda *refs: remap_kernel(dims, group, last is not None, *refs)
    return pl.pallas_call(
        body,
        out_shape=out,
        in_specs=[spec for _, spec in args],
        out_specs=out_specs,
        scratch_shapes=scratch,
        compiler_params=pltpu.CompilerParams(vmem_limit_bytes=16 * 2**20),
        cost_estimate=pl.CostEstimate(
            flops=nblk * sources * 32 * width * width,
            bytes_accessed=split.size,
            transcendentals=0 if last is None else 2 * steps * nblk * width,
        ),
        name="remap_last" if last is not None else "remap_%d" % group,
    )(*[arg for arg, _ in args])


def local(state, surface_kind, send_block, send_count, src_slot, src_count, remap_weight):
    tiles = lax.axis_size("comp")
    half = tiles // 2
    steps, fields, _ = state.shape
    nblk, sources, width, _ = remap_weight.shape
    neigh, capacity = send_block.shape[1:]
    passes, relayed, land, where = exchange_plan(tiles, neigh)
    span = nblk * steps
    rows = fields * span

    def passed(array, pairs):
        return lax.ppermute(array, "comp", pairs)

    def within(pairs):
        return pairs + [(s + half, t + half) for s, t in pairs]

    def ahead(early, late):
        return lax.optimization_barrier((early, late))

    siblings = [(i, i ^ 1) for i in range(tiles)]

    mine = state.reshape(steps, fields, nblk, width).transpose(1, 2, 0, 3).reshape(rows, width)
    table = encode(send_block[0], send_count, width)
    stride = rows + table.shape[0]
    crossing = [(i, (i % half ^ land) + (half if i < half else 0)) for i in range(tiles)]
    landed, table = passed(mine, crossing), passed(table, crossing)

    groups = 4 if relayed else 2
    received = neigh * capacity
    split, plan = prepare(
        src_slot.T, src_count, jnp.asarray(tile_facts(tiles, where)),
        remap_weight.reshape(nblk * sources, width, width),
        (nblk, sources, capacity, groups, received),
    )
    (landed, table), plan = ahead((landed, table), plan)
    across = jnp.concatenate([landed, table])

    others = [passed(across, within(pairs)) for pairs in passes]
    held = 1 + len(passes)
    if relayed:
        relay = passed(others[1], within(passes[0]))
        table = passed(table, within([(p, p ^ 6) for p in range(half)]))
    near = jnp.concatenate([across] + others + [table] * relayed)
    sibling = passed(near, siblings)

    dims = (steps, fields, nblk, sources, received, capacity, stride)
    last = (mine, surface_kind.reshape(nblk, width))
    sums = remap(dims, 0, plan, near, held, split)
    if relayed:
        sums, spots = remap(dims, 1, plan, sibling, held, split, sums, table=table)
        relay, sums = ahead(relay, sums)
        met = passed(relay, siblings)
        sums = remap(dims, 2, plan, relay, 1, split, sums, spots=spots)
        out = remap(dims, 3, plan, met, 1, split, sums, last, spots=spots)
    else:
        out = remap(dims, 1, plan, sibling, held, split, sums, last)
    out = out.reshape(steps, nblk, 4, width).transpose(0, 2, 1, 3)
    return out.reshape(steps, 4, nblk * width)


def solution(mesh):
    return jax.shard_map(
        local,
        mesh=mesh,
        in_specs=(
            P(None, None, ("group", "comp")),
            P("comp"),
            P("comp", None, None),
            P("comp", None),
            P("comp", None),
            P("comp"),
            P("comp", None, None, None),
        ),
        out_specs=P(None, None, ("group", "comp")),
        check_vma=False,
    )
```

```python
import jax
import jax.numpy as jnp
import numpy as np
from jax import lax
from jax.experimental import pallas as pl
from jax.experimental.pallas import tpu as pltpu
from jax.sharding import PartitionSpec as P


def exchange_plan(tiles, neigh):
    half = tiles // 2
    before, after = neigh // 2, neigh - 1 - neigh // 2
    where = np.zeros((half, neigh), np.int32)
    offsets = [
        (p, n, p + n - before)
        for p in range(half)
        for n in range(neigh)
        if 0 <= p + n - before < half
    ]
    if half == 8:
        passes = [
            [(p, p ^ (4 if p % 2 else 2)) for p in range(half)],
            [(p, p ^ (2 if p % 2 else 4)) for p in range(half)],
        ]
        land = 4
        for p, n, s in offsets:
            chip, other = (s ^ p ^ land) // 2, (s ^ p) % 2
            if s % 2 and chip in (1, 2):
                chip = 3 - chip
            where[p, n] = (2 + other) * 16 if chip == 3 else other * 16 + chip
        return passes, True, land, where
    wanted = set()
    for p, n, s in offsets:
        for core in (0, 1):
            if s // 2 != p // 2:
                wanted.add((2 * (s // 2) + s % 2, 2 * (p // 2) + s % 2))
    reach = max((abs(s // 2 - p // 2) for s, p in wanted), default=0)
    passes, place = [], {(c, c): 0 for c in range(half // 2)}
    for d in range(1, reach + 1):
        for phase in (0, 1):
            pairs = []
            for s, p in sorted(wanted):
                low = min(s // 2, p // 2)
                if abs(s // 2 - p // 2) == d and (low // d) % 2 == phase:
                    pairs.append((s, p))
                    place[s // 2, p // 2] = len(passes) + 1
            if pairs:
                passes.append(pairs)
    for p, n, s in offsets:
        where[p, n] = place[s // 2, p // 2] + 16 * (s % 2 != p % 2)
    return passes, False, 0, where


def tile_facts(tiles, where):
    half = tiles // 2
    return np.array(
        [[*where[t % half], t < half] for t in range(tiles)], np.int32
    )


def encode_kernel(block_ref, count_ref, out_ref):
    neigh, capacity = block_ref.shape
    slot = lax.broadcasted_iota(jnp.int32, (1, capacity), 1)
    out_ref[...] = jnp.full(out_ref.shape, -1.0, jnp.float32)
    for n in range(neigh):
        code = jnp.where(slot < count_ref[0, n], block_ref[n:n + 1, :], -1)
        out_ref[n:n + 1, :capacity] = code.astype(jnp.float32)


def encode(block, count, width):
    neigh = block.shape[0]
    return pl.pallas_call(
        encode_kernel,
        out_shape=jax.ShapeDtypeStruct((neigh + -neigh % 8, width), jnp.float32),
        in_specs=[pl.BlockSpec(memory_space=pltpu.VMEM), pl.BlockSpec(memory_space=pltpu.SMEM)],
        out_specs=pl.BlockSpec(memory_space=pltpu.VMEM),
        cost_estimate=pl.CostEstimate(flops=4096, bytes_accessed=8192, transcendentals=0),
        name="encode",
    )(block, count)


def power(n):
    return 1 << (n - 1).bit_length()


def over(x, n):
    return x >> (n.bit_length() - 1) if n == power(n) else lax.div(x, jnp.int32(n))


def rest_of(x, n):
    return x & (n - 1) if n == power(n) else lax.rem(x, jnp.int32(n))


UNROLL = 16
LATE = 32


def prepare_kernel(
    dims, chunks, slot_hbm, count_hbm, facts_hbm, w_hbm, split_ref, plan_ref,
    buf, slot_ref, count_ref, facts_ref, sems, small_sems,
):
    nblk, sources, capacity, groups, received = dims
    tile = lax.axis_index("comp")
    neigh = received // capacity
    slots, width = w_hbm.shape[:2]
    per = slots // chunks
    small = [
        pltpu.make_async_copy(src, dst, small_sems.at[i])
        for i, (src, dst) in enumerate(
            [(slot_hbm, slot_ref), (count_hbm, count_ref), (facts_hbm, facts_ref)]
        )
    ]
    copies = [
        pltpu.make_async_copy(
            w_hbm.at[pl.ds(i * per, per)], buf.at[pl.ds(i * per, per)], sems.at[i]
        )
        for i in range(chunks)
    ]
    for copy in small + copies:
        copy.start()
    for copy in small:
        copy.wait()

    low = power(slots + 1)
    lines = neigh + -neigh % 8
    split_ref[slots] = jnp.zeros(split_ref.shape[1:], split_ref.dtype)

    def block(b, numbers):
        count = count_ref[b]
        numbers = list(numbers)
        slot = [slot_ref[k, b] for k in range(sources)]
        place = [facts_ref[tile, over(s, capacity)] for s in slot]
        spots = []
        for k in range(sources):
            line = rest_of(place[k], 16) * lines + over(slot[k], capacity)
            group = over(place[k], 16)
            n = numbers[0]
            for g in range(1, groups):
                n = jnp.where(group == g, numbers[g], n)
            for g in range(groups):
                numbers[g] += ((group == g) & (k < count)).astype(jnp.int32)
            spots.append((group, n, (line * width + rest_of(slot[k], capacity)) * low + b * sources + k))
        for group, n, entry in spots:
            plan_ref[group, n] = entry
        for k in range(sources):
            j = b * sources + k
            w = buf[j]
            first = w.astype(jnp.bfloat16)
            rest = (w - first.astype(jnp.float32)).astype(jnp.bfloat16)
            split_ref[j, :, :width] = first
            split_ref[j, :, width:] = rest
        return tuple(numbers)

    numbers = (jnp.int32(0),) * groups
    blocks = nblk // chunks
    for i in range(chunks):
        copies[i].wait()
        numbers = lax.fori_loop(i * blocks, (i + 1) * blocks, block, numbers, unroll=2)
    for g in range(groups):
        for u in range(LATE):
            plan_ref[g, numbers[g] + u] = slots
        plan_ref[groups, g] = numbers[g]
    plan_ref[groups, groups] = facts_ref[tile, neigh]


def prepare(slot, count, facts, weight, dims):
    nblk, sources, capacity, groups, received = dims
    slots, width, _ = weight.shape
    chunks = 10 if nblk % 10 == 0 else 1
    smem = pl.BlockSpec(memory_space=pltpu.SMEM)
    vmem = pl.BlockSpec(memory_space=pltpu.VMEM)
    args = [pltpu.with_memory_space_constraint(a, pltpu.HBM) for a in (slot, count, facts, weight)]
    return pl.pallas_call(
        lambda *refs: prepare_kernel(dims, chunks, *refs),
        out_shape=(
            pltpu.VMEM((slots + 1, width, 2 * width), jnp.bfloat16),
            pltpu.SMEM((groups + 1, slots + LATE + -(slots + LATE) % 128), jnp.int32),
        ),
        in_specs=[pl.BlockSpec(memory_space=pl.ANY)] * 4,
        out_specs=(vmem, smem),
        scratch_shapes=[
            pltpu.VMEM(weight.shape, jnp.float32),
            pltpu.SMEM(slot.shape, jnp.int32),
            pltpu.SMEM(count.shape, jnp.int32),
            pltpu.SMEM(facts.shape, jnp.int32),
            pltpu.SemaphoreType.DMA((chunks,)),
            pltpu.SemaphoreType.DMA((3,)),
        ],
        compiler_params=pltpu.CompilerParams(vmem_limit_bytes=16 * 2**20),
        cost_estimate=pl.CostEstimate(
            flops=slots * width * width * 4, bytes_accessed=weight.size * 8, transcendentals=0
        ),
        name="prepare",
    )(*args)


def fluxes_of(air, sea, kind):
    wind_u, wind_v, air_temp, air_humid, radiation = air
    sea_temp, ice_conc, ice_temp, current_u, current_v = sea
    wet = (kind > 0).astype(jnp.float32)
    frac = jnp.clip(ice_conc, 0.0, 1.0) * (kind == 2).astype(jnp.float32)
    du = wind_u - current_u
    dv = wind_v - current_v
    speed = jnp.sqrt(du * du + dv * dv + 1.0)
    drag = 0.8 * (1.0 - frac) + 1.2 * frac

    def terms(ts, sens, albedo, latent):
        evap = 0.5 * speed * (0.6 * jnp.exp(0.3 * ts) - air_humid)
        heat = (
            sens * speed * (ts - air_temp)
            + latent * evap
            - ((1.0 - albedo) * radiation - 0.25 * ts)
        )
        return heat, evap

    heat_water, evap_water = terms(sea_temp, 0.6, 0.07, 1.0)
    heat_ice, evap_ice = terms(ice_temp, 0.4, 0.6, 1.2)
    pull = wet * drag * speed
    return (
        pull * du,
        pull * dv,
        wet * ((1.0 - frac) * heat_water + frac * heat_ice),
        wet * ((1.0 - frac) * evap_water + frac * evap_ice),
    )


def add_slots(dims, number, spot, x_ref, split_ref, acc, each=UNROLL):
    steps, fields, nblk, sources, received, capacity, stride = dims
    span = nblk * steps
    rows = 8
    width = split_ref.shape[1]
    spare = jnp.zeros((rows - fields, width), jnp.float32)

    def batch(i, carry):
        for j, base in [spot(i * each + u) for u in range(each)]:
            x = []
            for m in range(steps):
                x += [x_ref[pl.ds(base + m, fields, stride=span), :], spare]
            x = jnp.concatenate(x, axis=0)
            first = x.astype(jnp.bfloat16)
            rest = (x - first.astype(jnp.float32)).astype(jnp.bfloat16)
            both = jnp.dot(
                jnp.concatenate([first, rest], axis=0), split_ref[j],
                preferred_element_type=jnp.float32,
            )
            both = both[:, :width] + both[:, width:]
            n = rows * steps
            both = both[:n] + both[n:]
            for m in range(steps):
                at = pl.ds(m * rows * nblk + over(j, sources), rows, stride=nblk)
                acc[at, :] += both[m * rows:(m + 1) * rows]
        return carry

    lax.fori_loop(0, over(number + each - 1, each), batch, 0)


def find_starts(dims, x_ref, tiles, at, starts):
    steps, fields, nblk, sources, received, capacity, stride = dims
    lines = stride - steps * fields * nblk
    for i in range(tiles):
        code = x_ref[pl.ds(i * stride + stride - lines, lines), :]
        row = (code * steps + i * stride).astype(jnp.int32)
        starts[pl.ds(at + i * lines, lines), :] = jnp.where(code >= 0.0, row, -1)


def found(dims, entry, line, base_ref):
    steps, fields, nblk, sources, received, capacity, stride = dims
    low, width = power(nblk * sources + 1), base_ref.shape[1]
    base = base_ref[line + over(entry, low * width), rest_of(over(entry, low), width)]
    j = jnp.where(base < 0, nblk * sources, rest_of(entry, low))
    return j, jnp.maximum(base, 0)


def remap_kernel(dims, group, last, plan_ref, x_ref, split_ref, *refs):
    refs = list(refs)
    before = refs.pop(0) if group else None
    state_ref, kind_ref = (refs.pop(0), refs.pop(0)) if last else (None, None)
    out_ref = refs.pop(0)
    acc = refs.pop(0) if last else out_ref
    starts, base_ref, sem = refs
    groups = plan_ref.shape[0] - 1
    lines = dims[-1] - dims[0] * dims[1] * dims[2]
    find_starts(dims, x_ref, starts.shape[0] // lines, 0, starts)
    copy = pltpu.make_async_copy(starts, base_ref, sem)
    copy.start()
    acc[...] = jnp.zeros_like(acc) if before is None else before[...]
    copy.wait()
    add_slots(
        dims, plan_ref[groups, group], lambda i: found(dims, plan_ref[group, i], 0, base_ref),
        x_ref, split_ref, acc,
    )
    if last:
        write_fluxes(dims, plan_ref[groups, groups] > 0, state_ref, kind_ref, acc, out_ref)


def second_kernel(
    dims, tiles, plan_ref, x_ref, table_ref, split_ref, before, acc, spots_ref, starts, base_ref, sem,
):
    groups = plan_ref.shape[0] - 1
    steps = dims[0]
    lines = dims[-1] - dims[0] * dims[1] * dims[2]
    low = power(dims[2] * dims[3] + 1)
    find_starts(dims, x_ref, tiles, 0, starts)
    for g, code in enumerate((x_ref[pl.ds(tiles * dims[-1], lines), :], table_ref[...])):
        row = jnp.where(code >= 0.0, (code * steps).astype(jnp.int32), -1)
        starts[pl.ds((tiles + g) * lines, lines), :] = row
    copy = pltpu.make_async_copy(starts, base_ref, sem)
    copy.start()
    acc[...] = before[...]
    copy.wait()
    add_slots(
        dims, plan_ref[groups, 1], lambda i: found(dims, plan_ref[1, i], 0, base_ref),
        x_ref, split_ref, acc,
    )
    for g in range(2):

        def place(i, carry):
            for u in range(LATE):
                at = i * LATE + u
                j, base = found(dims, plan_ref[2 + g, at], (tiles + g) * lines, base_ref)
                spots_ref[g, at] = base * low + j
            return carry

        lax.fori_loop(0, over(plan_ref[groups, 2 + g] + LATE - 1, LATE), place, 0)


def relayed_kernel(dims, group, last, plan_ref, spots_ref, x_ref, split_ref, before, *refs):
    if last:
        state_ref, kind_ref, out_ref, acc = refs
    else:
        (acc,) = refs
    groups = plan_ref.shape[0] - 1
    low = power(dims[2] * dims[3] + 1)

    def spot(i):
        entry = spots_ref[group - 2, i]
        return rest_of(entry, low), over(entry, low)

    acc[...] = before[...]
    add_slots(dims, plan_ref[groups, group], spot, x_ref, split_ref, acc, LATE)
    if last:
        write_fluxes(dims, plan_ref[groups, groups] > 0, state_ref, kind_ref, acc, out_ref)


def write_fluxes(dims, is_air, state_ref, kind_ref, acc, out_ref):
    steps, fields, nblk = dims[:3]
    span = nblk * steps
    for m in range(steps):
        for j in range(nblk // 8):
            mapped = [acc[pl.ds((m * 8 + f) * nblk + 8 * j, 8), :] for f in range(fields)]
            own = [
                state_ref[pl.ds(f * span + 8 * j * steps + m, 8, stride=steps), :]
                for f in range(fields)
            ]
            air = [jnp.where(is_air, s, r) for s, r in zip(own, mapped)]
            sea = [jnp.where(is_air, r, s) for s, r in zip(own, mapped)]
            for o, value in enumerate(fluxes_of(air, sea, kind_ref[pl.ds(8 * j, 8), :])):
                out_ref[pl.ds(m * 4 * nblk + 32 * j + o, 8, stride=4), :] = value


def remap(dims, group, plan, x, tiles, split, before=None, last=None, table=None, spots=None):
    steps, fields, nblk, sources, received, capacity, stride = dims
    width = x.shape[1]
    lines = stride - steps * fields * nblk
    sums = jax.ShapeDtypeStruct((steps * 8 * nblk + 8, width), jnp.float32)
    smem = pl.BlockSpec(memory_space=pltpu.SMEM)
    vmem = pl.BlockSpec(memory_space=pltpu.VMEM)
    fixed = pltpu.with_memory_space_constraint
    args = [(fixed(plan, pltpu.SMEM), smem)]
    if spots is not None:
        args.append((fixed(spots, pltpu.SMEM), smem))
    args.append((x, vmem))
    if table is not None:
        args.append((table, vmem))
    args.append((fixed(split, pltpu.VMEM), vmem))
    args += [(a, vmem) for a in (before,) + (last or ()) if a is not None]
    found_in = ((tiles + 2 * (table is not None)) * lines, width)
    scratch = []
    if spots is None:
        scratch = [
            pltpu.VMEM(found_in, jnp.int32), pltpu.SMEM(found_in, jnp.int32), pltpu.SemaphoreType.DMA,
        ]
    out, out_specs = sums, vmem
    if last is not None:
        out = jax.ShapeDtypeStruct((steps * nblk * 4, width), jnp.float32)
        scratch = [pltpu.VMEM(sums.shape, jnp.float32)] + scratch
    if table is not None:
        body = lambda *refs: second_kernel(dims, tiles, *refs)
        out = (sums, pltpu.SMEM((2, plan.shape[1]), jnp.int32))
        out_specs = (vmem, smem)
    elif spots is not None:
        body = lambda *refs: relayed_kernel(dims, group, last is not None, *refs)
    else:
        body = lambda *refs: remap_kernel(dims, group, last is not None, *refs)
    return pl.pallas_call(
        body,
        out_shape=out,
        in_specs=[spec for _, spec in args],
        out_specs=out_specs,
        scratch_shapes=scratch,
        compiler_params=pltpu.CompilerParams(vmem_limit_bytes=16 * 2**20),
        cost_estimate=pl.CostEstimate(
            flops=nblk * sources * 32 * width * width,
            bytes_accessed=split.size,
            transcendentals=0 if last is None else 2 * steps * nblk * width,
        ),
        name="remap_last" if last is not None else "remap_%d" % group,
    )(*[arg for arg, _ in args])


def local(state, surface_kind, send_block, send_count, src_slot, src_count, remap_weight):
    tiles = lax.axis_size("comp")
    half = tiles // 2
    steps, fields, _ = state.shape
    nblk, sources, width, _ = remap_weight.shape
    neigh, capacity = send_block.shape[1:]
    passes, relayed, land, where = exchange_plan(tiles, neigh)
    span = nblk * steps
    rows = fields * span

    def passed(array, pairs):
        return lax.ppermute(array, "comp", pairs)

    def within(pairs):
        return pairs + [(s + half, t + half) for s, t in pairs]

    def ahead(early, late):
        return lax.optimization_barrier((early, late))

    siblings = [(i, i ^ 1) for i in range(tiles)]

    mine = state.reshape(steps, fields, nblk, width).transpose(1, 2, 0, 3).reshape(rows, width)
    table = encode(send_block[0], send_count, width)
    stride = rows + table.shape[0]
    crossing = [(i, (i % half ^ land) + (half if i < half else 0)) for i in range(tiles)]
    landed, table = passed(mine, crossing), passed(table, crossing)

    groups = 4 if relayed else 2
    received = neigh * capacity
    split, plan = prepare(
        src_slot.T, src_count, jnp.asarray(tile_facts(tiles, where)),
        remap_weight.reshape(nblk * sources, width, width),
        (nblk, sources, capacity, groups, received),
    )
    (landed, table), plan = ahead((landed, table), plan)
    across = jnp.concatenate([landed, table])

    others = [passed(across, within(pairs)) for pairs in passes]
    held = 1 + len(passes)
    if relayed:
        relay = passed(others[1], within(passes[0]))
        table = passed(table, within([(p, p ^ 7) for p in range(half)]))
    near = jnp.concatenate([across] + others + [table] * relayed)
    sibling = passed(near, siblings)

    dims = (steps, fields, nblk, sources, received, capacity, stride)
    last = (mine, surface_kind.reshape(nblk, width))
    sums = remap(dims, 0, plan, near, held, split)
    if relayed:
        sums, spots = remap(dims, 1, plan, sibling, held, split, sums, table=table)
        relay, sums = ahead(relay, sums)
        met = passed(relay, siblings)
        sums = remap(dims, 2, plan, relay, 1, split, sums, spots=spots)
        out = remap(dims, 3, plan, met, 1, split, sums, last, spots=spots)
    else:
        out = remap(dims, 1, plan, sibling, held, split, sums, last)
    out = out.reshape(steps, nblk, 4, width).transpose(0, 2, 1, 3)
    return out.reshape(steps, 4, nblk * width)


def solution(mesh):
    return jax.shard_map(
        local,
        mesh=mesh,
        in_specs=(
            P(None, None, ("group", "comp")),
            P("comp"),
            P("comp", None, None),
            P("comp", None),
            P("comp", None),
            P("comp"),
            P("comp", None, None, None),
        ),
        out_specs=P(None, None, ("group", "comp")),
        check_vma=False,
    )
```

```python
import jax
import jax.numpy as jnp
import numpy as np
from jax import lax
from jax.experimental import pallas as pl
from jax.experimental.pallas import tpu as pltpu
from jax.sharding import PartitionSpec as P


def exchange_plan(tiles, neigh):
    half = tiles // 2
    before, after = neigh // 2, neigh - 1 - neigh // 2
    where = np.zeros((half, neigh), np.int32)
    offsets = [
        (p, n, p + n - before)
        for p in range(half)
        for n in range(neigh)
        if 0 <= p + n - before < half
    ]
    if half == 8:
        passes = [
            [(p, p ^ (4 if p % 2 else 2)) for p in range(half)],
            [(p, p ^ (2 if p % 2 else 4)) for p in range(half)],
        ]
        land = 4
        for p, n, s in offsets:
            chip, other = (s ^ p ^ land) // 2, (s ^ p) % 2
            if s % 2 and chip in (1, 2):
                chip = 3 - chip
            where[p, n] = (3 - other) * 16 if chip == 3 else other * 16 + chip
        return passes, True, land, where
    wanted = set()
    for p, n, s in offsets:
        for core in (0, 1):
            if s // 2 != p // 2:
                wanted.add((2 * (s // 2) + s % 2, 2 * (p // 2) + s % 2))
    reach = max((abs(s // 2 - p // 2) for s, p in wanted), default=0)
    passes, place = [], {(c, c): 0 for c in range(half // 2)}
    for d in range(1, reach + 1):
        for phase in (0, 1):
            pairs = []
            for s, p in sorted(wanted):
                low = min(s // 2, p // 2)
                if abs(s // 2 - p // 2) == d and (low // d) % 2 == phase:
                    pairs.append((s, p))
                    place[s // 2, p // 2] = len(passes) + 1
            if pairs:
                passes.append(pairs)
    for p, n, s in offsets:
        where[p, n] = place[s // 2, p // 2] + 16 * (s % 2 != p % 2)
    return passes, False, 0, where


def tile_facts(tiles, where):
    half = tiles // 2
    return np.array(
        [[*where[t % half], t < half] for t in range(tiles)], np.int32
    )


def encode_kernel(block_ref, count_ref, out_ref):
    neigh, capacity = block_ref.shape
    slot = lax.broadcasted_iota(jnp.int32, (1, capacity), 1)
    out_ref[...] = jnp.full(out_ref.shape, -1.0, jnp.float32)
    for n in range(neigh):
        code = jnp.where(slot < count_ref[0, n], block_ref[n:n + 1, :], -1)
        out_ref[n:n + 1, :capacity] = code.astype(jnp.float32)


def encode(block, count, width):
    neigh = block.shape[0]
    return pl.pallas_call(
        encode_kernel,
        out_shape=jax.ShapeDtypeStruct((neigh + -neigh % 8, width), jnp.float32),
        in_specs=[pl.BlockSpec(memory_space=pltpu.VMEM), pl.BlockSpec(memory_space=pltpu.SMEM)],
        out_specs=pl.BlockSpec(memory_space=pltpu.VMEM),
        cost_estimate=pl.CostEstimate(flops=4096, bytes_accessed=8192, transcendentals=0),
        name="encode",
    )(block, count)


def power(n):
    return 1 << (n - 1).bit_length()


def over(x, n):
    return x >> (n.bit_length() - 1) if n == power(n) else lax.div(x, jnp.int32(n))


def rest_of(x, n):
    return x & (n - 1) if n == power(n) else lax.rem(x, jnp.int32(n))


UNROLL = 16
LATE = 32


def prepare_kernel(
    dims, chunks, slot_hbm, count_hbm, facts_hbm, w_hbm, split_ref, plan_ref,
    buf, slot_ref, count_ref, facts_ref, sems, small_sems,
):
    nblk, sources, capacity, groups, received = dims
    tile = lax.axis_index("comp")
    neigh = received // capacity
    slots, width = w_hbm.shape[:2]
    per = slots // chunks
    small = [
        pltpu.make_async_copy(src, dst, small_sems.at[i])
        for i, (src, dst) in enumerate(
            [(slot_hbm, slot_ref), (count_hbm, count_ref), (facts_hbm, facts_ref)]
        )
    ]
    copies = [
        pltpu.make_async_copy(
            w_hbm.at[pl.ds(i * per, per)], buf.at[pl.ds(i * per, per)], sems.at[i]
        )
        for i in range(chunks)
    ]
    for copy in small + copies:
        copy.start()
    for copy in small:
        copy.wait()

    low = power(slots + 1)
    lines = neigh + -neigh % 8
    split_ref[slots] = jnp.zeros(split_ref.shape[1:], split_ref.dtype)

    def block(b, numbers):
        count = count_ref[b]
        numbers = list(numbers)
        slot = [slot_ref[k, b] for k in range(sources)]
        place = [facts_ref[tile, over(s, capacity)] for s in slot]
        spots = []
        for k in range(sources):
            line = rest_of(place[k], 16) * lines + over(slot[k], capacity)
            group = over(place[k], 16)
            n = numbers[0]
            for g in range(1, groups):
                n = jnp.where(group == g, numbers[g], n)
            for g in range(groups):
                numbers[g] += ((group == g) & (k < count)).astype(jnp.int32)
            spots.append((group, n, (line * width + rest_of(slot[k], capacity)) * low + b * sources + k))
        for group, n, entry in spots:
            plan_ref[group, n] = entry
        for k in range(sources):
            j = b * sources + k
            w = buf[j]
            first = w.astype(jnp.bfloat16)
            rest = (w - first.astype(jnp.float32)).astype(jnp.bfloat16)
            split_ref[j, :, :width] = first
            split_ref[j, :, width:] = rest
        return tuple(numbers)

    numbers = (jnp.int32(0),) * groups
    blocks = nblk // chunks
    for i in range(chunks):
        copies[i].wait()
        numbers = lax.fori_loop(i * blocks, (i + 1) * blocks, block, numbers, unroll=2)
    for g in range(groups):
        for u in range(LATE):
            plan_ref[g, numbers[g] + u] = slots
        plan_ref[groups, g] = numbers[g]
    plan_ref[groups, groups] = facts_ref[tile, neigh]


def prepare(slot, count, facts, weight, dims):
    nblk, sources, capacity, groups, received = dims
    slots, width, _ = weight.shape
    chunks = 10 if nblk % 10 == 0 else 1
    smem = pl.BlockSpec(memory_space=pltpu.SMEM)
    vmem = pl.BlockSpec(memory_space=pltpu.VMEM)
    args = [pltpu.with_memory_space_constraint(a, pltpu.HBM) for a in (slot, count, facts, weight)]
    return pl.pallas_call(
        lambda *refs: prepare_kernel(dims, chunks, *refs),
        out_shape=(
            pltpu.VMEM((slots + 1, width, 2 * width), jnp.bfloat16),
            pltpu.SMEM((groups + 1, slots + LATE + -(slots + LATE) % 128), jnp.int32),
        ),
        in_specs=[pl.BlockSpec(memory_space=pl.ANY)] * 4,
        out_specs=(vmem, smem),
        scratch_shapes=[
            pltpu.VMEM(weight.shape, jnp.float32),
            pltpu.SMEM(slot.shape, jnp.int32),
            pltpu.SMEM(count.shape, jnp.int32),
            pltpu.SMEM(facts.shape, jnp.int32),
            pltpu.SemaphoreType.DMA((chunks,)),
            pltpu.SemaphoreType.DMA((3,)),
        ],
        compiler_params=pltpu.CompilerParams(vmem_limit_bytes=16 * 2**20),
        cost_estimate=pl.CostEstimate(
            flops=slots * width * width * 4, bytes_accessed=weight.size * 8, transcendentals=0
        ),
        name="prepare",
    )(*args)


def fluxes_of(air, sea, kind):
    wind_u, wind_v, air_temp, air_humid, radiation = air
    sea_temp, ice_conc, ice_temp, current_u, current_v = sea
    wet = (kind > 0).astype(jnp.float32)
    frac = jnp.clip(ice_conc, 0.0, 1.0) * (kind == 2).astype(jnp.float32)
    du = wind_u - current_u
    dv = wind_v - current_v
    speed = jnp.sqrt(du * du + dv * dv + 1.0)
    drag = 0.8 * (1.0 - frac) + 1.2 * frac

    def terms(ts, sens, albedo, latent):
        evap = 0.5 * speed * (0.6 * jnp.exp(0.3 * ts) - air_humid)
        heat = (
            sens * speed * (ts - air_temp)
            + latent * evap
            - ((1.0 - albedo) * radiation - 0.25 * ts)
        )
        return heat, evap

    heat_water, evap_water = terms(sea_temp, 0.6, 0.07, 1.0)
    heat_ice, evap_ice = terms(ice_temp, 0.4, 0.6, 1.2)
    pull = wet * drag * speed
    return (
        pull * du,
        pull * dv,
        wet * ((1.0 - frac) * heat_water + frac * heat_ice),
        wet * ((1.0 - frac) * evap_water + frac * evap_ice),
    )


def add_slots(dims, number, spot, x_ref, split_ref, acc, each=UNROLL):
    steps, fields, nblk, sources, received, capacity, stride = dims
    span = nblk * steps
    rows = 8
    width = split_ref.shape[1]
    spare = jnp.zeros((rows - fields, width), jnp.float32)

    def batch(i, carry):
        for j, base in [spot(i * each + u) for u in range(each)]:
            x = []
            for m in range(steps):
                x += [x_ref[pl.ds(base + m, fields, stride=span), :], spare]
            x = jnp.concatenate(x, axis=0)
            first = x.astype(jnp.bfloat16)
            rest = (x - first.astype(jnp.float32)).astype(jnp.bfloat16)
            both = jnp.dot(
                jnp.concatenate([first, rest], axis=0), split_ref[j],
                preferred_element_type=jnp.float32,
            )
            both = both[:, :width] + both[:, width:]
            n = rows * steps
            both = both[:n] + both[n:]
            for m in range(steps):
                at = pl.ds(m * rows * nblk + over(j, sources), rows, stride=nblk)
                acc[at, :] += both[m * rows:(m + 1) * rows]
        return carry

    lax.fori_loop(0, over(number + each - 1, each), batch, 0)


def find_starts(dims, x_ref, tiles, at, starts):
    steps, fields, nblk, sources, received, capacity, stride = dims
    lines = stride - steps * fields * nblk
    for i in range(tiles):
        code = x_ref[pl.ds(i * stride + stride - lines, lines), :]
        row = (code * steps + i * stride).astype(jnp.int32)
        starts[pl.ds(at + i * lines, lines), :] = jnp.where(code >= 0.0, row, -1)


def found(dims, entry, line, base_ref):
    steps, fields, nblk, sources, received, capacity, stride = dims
    low, width = power(nblk * sources + 1), base_ref.shape[1]
    base = base_ref[line + over(entry, low * width), rest_of(over(entry, low), width)]
    j = jnp.where(base < 0, nblk * sources, rest_of(entry, low))
    return j, jnp.maximum(base, 0)


def remap_kernel(dims, group, last, plan_ref, x_ref, split_ref, *refs):
    refs = list(refs)
    before = refs.pop(0) if group else None
    state_ref, kind_ref = (refs.pop(0), refs.pop(0)) if last else (None, None)
    out_ref = refs.pop(0)
    acc = refs.pop(0) if last else out_ref
    starts, base_ref, sem = refs
    groups = plan_ref.shape[0] - 1
    lines = dims[-1] - dims[0] * dims[1] * dims[2]
    find_starts(dims, x_ref, starts.shape[0] // lines, 0, starts)
    copy = pltpu.make_async_copy(starts, base_ref, sem)
    copy.start()
    acc[...] = jnp.zeros_like(acc) if before is None else before[...]
    copy.wait()
    add_slots(
        dims, plan_ref[groups, group], lambda i: found(dims, plan_ref[group, i], 0, base_ref),
        x_ref, split_ref, acc,
    )
    if last:
        write_fluxes(dims, plan_ref[groups, groups] > 0, state_ref, kind_ref, acc, out_ref)


def second_kernel(
    dims, tiles, plan_ref, x_ref, table_ref, split_ref, before, acc, spots_ref, starts, base_ref, sem,
):
    groups = plan_ref.shape[0] - 1
    steps = dims[0]
    lines = dims[-1] - dims[0] * dims[1] * dims[2]
    low = power(dims[2] * dims[3] + 1)
    find_starts(dims, x_ref, tiles, 0, starts)
    for g, code in enumerate((table_ref[...], x_ref[pl.ds(tiles * dims[-1], lines), :])):
        row = jnp.where(code >= 0.0, (code * steps).astype(jnp.int32), -1)
        starts[pl.ds((tiles + g) * lines, lines), :] = row
    copy = pltpu.make_async_copy(starts, base_ref, sem)
    copy.start()
    acc[...] = before[...]
    copy.wait()
    add_slots(
        dims, plan_ref[groups, 1], lambda i: found(dims, plan_ref[1, i], 0, base_ref),
        x_ref, split_ref, acc,
    )
    for g in range(2):

        def place(i, carry):
            for u in range(LATE):
                at = i * LATE + u
                j, base = found(dims, plan_ref[2 + g, at], (tiles + g) * lines, base_ref)
                spots_ref[g, at] = base * low + j
            return carry

        lax.fori_loop(0, over(plan_ref[groups, 2 + g] + LATE - 1, LATE), place, 0)


def relayed_kernel(dims, group, last, plan_ref, spots_ref, x_ref, split_ref, before, *refs):
    if last:
        state_ref, kind_ref, out_ref, acc = refs
    else:
        (acc,) = refs
    groups = plan_ref.shape[0] - 1
    low = power(dims[2] * dims[3] + 1)

    def spot(i):
        entry = spots_ref[group - 2, i]
        return rest_of(entry, low), over(entry, low)

    acc[...] = before[...]
    add_slots(dims, plan_ref[groups, group], spot, x_ref, split_ref, acc, LATE)
    if last:
        write_fluxes(dims, plan_ref[groups, groups] > 0, state_ref, kind_ref, acc, out_ref)


def write_fluxes(dims, is_air, state_ref, kind_ref, acc, out_ref):
    steps, fields, nblk = dims[:3]
    span = nblk * steps
    for m in range(steps):
        for j in range(nblk // 8):
            mapped = [acc[pl.ds((m * 8 + f) * nblk + 8 * j, 8), :] for f in range(fields)]
            own = [
                state_ref[pl.ds(f * span + 8 * j * steps + m, 8, stride=steps), :]
                for f in range(fields)
            ]
            air = [jnp.where(is_air, s, r) for s, r in zip(own, mapped)]
            sea = [jnp.where(is_air, r, s) for s, r in zip(own, mapped)]
            for o, value in enumerate(fluxes_of(air, sea, kind_ref[pl.ds(8 * j, 8), :])):
                out_ref[pl.ds(m * 4 * nblk + 32 * j + o, 8, stride=4), :] = value


def remap(dims, group, plan, x, tiles, split, before=None, last=None, table=None, spots=None):
    steps, fields, nblk, sources, received, capacity, stride = dims
    width = x.shape[1]
    lines = stride - steps * fields * nblk
    sums = jax.ShapeDtypeStruct((steps * 8 * nblk + 8, width), jnp.float32)
    smem = pl.BlockSpec(memory_space=pltpu.SMEM)
    vmem = pl.BlockSpec(memory_space=pltpu.VMEM)
    fixed = pltpu.with_memory_space_constraint
    args = [(fixed(plan, pltpu.SMEM), smem)]
    if spots is not None:
        args.append((fixed(spots, pltpu.SMEM), smem))
    args.append((x, vmem))
    if table is not None:
        args.append((table, vmem))
    args.append((fixed(split, pltpu.VMEM), vmem))
    args += [(a, vmem) for a in (before,) + (last or ()) if a is not None]
    found_in = ((tiles + 2 * (table is not None)) * lines, width)
    scratch = []
    if spots is None:
        scratch = [
            pltpu.VMEM(found_in, jnp.int32), pltpu.SMEM(found_in, jnp.int32), pltpu.SemaphoreType.DMA,
        ]
    out, out_specs = sums, vmem
    if last is not None:
        out = jax.ShapeDtypeStruct((steps * nblk * 4, width), jnp.float32)
        scratch = [pltpu.VMEM(sums.shape, jnp.float32)] + scratch
    if table is not None:
        body = lambda *refs: second_kernel(dims, tiles, *refs)
        out = (sums, pltpu.SMEM((2, plan.shape[1]), jnp.int32))
        out_specs = (vmem, smem)
    elif spots is not None:
        body = lambda *refs: relayed_kernel(dims, group, last is not None, *refs)
    else:
        body = lambda *refs: remap_kernel(dims, group, last is not None, *refs)
    return pl.pallas_call(
        body,
        out_shape=out,
        in_specs=[spec for _, spec in args],
        out_specs=out_specs,
        scratch_shapes=scratch,
        compiler_params=pltpu.CompilerParams(vmem_limit_bytes=16 * 2**20),
        cost_estimate=pl.CostEstimate(
            flops=nblk * sources * 32 * width * width,
            bytes_accessed=split.size,
            transcendentals=0 if last is None else 2 * steps * nblk * width,
        ),
        name="remap_last" if last is not None else "remap_%d" % group,
    )(*[arg for arg, _ in args])


def local(state, surface_kind, send_block, send_count, src_slot, src_count, remap_weight):
    tiles = lax.axis_size("comp")
    half = tiles // 2
    steps, fields, _ = state.shape
    nblk, sources, width, _ = remap_weight.shape
    neigh, capacity = send_block.shape[1:]
    passes, relayed, land, where = exchange_plan(tiles, neigh)
    span = nblk * steps
    rows = fields * span

    def passed(array, pairs):
        return lax.ppermute(array, "comp", pairs)

    def within(pairs):
        return pairs + [(s + half, t + half) for s, t in pairs]

    def ahead(early, late):
        return lax.optimization_barrier((early, late))

    siblings = [(i, i ^ 1) for i in range(tiles)]

    mine = state.reshape(steps, fields, nblk, width).transpose(1, 2, 0, 3).reshape(rows, width)
    table = encode(send_block[0], send_count, width)
    stride = rows + table.shape[0]
    crossing = [(i, (i % half ^ land) + (half if i < half else 0)) for i in range(tiles)]
    landed, table = passed(mine, crossing), passed(table, crossing)

    groups = 4 if relayed else 2
    received = neigh * capacity
    split, plan = prepare(
        src_slot.T, src_count, jnp.asarray(tile_facts(tiles, where)),
        remap_weight.reshape(nblk * sources, width, width),
        (nblk, sources, capacity, groups, received),
    )
    (landed, table), plan = ahead((landed, table), plan)
    across = jnp.concatenate([landed, table])

    others = [passed(across, within(pairs)) for pairs in passes]
    held = 1 + len(passes)
    if relayed:
        relay = passed(others[1], within([(s, t ^ 1) for s, t in passes[0]]))
        table = passed(table, within([(p, p ^ 7) for p in range(half)]))
    near = jnp.concatenate([across] + others + [table] * relayed)
    sibling = passed(near, siblings)

    dims = (steps, fields, nblk, sources, received, capacity, stride)
    last = (mine, surface_kind.reshape(nblk, width))
    sums = remap(dims, 0, plan, near, held, split)
    if relayed:
        sums, spots = remap(dims, 1, plan, sibling, held, split, sums, table=table)
        relay, sums = ahead(relay, sums)
        met = passed(relay, siblings)
        sums = remap(dims, 2, plan, relay, 1, split, sums, spots=spots)
        out = remap(dims, 3, plan, met, 1, split, sums, last, spots=spots)
    else:
        out = remap(dims, 1, plan, sibling, held, split, sums, last)
    out = out.reshape(steps, nblk, 4, width).transpose(0, 2, 1, 3)
    return out.reshape(steps, 4, nblk * width)


def solution(mesh):
    return jax.shard_map(
        local,
        mesh=mesh,
        in_specs=(
            P(None, None, ("group", "comp")),
            P("comp"),
            P("comp", None, None),
            P("comp", None),
            P("comp", None),
            P("comp"),
            P("comp", None, None, None),
        ),
        out_specs=P(None, None, ("group", "comp")),
        check_vma=False,
    )
```

```python
import jax
import jax.numpy as jnp
import numpy as np
from jax import lax
from jax.experimental import pallas as pl
from jax.experimental.pallas import tpu as pltpu
from jax.sharding import PartitionSpec as P


def exchange_plan(tiles, neigh):
    half = tiles // 2
    before, after = neigh // 2, neigh - 1 - neigh // 2
    where = np.zeros((half, neigh), np.int32)
    offsets = [
        (p, n, p + n - before)
        for p in range(half)
        for n in range(neigh)
        if 0 <= p + n - before < half
    ]
    if half == 8:
        passes = [
            [(p, p ^ (4 if p % 2 else 2)) for p in range(half)],
            [(p, p ^ (2 if p % 2 else 4)) for p in range(half)],
        ]
        land = 4
        for p, n, s in offsets:
            chip, other = (s ^ p ^ land) // 2, (s ^ p) % 2
            if s % 2 and chip in (1, 2):
                chip = 3 - chip
            where[p, n] = (3 - other) * 16 if chip == 3 else other * 16 + chip
        return passes, True, land, where
    wanted = set()
    for p, n, s in offsets:
        for core in (0, 1):
            if s // 2 != p // 2:
                wanted.add((2 * (s // 2) + s % 2, 2 * (p // 2) + s % 2))
    reach = max((abs(s // 2 - p // 2) for s, p in wanted), default=0)
    passes, place = [], {(c, c): 0 for c in range(half // 2)}
    for d in range(1, reach + 1):
        for phase in (0, 1):
            pairs = []
            for s, p in sorted(wanted):
                low = min(s // 2, p // 2)
                if abs(s // 2 - p // 2) == d and (low // d) % 2 == phase:
                    pairs.append((s, p))
                    place[s // 2, p // 2] = len(passes) + 1
            if pairs:
                passes.append(pairs)
    for p, n, s in offsets:
        where[p, n] = place[s // 2, p // 2] + 16 * (s % 2 != p % 2)
    return passes, False, 0, where


def tile_facts(tiles, where):
    half = tiles // 2
    return np.array(
        [[*where[t % half], t < half] for t in range(tiles)], np.int32
    )


def encode_kernel(block_ref, count_ref, out_ref):
    neigh, capacity = block_ref.shape
    slot = lax.broadcasted_iota(jnp.int32, (1, capacity), 1)
    out_ref[...] = jnp.full(out_ref.shape, -1.0, jnp.float32)
    for n in range(neigh):
        code = jnp.where(slot < count_ref[0, n], block_ref[n:n + 1, :], -1)
        out_ref[n:n + 1, :capacity] = code.astype(jnp.float32)


def encode(block, count, width):
    neigh = block.shape[0]
    return pl.pallas_call(
        encode_kernel,
        out_shape=jax.ShapeDtypeStruct((neigh + -neigh % 8, width), jnp.float32),
        in_specs=[pl.BlockSpec(memory_space=pltpu.VMEM), pl.BlockSpec(memory_space=pltpu.SMEM)],
        out_specs=pl.BlockSpec(memory_space=pltpu.VMEM),
        cost_estimate=pl.CostEstimate(flops=4096, bytes_accessed=8192, transcendentals=0),
        name="encode",
    )(block, count)


def power(n):
    return 1 << (n - 1).bit_length()


def over(x, n):
    return x >> (n.bit_length() - 1) if n == power(n) else lax.div(x, jnp.int32(n))


def rest_of(x, n):
    return x & (n - 1) if n == power(n) else lax.rem(x, jnp.int32(n))


UNROLL = 32
LATE = 32


def prepare_kernel(
    dims, chunks, slot_hbm, count_hbm, facts_hbm, w_hbm, split_ref, plan_ref,
    buf, slot_ref, count_ref, facts_ref, sems, small_sems,
):
    nblk, sources, capacity, groups, received = dims
    tile = lax.axis_index("comp")
    neigh = received // capacity
    slots, width = w_hbm.shape[:2]
    per = slots // chunks
    small = [
        pltpu.make_async_copy(src, dst, small_sems.at[i])
        for i, (src, dst) in enumerate(
            [(slot_hbm, slot_ref), (count_hbm, count_ref), (facts_hbm, facts_ref)]
        )
    ]
    copies = [
        pltpu.make_async_copy(
            w_hbm.at[pl.ds(i * per, per)], buf.at[pl.ds(i * per, per)], sems.at[i]
        )
        for i in range(chunks)
    ]
    for copy in small + copies:
        copy.start()
    for copy in small:
        copy.wait()

    low = power(slots + 1)
    lines = neigh + -neigh % 8
    split_ref[slots] = jnp.zeros(split_ref.shape[1:], split_ref.dtype)

    def block(b, numbers):
        count = count_ref[b]
        numbers = list(numbers)
        slot = [slot_ref[k, b] for k in range(sources)]
        place = [facts_ref[tile, over(s, capacity)] for s in slot]
        spots = []
        for k in range(sources):
            line = rest_of(place[k], 16) * lines + over(slot[k], capacity)
            group = over(place[k], 16)
            n = numbers[0]
            for g in range(1, groups):
                n = jnp.where(group == g, numbers[g], n)
            for g in range(groups):
                numbers[g] += ((group == g) & (k < count)).astype(jnp.int32)
            spots.append((group, n, (line * width + rest_of(slot[k], capacity)) * low + b * sources + k))
        for group, n, entry in spots:
            plan_ref[group, n] = entry
        for k in range(sources):
            j = b * sources + k
            w = buf[j]
            first = w.astype(jnp.bfloat16)
            rest = (w - first.astype(jnp.float32)).astype(jnp.bfloat16)
            split_ref[j, :, :width] = first
            split_ref[j, :, width:] = rest
        return tuple(numbers)

    numbers = (jnp.int32(0),) * groups
    blocks = nblk // chunks
    for i in range(chunks):
        copies[i].wait()
        numbers = lax.fori_loop(i * blocks, (i + 1) * blocks, block, numbers, unroll=2)
    for g in range(groups):
        for u in range(LATE):
            plan_ref[g, numbers[g] + u] = slots
        plan_ref[groups, g] = numbers[g]
    plan_ref[groups, groups] = facts_ref[tile, neigh]


def prepare(slot, count, facts, weight, dims):
    nblk, sources, capacity, groups, received = dims
    slots, width, _ = weight.shape
    chunks = 10 if nblk % 10 == 0 else 1
    smem = pl.BlockSpec(memory_space=pltpu.SMEM)
    vmem = pl.BlockSpec(memory_space=pltpu.VMEM)
    args = [pltpu.with_memory_space_constraint(a, pltpu.HBM) for a in (slot, count, facts, weight)]
    return pl.pallas_call(
        lambda *refs: prepare_kernel(dims, chunks, *refs),
        out_shape=(
            pltpu.VMEM((slots + 1, width, 2 * width), jnp.bfloat16),
            pltpu.SMEM((groups + 1, slots + LATE + -(slots + LATE) % 128), jnp.int32),
        ),
        in_specs=[pl.BlockSpec(memory_space=pl.ANY)] * 4,
        out_specs=(vmem, smem),
        scratch_shapes=[
            pltpu.VMEM(weight.shape, jnp.float32),
            pltpu.SMEM(slot.shape, jnp.int32),
            pltpu.SMEM(count.shape, jnp.int32),
            pltpu.SMEM(facts.shape, jnp.int32),
            pltpu.SemaphoreType.DMA((chunks,)),
            pltpu.SemaphoreType.DMA((3,)),
        ],
        compiler_params=pltpu.CompilerParams(vmem_limit_bytes=16 * 2**20),
        cost_estimate=pl.CostEstimate(
            flops=slots * width * width * 4, bytes_accessed=weight.size * 8, transcendentals=0
        ),
        name="prepare",
    )(*args)


def fluxes_of(air, sea, kind):
    wind_u, wind_v, air_temp, air_humid, radiation = air
    sea_temp, ice_conc, ice_temp, current_u, current_v = sea
    wet = (kind > 0).astype(jnp.float32)
    frac = jnp.clip(ice_conc, 0.0, 1.0) * (kind == 2).astype(jnp.float32)
    du = wind_u - current_u
    dv = wind_v - current_v
    speed = jnp.sqrt(du * du + dv * dv + 1.0)
    drag = 0.8 * (1.0 - frac) + 1.2 * frac

    def terms(ts, sens, albedo, latent):
        evap = 0.5 * speed * (0.6 * jnp.exp(0.3 * ts) - air_humid)
        heat = (
            sens * speed * (ts - air_temp)
            + latent * evap
            - ((1.0 - albedo) * radiation - 0.25 * ts)
        )
        return heat, evap

    heat_water, evap_water = terms(sea_temp, 0.6, 0.07, 1.0)
    heat_ice, evap_ice = terms(ice_temp, 0.4, 0.6, 1.2)
    pull = wet * drag * speed
    return (
        pull * du,
        pull * dv,
        wet * ((1.0 - frac) * heat_water + frac * heat_ice),
        wet * ((1.0 - frac) * evap_water + frac * evap_ice),
    )


def add_slots(dims, number, spot, x_ref, split_ref, acc, each=UNROLL):
    steps, fields, nblk, sources, received, capacity, stride = dims
    span = nblk * steps
    rows = 8
    width = split_ref.shape[1]
    spare = jnp.zeros((rows - fields, width), jnp.float32)

    def batch(i, carry):
        for j, base in [spot(i * each + u) for u in range(each)]:
            x = []
            for m in range(steps):
                x += [x_ref[pl.ds(base + m, fields, stride=span), :], spare]
            x = jnp.concatenate(x, axis=0)
            first = x.astype(jnp.bfloat16)
            rest = (x - first.astype(jnp.float32)).astype(jnp.bfloat16)
            both = jnp.dot(
                jnp.concatenate([first, rest], axis=0), split_ref[j],
                preferred_element_type=jnp.float32,
            )
            both = both[:, :width] + both[:, width:]
            n = rows * steps
            both = both[:n] + both[n:]
            for m in range(steps):
                at = pl.ds(m * rows * nblk + over(j, sources), rows, stride=nblk)
                acc[at, :] += both[m * rows:(m + 1) * rows]
        return carry

    lax.fori_loop(0, over(number + each - 1, each), batch, 0)


def find_starts(dims, x_ref, tiles, at, starts):
    steps, fields, nblk, sources, received, capacity, stride = dims
    lines = stride - steps * fields * nblk
    for i in range(tiles):
        code = x_ref[pl.ds(i * stride + stride - lines, lines), :]
        row = (code * steps + i * stride).astype(jnp.int32)
        starts[pl.ds(at + i * lines, lines), :] = jnp.where(code >= 0.0, row, -1)


def found(dims, entry, line, base_ref):
    steps, fields, nblk, sources, received, capacity, stride = dims
    low, width = power(nblk * sources + 1), base_ref.shape[1]
    base = base_ref[line + over(entry, low * width), rest_of(over(entry, low), width)]
    j = jnp.where(base < 0, nblk * sources, rest_of(entry, low))
    return j, jnp.maximum(base, 0)


def remap_kernel(dims, group, last, plan_ref, x_ref, split_ref, *refs):
    refs = list(refs)
    before = refs.pop(0) if group else None
    state_ref, kind_ref = (refs.pop(0), refs.pop(0)) if last else (None, None)
    out_ref = refs.pop(0)
    acc = refs.pop(0) if last else out_ref
    starts, base_ref, sem = refs
    groups = plan_ref.shape[0] - 1
    lines = dims[-1] - dims[0] * dims[1] * dims[2]
    find_starts(dims, x_ref, starts.shape[0] // lines, 0, starts)
    copy = pltpu.make_async_copy(starts, base_ref, sem)
    copy.start()
    acc[...] = jnp.zeros_like(acc) if before is None else before[...]
    copy.wait()
    add_slots(
        dims, plan_ref[groups, group], lambda i: found(dims, plan_ref[group, i], 0, base_ref),
        x_ref, split_ref, acc,
    )
    if last:
        write_fluxes(dims, plan_ref[groups, groups] > 0, state_ref, kind_ref, acc, out_ref)


def second_kernel(
    dims, tiles, plan_ref, x_ref, table_ref, split_ref, before, acc, spots_ref, starts, base_ref, sem,
):
    groups = plan_ref.shape[0] - 1
    steps = dims[0]
    lines = dims[-1] - dims[0] * dims[1] * dims[2]
    low = power(dims[2] * dims[3] + 1)
    find_starts(dims, x_ref, tiles, 0, starts)
    for g, code in enumerate((table_ref[...], x_ref[pl.ds(tiles * dims[-1], lines), :])):
        row = jnp.where(code >= 0.0, (code * steps).astype(jnp.int32), -1)
        starts[pl.ds((tiles + g) * lines, lines), :] = row
    copy = pltpu.make_async_copy(starts, base_ref, sem)
    copy.start()
    acc[...] = before[...]
    copy.wait()
    add_slots(
        dims, plan_ref[groups, 1], lambda i: found(dims, plan_ref[1, i], 0, base_ref),
        x_ref, split_ref, acc,
    )
    for g in range(2):

        def place(i, carry):
            for u in range(LATE):
                at = i * LATE + u
                j, base = found(dims, plan_ref[2 + g, at], (tiles + g) * lines, base_ref)
                spots_ref[g, at] = base * low + j
            return carry

        lax.fori_loop(0, over(plan_ref[groups, 2 + g] + LATE - 1, LATE), place, 0)


def relayed_kernel(dims, group, last, plan_ref, spots_ref, x_ref, split_ref, before, *refs):
    if last:
        state_ref, kind_ref, out_ref, acc = refs
    else:
        (acc,) = refs
    groups = plan_ref.shape[0] - 1
    low = power(dims[2] * dims[3] + 1)

    def spot(i):
        entry = spots_ref[group - 2, i]
        return rest_of(entry, low), over(entry, low)

    acc[...] = before[...]
    add_slots(dims, plan_ref[groups, group], spot, x_ref, split_ref, acc, LATE)
    if last:
        write_fluxes(dims, plan_ref[groups, groups] > 0, state_ref, kind_ref, acc, out_ref)


def write_fluxes(dims, is_air, state_ref, kind_ref, acc, out_ref):
    steps, fields, nblk = dims[:3]
    span = nblk * steps
    for m in range(steps):
        for j in range(nblk // 8):
            mapped = [acc[pl.ds((m * 8 + f) * nblk + 8 * j, 8), :] for f in range(fields)]
            own = [
                state_ref[pl.ds(f * span + 8 * j * steps + m, 8, stride=steps), :]
                for f in range(fields)
            ]
            air = [jnp.where(is_air, s, r) for s, r in zip(own, mapped)]
            sea = [jnp.where(is_air, r, s) for s, r in zip(own, mapped)]
            for o, value in enumerate(fluxes_of(air, sea, kind_ref[pl.ds(8 * j, 8), :])):
                out_ref[pl.ds(m * 4 * nblk + 32 * j + o, 8, stride=4), :] = value


def remap(dims, group, plan, x, tiles, split, before=None, last=None, table=None, spots=None):
    steps, fields, nblk, sources, received, capacity, stride = dims
    width = x.shape[1]
    lines = stride - steps * fields * nblk
    sums = jax.ShapeDtypeStruct((steps * 8 * nblk + 8, width), jnp.float32)
    smem = pl.BlockSpec(memory_space=pltpu.SMEM)
    vmem = pl.BlockSpec(memory_space=pltpu.VMEM)
    fixed = pltpu.with_memory_space_constraint
    args = [(fixed(plan, pltpu.SMEM), smem)]
    if spots is not None:
        args.append((fixed(spots, pltpu.SMEM), smem))
    args.append((x, vmem))
    if table is not None:
        args.append((table, vmem))
    args.append((fixed(split, pltpu.VMEM), vmem))
    args += [(a, vmem) for a in (before,) + (last or ()) if a is not None]
    found_in = ((tiles + 2 * (table is not None)) * lines, width)
    scratch = []
    if spots is None:
        scratch = [
            pltpu.VMEM(found_in, jnp.int32), pltpu.SMEM(found_in, jnp.int32), pltpu.SemaphoreType.DMA,
        ]
    out, out_specs = sums, vmem
    if last is not None:
        out = jax.ShapeDtypeStruct((steps * nblk * 4, width), jnp.float32)
        scratch = [pltpu.VMEM(sums.shape, jnp.float32)] + scratch
    if table is not None:
        body = lambda *refs: second_kernel(dims, tiles, *refs)
        out = (sums, pltpu.SMEM((2, plan.shape[1]), jnp.int32))
        out_specs = (vmem, smem)
    elif spots is not None:
        body = lambda *refs: relayed_kernel(dims, group, last is not None, *refs)
    else:
        body = lambda *refs: remap_kernel(dims, group, last is not None, *refs)
    return pl.pallas_call(
        body,
        out_shape=out,
        in_specs=[spec for _, spec in args],
        out_specs=out_specs,
        scratch_shapes=scratch,
        compiler_params=pltpu.CompilerParams(vmem_limit_bytes=16 * 2**20),
        cost_estimate=pl.CostEstimate(
            flops=nblk * sources * 32 * width * width,
            bytes_accessed=split.size,
            transcendentals=0 if last is None else 2 * steps * nblk * width,
        ),
        name="remap_last" if last is not None else "remap_%d" % group,
    )(*[arg for arg, _ in args])


def local(state, surface_kind, send_block, send_count, src_slot, src_count, remap_weight):
    tiles = lax.axis_size("comp")
    half = tiles // 2
    steps, fields, _ = state.shape
    nblk, sources, width, _ = remap_weight.shape
    neigh, capacity = send_block.shape[1:]
    passes, relayed, land, where = exchange_plan(tiles, neigh)
    span = nblk * steps
    rows = fields * span

    def passed(array, pairs):
        return lax.ppermute(array, "comp", pairs)

    def within(pairs):
        return pairs + [(s + half, t + half) for s, t in pairs]

    def ahead(early, late):
        return lax.optimization_barrier((early, late))

    siblings = [(i, i ^ 1) for i in range(tiles)]

    mine = state.reshape(steps, fields, nblk, width).transpose(1, 2, 0, 3).reshape(rows, width)
    table = encode(send_block[0], send_count, width)
    stride = rows + table.shape[0]
    crossing = [(i, (i % half ^ land) + (half if i < half else 0)) for i in range(tiles)]
    landed, table = passed(mine, crossing), passed(table, crossing)

    groups = 4 if relayed else 2
    received = neigh * capacity
    split, plan = prepare(
        src_slot.T, src_count, jnp.asarray(tile_facts(tiles, where)),
        remap_weight.reshape(nblk * sources, width, width),
        (nblk, sources, capacity, groups, received),
    )
    (landed, table), plan = ahead((landed, table), plan)
    across = jnp.concatenate([landed, table])

    others = [passed(across, within(pairs)) for pairs in passes]
    held = 1 + len(passes)
    if relayed:
        relay = passed(others[1], within([(s, t ^ 1) for s, t in passes[0]]))
        table = passed(table, within([(p, p ^ 7) for p in range(half)]))
    near = jnp.concatenate([across] + others + [table] * relayed)
    sibling = passed(near, siblings)

    dims = (steps, fields, nblk, sources, received, capacity, stride)
    last = (mine, surface_kind.reshape(nblk, width))
    sums = remap(dims, 0, plan, near, held, split)
    if relayed:
        sums, spots = remap(dims, 1, plan, sibling, held, split, sums, table=table)
        relay, sums = ahead(relay, sums)
        met = passed(relay, siblings)
        sums = remap(dims, 2, plan, relay, 1, split, sums, spots=spots)
        out = remap(dims, 3, plan, met, 1, split, sums, last, spots=spots)
    else:
        out = remap(dims, 1, plan, sibling, held, split, sums, last)
    out = out.reshape(steps, nblk, 4, width).transpose(0, 2, 1, 3)
    return out.reshape(steps, 4, nblk * width)


def solution(mesh):
    return jax.shard_map(
        local,
        mesh=mesh,
        in_specs=(
            P(None, None, ("group", "comp")),
            P("comp"),
            P("comp", None, None),
            P("comp", None),
            P("comp", None),
            P("comp"),
            P("comp", None, None, None),
        ),
        out_specs=P(None, None, ("group", "comp")),
        check_vma=False,
    )
```

```python
import jax
import jax.numpy as jnp
import numpy as np
from jax import lax
from jax.experimental import pallas as pl
from jax.experimental.pallas import tpu as pltpu
from jax.sharding import PartitionSpec as P


def exchange_plan(tiles, neigh):
    half = tiles // 2
    before, after = neigh // 2, neigh - 1 - neigh // 2
    where = np.zeros((half, neigh), np.int32)
    offsets = [
        (p, n, p + n - before)
        for p in range(half)
        for n in range(neigh)
        if 0 <= p + n - before < half
    ]
    if half == 8:
        passes = [
            [(p, p ^ (4 if p % 2 else 2)) for p in range(half)],
            [(p, p ^ (2 if p % 2 else 4)) for p in range(half)],
        ]
        land = 4
        for p, n, s in offsets:
            chip, other = (s ^ p ^ land) // 2, (s ^ p) % 2
            if s % 2 and chip in (1, 2):
                chip = 3 - chip
            where[p, n] = (3 - other) * 16 if chip == 3 else other * 16 + chip
        return passes, True, land, where
    wanted = set()
    for p, n, s in offsets:
        for core in (0, 1):
            if s // 2 != p // 2:
                wanted.add((2 * (s // 2) + s % 2, 2 * (p // 2) + s % 2))
    reach = max((abs(s // 2 - p // 2) for s, p in wanted), default=0)
    passes, place = [], {(c, c): 0 for c in range(half // 2)}
    for d in range(1, reach + 1):
        for phase in (0, 1):
            pairs = []
            for s, p in sorted(wanted):
                low = min(s // 2, p // 2)
                if abs(s // 2 - p // 2) == d and (low // d) % 2 == phase:
                    pairs.append((s, p))
                    place[s // 2, p // 2] = len(passes) + 1
            if pairs:
                passes.append(pairs)
    for p, n, s in offsets:
        where[p, n] = place[s // 2, p // 2] + 16 * (s % 2 != p % 2)
    return passes, False, 0, where


def tile_facts(tiles, where):
    half = tiles // 2
    return np.array(
        [[*where[t % half], t < half] for t in range(tiles)], np.int32
    )


def encode_kernel(block_ref, count_ref, out_ref):
    neigh, capacity = block_ref.shape
    slot = lax.broadcasted_iota(jnp.int32, (1, capacity), 1)
    out_ref[...] = jnp.full(out_ref.shape, -1.0, jnp.float32)
    for n in range(neigh):
        code = jnp.where(slot < count_ref[0, n], block_ref[n:n + 1, :], -1)
        out_ref[n:n + 1, :capacity] = code.astype(jnp.float32)


def encode(block, count, width):
    neigh = block.shape[0]
    return pl.pallas_call(
        encode_kernel,
        out_shape=jax.ShapeDtypeStruct((neigh + -neigh % 8, width), jnp.float32),
        in_specs=[pl.BlockSpec(memory_space=pltpu.VMEM), pl.BlockSpec(memory_space=pltpu.SMEM)],
        out_specs=pl.BlockSpec(memory_space=pltpu.VMEM),
        cost_estimate=pl.CostEstimate(flops=4096, bytes_accessed=8192, transcendentals=0),
        name="encode",
    )(block, count)


def power(n):
    return 1 << (n - 1).bit_length()


def over(x, n):
    return x >> (n.bit_length() - 1) if n == power(n) else lax.div(x, jnp.int32(n))


def rest_of(x, n):
    return x & (n - 1) if n == power(n) else lax.rem(x, jnp.int32(n))


UNROLL = 32
LATE = 32


def prepare_kernel(
    dims, chunks, slot_hbm, count_hbm, facts_hbm, w_hbm, split_ref, plan_ref,
    buf, slot_ref, count_ref, facts_ref, sems, small_sems,
):
    nblk, sources, capacity, groups, received = dims
    tile = lax.axis_index("comp")
    neigh = received // capacity
    slots, width = w_hbm.shape[:2]
    per = slots // chunks
    small = [
        pltpu.make_async_copy(src, dst, small_sems.at[i])
        for i, (src, dst) in enumerate(
            [(slot_hbm, slot_ref), (count_hbm, count_ref), (facts_hbm, facts_ref)]
        )
    ]
    copies = [
        pltpu.make_async_copy(
            w_hbm.at[pl.ds(i * per, per)], buf.at[pl.ds(i * per, per)], sems.at[i]
        )
        for i in range(chunks)
    ]
    for copy in small + copies:
        copy.start()
    for copy in small:
        copy.wait()

    low = power(slots + 1)
    lines = neigh + -neigh % 8
    split_ref[slots] = jnp.zeros(split_ref.shape[1:], split_ref.dtype)

    def block(b, numbers):
        count = count_ref[b]
        numbers = list(numbers)
        slot = [slot_ref[k, b] for k in range(sources)]
        place = [facts_ref[tile, over(s, capacity)] for s in slot]
        spots = []
        for k in range(sources):
            line = rest_of(place[k], 16) * lines + over(slot[k], capacity)
            group = over(place[k], 16)
            n = numbers[0]
            for g in range(1, groups):
                n = jnp.where(group == g, numbers[g], n)
            for g in range(groups):
                numbers[g] += ((group == g) & (k < count)).astype(jnp.int32)
            spots.append((group, n, (line * width + rest_of(slot[k], capacity)) * low + b * sources + k))
        for group, n, entry in spots:
            plan_ref[group, n] = entry
        for k in range(sources):
            j = b * sources + k
            w = buf[j]
            first = w.astype(jnp.bfloat16)
            rest = (w - first.astype(jnp.float32)).astype(jnp.bfloat16)
            split_ref[j, :, :width] = first
            split_ref[j, :, width:] = rest
        return tuple(numbers)

    numbers = (jnp.int32(0),) * groups
    blocks = nblk // chunks
    for i in range(chunks):
        copies[i].wait()
        numbers = lax.fori_loop(i * blocks, (i + 1) * blocks, block, numbers, unroll=2)
    for g in range(groups):
        for u in range(LATE):
            plan_ref[g, numbers[g] + u] = slots
        plan_ref[groups, g] = numbers[g]
    plan_ref[groups, groups] = facts_ref[tile, neigh]


def prepare(slot, count, facts, weight, dims):
    nblk, sources, capacity, groups, received = dims
    slots, width, _ = weight.shape
    chunks = 10 if nblk % 10 == 0 else 1
    smem = pl.BlockSpec(memory_space=pltpu.SMEM)
    vmem = pl.BlockSpec(memory_space=pltpu.VMEM)
    args = [pltpu.with_memory_space_constraint(a, pltpu.HBM) for a in (slot, count, facts, weight)]
    return pl.pallas_call(
        lambda *refs: prepare_kernel(dims, chunks, *refs),
        out_shape=(
            pltpu.VMEM((slots + 1, width, 2 * width), jnp.bfloat16),
            pltpu.SMEM((groups + 1, slots + LATE + -(slots + LATE) % 128), jnp.int32),
        ),
        in_specs=[pl.BlockSpec(memory_space=pl.ANY)] * 4,
        out_specs=(vmem, smem),
        scratch_shapes=[
            pltpu.VMEM(weight.shape, jnp.float32),
            pltpu.SMEM(slot.shape, jnp.int32),
            pltpu.SMEM(count.shape, jnp.int32),
            pltpu.SMEM(facts.shape, jnp.int32),
            pltpu.SemaphoreType.DMA((chunks,)),
            pltpu.SemaphoreType.DMA((3,)),
        ],
        compiler_params=pltpu.CompilerParams(vmem_limit_bytes=16 * 2**20),
        cost_estimate=pl.CostEstimate(
            flops=slots * width * width * 4, bytes_accessed=weight.size * 8, transcendentals=0
        ),
        name="prepare",
    )(*args)


def fluxes_of(air, sea, kind):
    wind_u, wind_v, air_temp, air_humid, radiation = air
    sea_temp, ice_conc, ice_temp, current_u, current_v = sea
    wet = (kind > 0).astype(jnp.float32)
    frac = jnp.clip(ice_conc, 0.0, 1.0) * (kind == 2).astype(jnp.float32)
    du = wind_u - current_u
    dv = wind_v - current_v
    speed = jnp.sqrt(du * du + dv * dv + 1.0)
    drag = 0.8 * (1.0 - frac) + 1.2 * frac

    def terms(ts, sens, albedo, latent):
        evap = 0.5 * speed * (0.6 * jnp.exp(0.3 * ts) - air_humid)
        heat = (
            sens * speed * (ts - air_temp)
            + latent * evap
            - ((1.0 - albedo) * radiation - 0.25 * ts)
        )
        return heat, evap

    heat_water, evap_water = terms(sea_temp, 0.6, 0.07, 1.0)
    heat_ice, evap_ice = terms(ice_temp, 0.4, 0.6, 1.2)
    pull = wet * drag * speed
    return (
        pull * du,
        pull * dv,
        wet * ((1.0 - frac) * heat_water + frac * heat_ice),
        wet * ((1.0 - frac) * evap_water + frac * evap_ice),
    )


def add_slots(dims, number, spot, x_ref, split_ref, acc, each=UNROLL):
    steps, fields, nblk, sources, received, capacity, stride = dims
    span = nblk * steps
    rows = 8
    width = split_ref.shape[1]
    spare = jnp.zeros((rows - fields, width), jnp.float32)

    def batch(i, carry):
        for j, base in [spot(i * each + u) for u in range(each)]:
            x = []
            for m in range(steps):
                x += [x_ref[pl.ds(base + m, fields, stride=span), :], spare]
            x = jnp.concatenate(x, axis=0)
            first = x.astype(jnp.bfloat16)
            rest = (x - first.astype(jnp.float32)).astype(jnp.bfloat16)
            both = jnp.dot(
                jnp.concatenate([first, rest], axis=0), split_ref[j],
                preferred_element_type=jnp.float32,
            )
            both = both[:, :width] + both[:, width:]
            n = rows * steps
            both = both[:n] + both[n:]
            for m in range(steps):
                at = pl.ds(m * rows * nblk + over(j, sources), rows, stride=nblk)
                acc[at, :] += both[m * rows:(m + 1) * rows]
        return carry

    lax.fori_loop(0, over(number + each - 1, each), batch, 0)


def find_starts(dims, x_ref, tiles, at, starts):
    steps, fields, nblk, sources, received, capacity, stride = dims
    lines = stride - steps * fields * nblk
    for i in range(tiles):
        code = x_ref[pl.ds(i * stride + stride - lines, lines), :]
        row = (code * steps + i * stride).astype(jnp.int32)
        starts[pl.ds(at + i * lines, lines), :] = jnp.where(code >= 0.0, row, -1)


def found(dims, entry, line, base_ref):
    steps, fields, nblk, sources, received, capacity, stride = dims
    low, width = power(nblk * sources + 1), base_ref.shape[1]
    base = base_ref[line + over(entry, low * width), rest_of(over(entry, low), width)]
    j = jnp.where(base < 0, nblk * sources, rest_of(entry, low))
    return j, jnp.maximum(base, 0)


def remap_kernel(dims, group, last, plan_ref, x_ref, split_ref, *refs):
    refs = list(refs)
    before = refs.pop(0) if group else None
    state_ref, kind_ref = (refs.pop(0), refs.pop(0)) if last else (None, None)
    out_ref = refs.pop(0)
    acc = refs.pop(0) if last else out_ref
    starts, base_ref, sem = refs
    groups = plan_ref.shape[0] - 1
    lines = dims[-1] - dims[0] * dims[1] * dims[2]
    find_starts(dims, x_ref, starts.shape[0] // lines, 0, starts)
    copy = pltpu.make_async_copy(starts, base_ref, sem)
    copy.start()
    acc[...] = jnp.zeros_like(acc) if before is None else before[...]
    copy.wait()
    add_slots(
        dims, plan_ref[groups, group], lambda i: found(dims, plan_ref[group, i], 0, base_ref),
        x_ref, split_ref, acc,
    )
    if last:
        write_fluxes(dims, plan_ref[groups, groups] > 0, state_ref, kind_ref, acc, out_ref)


def second_kernel(
    dims, tiles, plan_ref, x_ref, table_ref, split_ref, before, acc, spots_ref, starts, base_ref, sem,
):
    groups = plan_ref.shape[0] - 1
    steps = dims[0]
    lines = dims[-1] - dims[0] * dims[1] * dims[2]
    low = power(dims[2] * dims[3] + 1)
    find_starts(dims, x_ref, tiles, 0, starts)
    for g, code in enumerate((table_ref[...], x_ref[pl.ds(tiles * dims[-1], lines), :])):
        row = jnp.where(code >= 0.0, (code * steps).astype(jnp.int32), -1)
        starts[pl.ds((tiles + g) * lines, lines), :] = row
    copy = pltpu.make_async_copy(starts, base_ref, sem)
    copy.start()
    acc[...] = before[...]
    copy.wait()
    add_slots(
        dims, plan_ref[groups, 1], lambda i: found(dims, plan_ref[1, i], 0, base_ref),
        x_ref, split_ref, acc,
    )
    for g in range(2):

        def place(i, carry):
            for u in range(LATE):
                at = i * LATE + u
                j, base = found(dims, plan_ref[2 + g, at], (tiles + g) * lines, base_ref)
                spots_ref[g, at] = base * low + j
            return carry

        lax.fori_loop(0, over(plan_ref[groups, 2 + g] + LATE - 1, LATE), place, 0)


def relayed_kernel(dims, group, last, plan_ref, spots_ref, x_ref, split_ref, before, *refs):
    if last:
        state_ref, kind_ref, out_ref, acc = refs
    else:
        (acc,) = refs
    groups = plan_ref.shape[0] - 1
    low = power(dims[2] * dims[3] + 1)

    def spot(i):
        entry = spots_ref[group - 2, i]
        return rest_of(entry, low), over(entry, low)

    acc[...] = before[...]
    add_slots(dims, plan_ref[groups, group], spot, x_ref, split_ref, acc, LATE)
    if last:
        write_fluxes(dims, plan_ref[groups, groups] > 0, state_ref, kind_ref, acc, out_ref)


def write_fluxes(dims, is_air, state_ref, kind_ref, acc, out_ref):
    steps, fields, nblk = dims[:3]
    span = nblk * steps
    for m in range(steps):
        for j in range(nblk // 8):
            mapped = [acc[pl.ds((m * 8 + f) * nblk + 8 * j, 8), :] for f in range(fields)]
            own = [
                state_ref[pl.ds(f * span + 8 * j * steps + m, 8, stride=steps), :]
                for f in range(fields)
            ]
            air = [jnp.where(is_air, s, r) for s, r in zip(own, mapped)]
            sea = [jnp.where(is_air, r, s) for s, r in zip(own, mapped)]
            for o, value in enumerate(fluxes_of(air, sea, kind_ref[pl.ds(8 * j, 8), :])):
                out_ref[pl.ds(m * 4 * nblk + 32 * j + o, 8, stride=4), :] = value


def remap(dims, group, plan, x, tiles, split, before=None, last=None, table=None, spots=None):
    steps, fields, nblk, sources, received, capacity, stride = dims
    width = x.shape[1]
    lines = stride - steps * fields * nblk
    sums = jax.ShapeDtypeStruct((steps * 8 * nblk + 8, width), jnp.float32)
    smem = pl.BlockSpec(memory_space=pltpu.SMEM)
    vmem = pl.BlockSpec(memory_space=pltpu.VMEM)
    fixed = pltpu.with_memory_space_constraint
    args = [(fixed(plan, pltpu.SMEM), smem)]
    if spots is not None:
        args.append((fixed(spots, pltpu.SMEM), smem))
    args.append((x, vmem))
    if table is not None:
        args.append((table, vmem))
    args.append((fixed(split, pltpu.VMEM), vmem))
    args += [(a, vmem) for a in (before,) + (last or ()) if a is not None]
    found_in = ((tiles + 2 * (table is not None)) * lines, width)
    scratch = []
    if spots is None:
        scratch = [
            pltpu.VMEM(found_in, jnp.int32), pltpu.SMEM(found_in, jnp.int32), pltpu.SemaphoreType.DMA,
        ]
    out, out_specs = sums, vmem
    if last is not None:
        out = jax.ShapeDtypeStruct((steps * nblk * 4, width), jnp.float32)
        scratch = [pltpu.VMEM(sums.shape, jnp.float32)] + scratch
    if table is not None:
        body = lambda *refs: second_kernel(dims, tiles, *refs)
        out = (sums, pltpu.SMEM((2, plan.shape[1]), jnp.int32))
        out_specs = (vmem, smem)
    elif spots is not None:
        body = lambda *refs: relayed_kernel(dims, group, last is not None, *refs)
    else:
        body = lambda *refs: remap_kernel(dims, group, last is not None, *refs)
    return pl.pallas_call(
        body,
        out_shape=out,
        in_specs=[spec for _, spec in args],
        out_specs=out_specs,
        scratch_shapes=scratch,
        compiler_params=pltpu.CompilerParams(vmem_limit_bytes=16 * 2**20),
        cost_estimate=pl.CostEstimate(
            flops=nblk * sources * 32 * width * width,
            bytes_accessed=split.size,
            transcendentals=0 if last is None else 2 * steps * nblk * width,
        ),
        name="remap_last" if last is not None else "remap_%d" % group,
    )(*[arg for arg, _ in args])


def local(state, surface_kind, send_block, send_count, src_slot, src_count, remap_weight):
    tiles = lax.axis_size("comp")
    half = tiles // 2
    steps, fields, _ = state.shape
    nblk, sources, width, _ = remap_weight.shape
    neigh, capacity = send_block.shape[1:]
    passes, relayed, land, where = exchange_plan(tiles, neigh)
    span = nblk * steps
    rows = fields * span

    def passed(array, pairs):
        return lax.ppermute(array, "comp", pairs)

    def within(pairs):
        return pairs + [(s + half, t + half) for s, t in pairs]

    def ahead(early, late):
        return lax.optimization_barrier((early, late))

    siblings = [(i, i ^ 1) for i in range(tiles)]

    mine = state.reshape(steps, fields, nblk, width).transpose(1, 2, 0, 3).reshape(rows, width)
    table = encode(send_block[0], send_count, width)
    stride = rows + table.shape[0]
    crossing = [(i, (i % half ^ land) + (half if i < half else 0)) for i in range(tiles)]
    landed, table = passed(mine, crossing), passed(table, crossing)

    groups = 4 if relayed else 2
    received = neigh * capacity
    split, plan = prepare(
        src_slot.T, src_count, jnp.asarray(tile_facts(tiles, where)),
        remap_weight.reshape(nblk * sources, width, width),
        (nblk, sources, capacity, groups, received),
    )
    (landed, table), plan = ahead((landed, table), plan)
    across = jnp.concatenate([landed, table])

    others = [passed(across, within(pairs)) for pairs in passes]
    held = 1 + len(passes)
    if relayed:
        relay = passed(others[0], within([(s, t ^ 1) for s, t in passes[1]]))
        table = passed(table, within([(p, p ^ 7) for p in range(half)]))
    near = jnp.concatenate([across] + others + [table] * relayed)
    sibling = passed(near, siblings)

    dims = (steps, fields, nblk, sources, received, capacity, stride)
    last = (mine, surface_kind.reshape(nblk, width))
    sums = remap(dims, 0, plan, near, held, split)
    if relayed:
        sums, spots = remap(dims, 1, plan, sibling, held, split, sums, table=table)
        relay, sums = ahead(relay, sums)
        met = passed(relay, siblings)
        sums = remap(dims, 2, plan, relay, 1, split, sums, spots=spots)
        out = remap(dims, 3, plan, met, 1, split, sums, last, spots=spots)
    else:
        out = remap(dims, 1, plan, sibling, held, split, sums, last)
    out = out.reshape(steps, nblk, 4, width).transpose(0, 2, 1, 3)
    return out.reshape(steps, 4, nblk * width)


def solution(mesh):
    return jax.shard_map(
        local,
        mesh=mesh,
        in_specs=(
            P(None, None, ("group", "comp")),
            P("comp"),
            P("comp", None, None),
            P("comp", None),
            P("comp", None),
            P("comp"),
            P("comp", None, None, None),
        ),
        out_specs=P(None, None, ("group", "comp")),
        check_vma=False,
    )
```

```python
import jax
import jax.numpy as jnp
import numpy as np
from jax import lax
from jax.experimental import pallas as pl
from jax.experimental.pallas import tpu as pltpu
from jax.sharding import PartitionSpec as P


def exchange_plan(tiles, neigh):
    half = tiles // 2
    before, after = neigh // 2, neigh - 1 - neigh // 2
    where = np.zeros((half, neigh), np.int32)
    offsets = [
        (p, n, p + n - before)
        for p in range(half)
        for n in range(neigh)
        if 0 <= p + n - before < half
    ]
    if half == 8:
        passes = [
            [(p, p ^ (4 if p % 2 else 2)) for p in range(half)],
            [(p, p ^ (2 if p % 2 else 4)) for p in range(half)],
        ]
        land = 4
        for p, n, s in offsets:
            chip, other = (s ^ p ^ land) // 2, (s ^ p) % 2
            if s % 2 and chip in (1, 2):
                chip = 3 - chip
            where[p, n] = (3 - other) * 16 if chip == 3 else other * 16 + chip
        return passes, True, land, where
    wanted = set()
    for p, n, s in offsets:
        for core in (0, 1):
            if s // 2 != p // 2:
                wanted.add((2 * (s // 2) + s % 2, 2 * (p // 2) + s % 2))
    reach = max((abs(s // 2 - p // 2) for s, p in wanted), default=0)
    passes, place = [], {(c, c): 0 for c in range(half // 2)}
    for d in range(1, reach + 1):
        for phase in (0, 1):
            pairs = []
            for s, p in sorted(wanted):
                low = min(s // 2, p // 2)
                if abs(s // 2 - p // 2) == d and (low // d) % 2 == phase:
                    pairs.append((s, p))
                    place[s // 2, p // 2] = len(passes) + 1
            if pairs:
                passes.append(pairs)
    for p, n, s in offsets:
        where[p, n] = place[s // 2, p // 2] + 16 * (s % 2 != p % 2)
    return passes, False, 0, where


def tile_facts(tiles, where):
    half = tiles // 2
    return np.array(
        [[*where[t % half], t < half] for t in range(tiles)], np.int32
    )


def encode_kernel(block_ref, count_ref, out_ref):
    neigh, capacity = block_ref.shape
    slot = lax.broadcasted_iota(jnp.int32, (1, capacity), 1)
    out_ref[...] = jnp.full(out_ref.shape, -1.0, jnp.float32)
    for n in range(neigh):
        code = jnp.where(slot < count_ref[0, n], block_ref[n:n + 1, :], -1)
        out_ref[n:n + 1, :capacity] = code.astype(jnp.float32)


def encode(block, count, width):
    neigh = block.shape[0]
    return pl.pallas_call(
        encode_kernel,
        out_shape=jax.ShapeDtypeStruct((neigh + -neigh % 8, width), jnp.float32),
        in_specs=[pl.BlockSpec(memory_space=pltpu.VMEM), pl.BlockSpec(memory_space=pltpu.SMEM)],
        out_specs=pl.BlockSpec(memory_space=pltpu.VMEM),
        cost_estimate=pl.CostEstimate(flops=4096, bytes_accessed=8192, transcendentals=0),
        name="encode",
    )(block, count)


def power(n):
    return 1 << (n - 1).bit_length()


def over(x, n):
    return x >> (n.bit_length() - 1) if n == power(n) else lax.div(x, jnp.int32(n))


def rest_of(x, n):
    return x & (n - 1) if n == power(n) else lax.rem(x, jnp.int32(n))


UNROLL = 16
LATE = 32


def prepare_kernel(
    dims, chunks, slot_hbm, count_hbm, facts_hbm, w_hbm, split_ref, plan_ref,
    buf, slot_ref, count_ref, facts_ref, sems, small_sems,
):
    nblk, sources, capacity, groups, received = dims
    tile = lax.axis_index("comp")
    neigh = received // capacity
    slots, width = w_hbm.shape[:2]
    per = slots // chunks
    small = [
        pltpu.make_async_copy(src, dst, small_sems.at[i])
        for i, (src, dst) in enumerate(
            [(slot_hbm, slot_ref), (count_hbm, count_ref), (facts_hbm, facts_ref)]
        )
    ]
    copies = [
        pltpu.make_async_copy(
            w_hbm.at[pl.ds(i * per, per)], buf.at[pl.ds(i * per, per)], sems.at[i]
        )
        for i in range(chunks)
    ]
    for copy in small + copies:
        copy.start()
    for copy in small:
        copy.wait()

    low = power(slots + 1)
    lines = neigh + -neigh % 8
    split_ref[slots] = jnp.zeros(split_ref.shape[1:], split_ref.dtype)

    def block(b, numbers):
        count = count_ref[b]
        numbers = list(numbers)
        slot = [slot_ref[k, b] for k in range(sources)]
        place = [facts_ref[tile, over(s, capacity)] for s in slot]
        spots = []
        for k in range(sources):
            line = rest_of(place[k], 16) * lines + over(slot[k], capacity)
            group = over(place[k], 16)
            n = numbers[0]
            for g in range(1, groups):
                n = jnp.where(group == g, numbers[g], n)
            for g in range(groups):
                numbers[g] += ((group == g) & (k < count)).astype(jnp.int32)
            spots.append((group, n, (line * width + rest_of(slot[k], capacity)) * low + b * sources + k))
        for group, n, entry in spots:
            plan_ref[group, n] = entry
        for k in range(sources):
            j = b * sources + k
            w = buf[j]
            first = w.astype(jnp.bfloat16)
            rest = (w - first.astype(jnp.float32)).astype(jnp.bfloat16)
            split_ref[j, :, :width] = first
            split_ref[j, :, width:] = rest
        return tuple(numbers)

    numbers = (jnp.int32(0),) * groups
    blocks = nblk // chunks
    for i in range(chunks):
        copies[i].wait()
        numbers = lax.fori_loop(i * blocks, (i + 1) * blocks, block, numbers, unroll=2)
    for g in range(groups):
        for u in range(LATE):
            plan_ref[g, numbers[g] + u] = slots
        plan_ref[groups, g] = numbers[g]
    plan_ref[groups, groups] = facts_ref[tile, neigh]


def prepare(slot, count, facts, weight, dims):
    nblk, sources, capacity, groups, received = dims
    slots, width, _ = weight.shape
    chunks = 10 if nblk % 10 == 0 else 1
    smem = pl.BlockSpec(memory_space=pltpu.SMEM)
    vmem = pl.BlockSpec(memory_space=pltpu.VMEM)
    args = [pltpu.with_memory_space_constraint(a, pltpu.HBM) for a in (slot, count, facts, weight)]
    return pl.pallas_call(
        lambda *refs: prepare_kernel(dims, chunks, *refs),
        out_shape=(
            pltpu.VMEM((slots + 1, width, 2 * width), jnp.bfloat16),
            pltpu.SMEM((groups + 1, slots + LATE + -(slots + LATE) % 128), jnp.int32),
        ),
        in_specs=[pl.BlockSpec(memory_space=pl.ANY)] * 4,
        out_specs=(vmem, smem),
        scratch_shapes=[
            pltpu.VMEM(weight.shape, jnp.float32),
            pltpu.SMEM(slot.shape, jnp.int32),
            pltpu.SMEM(count.shape, jnp.int32),
            pltpu.SMEM(facts.shape, jnp.int32),
            pltpu.SemaphoreType.DMA((chunks,)),
            pltpu.SemaphoreType.DMA((3,)),
        ],
        compiler_params=pltpu.CompilerParams(vmem_limit_bytes=16 * 2**20),
        cost_estimate=pl.CostEstimate(
            flops=slots * width * width * 4, bytes_accessed=weight.size * 8, transcendentals=0
        ),
        name="prepare",
    )(*args)


def fluxes_of(air, sea, kind):
    wind_u, wind_v, air_temp, air_humid, radiation = air
    sea_temp, ice_conc, ice_temp, current_u, current_v = sea
    wet = (kind > 0).astype(jnp.float32)
    frac = jnp.clip(ice_conc, 0.0, 1.0) * (kind == 2).astype(jnp.float32)
    du = wind_u - current_u
    dv = wind_v - current_v
    speed = jnp.sqrt(du * du + dv * dv + 1.0)
    drag = 0.8 * (1.0 - frac) + 1.2 * frac

    def terms(ts, sens, albedo, latent):
        evap = 0.5 * speed * (0.6 * jnp.exp(0.3 * ts) - air_humid)
        heat = (
            sens * speed * (ts - air_temp)
            + latent * evap
            - ((1.0 - albedo) * radiation - 0.25 * ts)
        )
        return heat, evap

    heat_water, evap_water = terms(sea_temp, 0.6, 0.07, 1.0)
    heat_ice, evap_ice = terms(ice_temp, 0.4, 0.6, 1.2)
    pull = wet * drag * speed
    return (
        pull * du,
        pull * dv,
        wet * ((1.0 - frac) * heat_water + frac * heat_ice),
        wet * ((1.0 - frac) * evap_water + frac * evap_ice),
    )


def add_slots(dims, number, spot, x_ref, split_ref, acc, each=UNROLL):
    steps, fields, nblk, sources, received, capacity, stride = dims
    span = nblk * steps
    rows = 8
    width = split_ref.shape[1]
    spare = jnp.zeros((rows - fields, width), jnp.float32)

    def batch(i, carry):
        for j, base in [spot(i * each + u) for u in range(each)]:
            x = []
            for m in range(steps):
                x += [x_ref[pl.ds(base + m, fields, stride=span), :], spare]
            x = jnp.concatenate(x, axis=0)
            first = x.astype(jnp.bfloat16)
            rest = (x - first.astype(jnp.float32)).astype(jnp.bfloat16)
            both = jnp.dot(
                jnp.concatenate([first, rest], axis=0), split_ref[j],
                preferred_element_type=jnp.float32,
            )
            both = both[:, :width] + both[:, width:]
            n = rows * steps
            both = both[:n] + both[n:]
            for m in range(steps):
                at = pl.ds(m * rows * nblk + over(j, sources), rows, stride=nblk)
                acc[at, :] += both[m * rows:(m + 1) * rows]
        return carry

    lax.fori_loop(0, over(number + each - 1, each), batch, 0)


def find_starts(dims, x_ref, tiles, at, starts):
    steps, fields, nblk, sources, received, capacity, stride = dims
    lines = stride - steps * fields * nblk
    for i in range(tiles):
        code = x_ref[pl.ds(i * stride + stride - lines, lines), :]
        row = (code * steps + i * stride).astype(jnp.int32)
        starts[pl.ds(at + i * lines, lines), :] = jnp.where(code >= 0.0, row, -1)


def found(dims, entry, line, base_ref):
    steps, fields, nblk, sources, received, capacity, stride = dims
    low, width = power(nblk * sources + 1), base_ref.shape[1]
    base = base_ref[line + over(entry, low * width), rest_of(over(entry, low), width)]
    j = jnp.where(base < 0, nblk * sources, rest_of(entry, low))
    return j, jnp.maximum(base, 0)


def remap_kernel(dims, group, last, plan_ref, x_ref, split_ref, *refs):
    refs = list(refs)
    before = refs.pop(0) if group else None
    state_ref, kind_ref = (refs.pop(0), refs.pop(0)) if last else (None, None)
    out_ref = refs.pop(0)
    acc = refs.pop(0) if last else out_ref
    starts, base_ref, sem = refs
    groups = plan_ref.shape[0] - 1
    lines = dims[-1] - dims[0] * dims[1] * dims[2]
    find_starts(dims, x_ref, starts.shape[0] // lines, 0, starts)
    copy = pltpu.make_async_copy(starts, base_ref, sem)
    copy.start()
    acc[...] = jnp.zeros_like(acc) if before is None else before[...]
    copy.wait()
    add_slots(
        dims, plan_ref[groups, group], lambda i: found(dims, plan_ref[group, i], 0, base_ref),
        x_ref, split_ref, acc,
    )
    if last:
        write_fluxes(dims, plan_ref[groups, groups] > 0, state_ref, kind_ref, acc, out_ref)


def second_kernel(
    dims, tiles, plan_ref, x_ref, table_ref, split_ref, before, acc, spots_ref, starts, base_ref, sem,
):
    groups = plan_ref.shape[0] - 1
    steps = dims[0]
    lines = dims[-1] - dims[0] * dims[1] * dims[2]
    low = power(dims[2] * dims[3] + 1)
    find_starts(dims, x_ref, tiles, 0, starts)
    for g, code in enumerate((table_ref[...], x_ref[pl.ds(tiles * dims[-1], lines), :])):
        row = jnp.where(code >= 0.0, (code * steps).astype(jnp.int32), -1)
        starts[pl.ds((tiles + g) * lines, lines), :] = row
    copy = pltpu.make_async_copy(starts, base_ref, sem)
    copy.start()
    acc[...] = before[...]
    copy.wait()
    add_slots(
        dims, plan_ref[groups, 1], lambda i: found(dims, plan_ref[1, i], 0, base_ref),
        x_ref, split_ref, acc,
    )
    for g in range(2):

        def place(i, carry):
            for u in range(LATE):
                at = i * LATE + u
                j, base = found(dims, plan_ref[2 + g, at], (tiles + g) * lines, base_ref)
                spots_ref[g, at] = base * low + j
            return carry

        lax.fori_loop(0, over(plan_ref[groups, 2 + g] + LATE - 1, LATE), place, 0)


def relayed_kernel(dims, group, last, plan_ref, spots_ref, x_ref, split_ref, before, *refs):
    if last:
        state_ref, kind_ref, out_ref, acc = refs
    else:
        (acc,) = refs
    groups = plan_ref.shape[0] - 1
    low = power(dims[2] * dims[3] + 1)

    def spot(i):
        entry = spots_ref[group - 2, i]
        return rest_of(entry, low), over(entry, low)

    acc[...] = before[...]
    add_slots(dims, plan_ref[groups, group], spot, x_ref, split_ref, acc, LATE)
    if last:
        write_fluxes(dims, plan_ref[groups, groups] > 0, state_ref, kind_ref, acc, out_ref)


def write_fluxes(dims, is_air, state_ref, kind_ref, acc, out_ref):
    steps, fields, nblk = dims[:3]
    span = nblk * steps
    for m in range(steps):
        for j in range(nblk // 8):
            mapped = [acc[pl.ds((m * 8 + f) * nblk + 8 * j, 8), :] for f in range(fields)]
            own = [
                state_ref[pl.ds(f * span + 8 * j * steps + m, 8, stride=steps), :]
                for f in range(fields)
            ]
            air = [jnp.where(is_air, s, r) for s, r in zip(own, mapped)]
            sea = [jnp.where(is_air, r, s) for s, r in zip(own, mapped)]
            for o, value in enumerate(fluxes_of(air, sea, kind_ref[pl.ds(8 * j, 8), :])):
                out_ref[pl.ds(m * 4 * nblk + 32 * j + o, 8, stride=4), :] = value


def remap(dims, group, plan, x, tiles, split, before=None, last=None, table=None, spots=None):
    steps, fields, nblk, sources, received, capacity, stride = dims
    width = x.shape[1]
    lines = stride - steps * fields * nblk
    sums = jax.ShapeDtypeStruct((steps * 8 * nblk + 8, width), jnp.float32)
    smem = pl.BlockSpec(memory_space=pltpu.SMEM)
    vmem = pl.BlockSpec(memory_space=pltpu.VMEM)
    fixed = pltpu.with_memory_space_constraint
    args = [(fixed(plan, pltpu.SMEM), smem)]
    if spots is not None:
        args.append((fixed(spots, pltpu.SMEM), smem))
    args.append((x, vmem))
    if table is not None:
        args.append((table, vmem))
    args.append((fixed(split, pltpu.VMEM), vmem))
    args += [(a, vmem) for a in (before,) + (last or ()) if a is not None]
    found_in = ((tiles + 2 * (table is not None)) * lines, width)
    scratch = []
    if spots is None:
        scratch = [
            pltpu.VMEM(found_in, jnp.int32), pltpu.SMEM(found_in, jnp.int32), pltpu.SemaphoreType.DMA,
        ]
    out, out_specs = sums, vmem
    if last is not None:
        out = jax.ShapeDtypeStruct((steps * nblk * 4, width), jnp.float32)
        scratch = [pltpu.VMEM(sums.shape, jnp.float32)] + scratch
    if table is not None:
        body = lambda *refs: second_kernel(dims, tiles, *refs)
        out = (sums, pltpu.SMEM((2, plan.shape[1]), jnp.int32))
        out_specs = (vmem, smem)
    elif spots is not None:
        body = lambda *refs: relayed_kernel(dims, group, last is not None, *refs)
    else:
        body = lambda *refs: remap_kernel(dims, group, last is not None, *refs)
    return pl.pallas_call(
        body,
        out_shape=out,
        in_specs=[spec for _, spec in args],
        out_specs=out_specs,
        scratch_shapes=scratch,
        compiler_params=pltpu.CompilerParams(vmem_limit_bytes=16 * 2**20),
        cost_estimate=pl.CostEstimate(
            flops=nblk * sources * 32 * width * width,
            bytes_accessed=split.size,
            transcendentals=0 if last is None else 2 * steps * nblk * width,
        ),
        name="remap_last" if last is not None else "remap_%d" % group,
    )(*[arg for arg, _ in args])


def local(state, surface_kind, send_block, send_count, src_slot, src_count, remap_weight):
    tiles = lax.axis_size("comp")
    half = tiles // 2
    steps, fields, _ = state.shape
    nblk, sources, width, _ = remap_weight.shape
    neigh, capacity = send_block.shape[1:]
    passes, relayed, land, where = exchange_plan(tiles, neigh)
    span = nblk * steps
    rows = fields * span

    def passed(array, pairs):
        return lax.ppermute(array, "comp", pairs)

    def within(pairs):
        return pairs + [(s + half, t + half) for s, t in pairs]

    def ahead(early, late):
        return lax.optimization_barrier((early, late))

    siblings = [(i, i ^ 1) for i in range(tiles)]

    mine = state.reshape(steps, fields, nblk, width).transpose(1, 2, 0, 3).reshape(rows, width)
    table = encode(send_block[0], send_count, width)
    stride = rows + table.shape[0]
    crossing = [(i, (i % half ^ land) + (half if i < half else 0)) for i in range(tiles)]
    landed, table = passed(mine, crossing), passed(table, crossing)

    groups = 4 if relayed else 2
    received = neigh * capacity
    split, plan = prepare(
        src_slot.T, src_count, jnp.asarray(tile_facts(tiles, where)),
        remap_weight.reshape(nblk * sources, width, width),
        (nblk, sources, capacity, groups, received),
    )
    (landed, table), plan = ahead((landed, table), plan)
    across = jnp.concatenate([landed, table])

    others = [passed(across, within(pairs)) for pairs in passes]
    held = 1 + len(passes)
    if relayed:
        relay = passed(others[1], within([(s, t ^ 1) for s, t in passes[0]]))
        table = passed(table, within([(p, p ^ 7) for p in range(half)]))
    near = jnp.concatenate([across] + others + [table] * relayed)
    sibling = passed(near, siblings)

    dims = (steps, fields, nblk, sources, received, capacity, stride)
    last = (mine, surface_kind.reshape(nblk, width))
    sums = remap(dims, 0, plan, near, held, split)
    if relayed:
        sums, spots = remap(dims, 1, plan, sibling, held, split, sums, table=table)
        met = passed(relay, siblings)
        sums = remap(dims, 2, plan, relay, 1, split, sums, spots=spots)
        out = remap(dims, 3, plan, met, 1, split, sums, last, spots=spots)
    else:
        out = remap(dims, 1, plan, sibling, held, split, sums, last)
    out = out.reshape(steps, nblk, 4, width).transpose(0, 2, 1, 3)
    return out.reshape(steps, 4, nblk * width)


def solution(mesh):
    return jax.shard_map(
        local,
        mesh=mesh,
        in_specs=(
            P(None, None, ("group", "comp")),
            P("comp"),
            P("comp", None, None),
            P("comp", None),
            P("comp", None),
            P("comp"),
            P("comp", None, None, None),
        ),
        out_specs=P(None, None, ("group", "comp")),
        check_vma=False,
    )
```
